256 devices in a mesh: tm: 32 (over x, z), dp: 8 (over y, core).
Axes of the slice: x: 4, y: 4, z: 8, core: 2. Of those that a mesh axis runs over, the one named last changes fastest.
Arguments:
- video: bfloat16 [8, 64, 16, 64, 128], P('dp', 'tm')
- clip_first: int32 [8, 64], P('dp', 'tm'), may hold values from 0 to 63, as said below
- kernel: bfloat16 [3, 3, 3, 128, 128], replicated, may hold values from -0.109375 to 0.109375
- bias: float32 [128], replicated, may hold values from -3 to 3
- cotangent: bfloat16 [8, 64, 8, 32, 128], P('dp', 'tm'), may hold values from -6 to 6
Outputs:
- downsampled: bfloat16 [8, 64, 8, 32, 128], P('dp', 'tm')
- kernel_grad: float32 [3, 3, 3, 128, 128], replicated
The draws below stay inside these ranges and needn't reach their ends.
Inputs may be any that keep to these rules, and one draw needn't show every extreme that they name: `clip_first`: frames of one clip share the index of the clip's first frame; it never falls along a stream and is at most the frame's own index. Every stream holds at least two clips. Clips are 17 to 121 frames long, the first one of a stream cut off at its start and the last one at its end.
All inputs are finite; a program needn't handle non-finite values.
Results may differ from the reference program's by a relative error of at most 0.02.
Values may be sent and summed in bfloat16 or wider, within the bound.
A program may use at most 64 MiB of HBM per device.

```python
import jax
import jax.numpy as jnp
from jax import lax

C = 128
HH = 16
WW = 64
FRAMES = 64
N_DP = 8


def draw_video(key, part):
    key = jax.random.fold_in(key, 1)
    key_scale = jax.random.fold_in(key, 11)
    key_shift = jax.random.fold_in(key, 12)
    key_vals = jax.random.fold_in(key, 13)
    place = jnp.arange(FRAMES, dtype=jnp.float32)
    ramp = jnp.exp(place * (jnp.log(3.0) / FRAMES))
    frame_scale = jnp.exp(jax.random.uniform(key_scale, (N_DP, FRAMES), jnp.float32, 0.0, jnp.log(10.0))) * ramp[None, :]
    shift = 0.5 * jax.random.normal(key_shift, (N_DP, FRAMES, 1, 1, C), jnp.float32)
    base = jax.random.normal(key_vals, (N_DP, FRAMES, HH, WW, C), jnp.float32)
    values = shift + base * frame_scale[:, :, None, None, None] * 0.3
    return values.astype(jnp.bfloat16)


def draw_clip_first(key, part):
    key = jax.random.fold_in(key, 2)
    key_head = jax.random.fold_in(key, 21)
    key_rest = jax.random.fold_in(key, 22)
    count = FRAMES // 17 + 2
    head = jax.random.randint(key_head, (N_DP, 1), 1, min(FRAMES, 122)).astype(jnp.int32)
    lengths = jax.random.randint(key_rest, (N_DP, count), 17, 122).astype(jnp.int32)
    later = head + jnp.cumsum(lengths, axis=1) - lengths
    starts = jnp.concatenate([jnp.zeros((N_DP, 1), jnp.int32), later.astype(jnp.int32)], axis=1)
    place = jnp.arange(FRAMES, dtype=jnp.int32)
    chosen = jnp.where(starts[:, None, :] <= place[None, :, None], starts[:, None, :], 0)
    return jnp.max(chosen, axis=-1).astype(jnp.int32)


def block_scale(stream_key, extent, pieces, low, top_value):
    loudness, own = 1.0, jax.random.fold_in(stream_key, 6)
    for dim, parts in pieces:
        draws = jnp.exp(jax.random.uniform(jax.random.fold_in(own, dim), (parts,), jnp.float32, low / len(pieces), top_value / len(pieces)))
        loudness = loudness * jnp.repeat(draws, extent[dim] // parts).reshape([-1 if axis == dim else 1 for axis in range(len(extent))])
    return loudness


def scatter_about(rng, shape, scale, limit, cuts=(), held_as=jnp.bfloat16):
    array = scale * jax.random.normal(rng, shape, jnp.float32)
    if cuts:
        array = array * block_scale(rng, shape, cuts, -0.22, 0.18)
    return jnp.clip(array, -limit, limit).astype(held_as)


def setup_inputs(seed: int = 0) -> dict:
    streams_of = jax.random.split(jax.random.key(seed), 6)
    video = draw_video(jax.random.fold_in(streams_of[5], 71), 0)
    clip_first = draw_clip_first(jax.random.fold_in(streams_of[5], 71), 0)
    kernel = scatter_about(streams_of[2], (3, 3, 3, C, C), (27 * C) ** -0.5, 0.109375)
    bias = scatter_about(streams_of[3], (C,), 0.5, 3.0, (), jnp.float32)
    cotangent = scatter_about(streams_of[4], (N_DP, FRAMES, HH // 2, WW // 2, C), 1.0, 6.0, ((0, 8), (1, 32)))
    return {"video": video, "clip_first": clip_first, "kernel": kernel, "bias": bias, "cotangent": cotangent}


def slope(value):
    logistic = jax.nn.sigmoid(value)
    return logistic * (1.0 + value * (1.0 - logistic))

def conv_taps(padded, valid, kernel, bias):
    frames = valid.shape[0]
    height = padded.shape[1] - 2
    width = padded.shape[2] - 2
    chans = padded.shape[3]
    total = jnp.zeros((frames * height * width, chans), jnp.float32)
    for step in range(3):
        part = jnp.zeros((frames * height * width, chans), jnp.float32)
        for row_off in range(3):
            for col_off in range(3):
                piece = padded[step:step + frames, row_off:row_off + height, col_off:col_off + width].reshape(-1, chans)
                part = part + jnp.dot(piece, kernel[step, row_off, col_off], preferred_element_type=jnp.float32)
        weight = jnp.repeat(valid[:, step], height * width)
        total = total + part * weight[:, None]
    return total + bias[None, :]

def tap_grads(padded, valid, dconv):
    frames = valid.shape[0]
    height = padded.shape[1] - 2
    width = padded.shape[2] - 2
    chans = padded.shape[3]
    shaped = dconv.reshape(frames, height * width, chans)
    result = []
    for step in range(3):
        masked = (shaped * valid[:, step][:, None, None].astype(jnp.bfloat16)).reshape(-1, chans)
        for row_off in range(3):
            for col_off in range(3):
                piece = padded[step:step + frames, row_off:row_off + height, col_off:col_off + width].reshape(-1, chans)
                result.append(lax.dot_general(piece, masked, (((0,), (0,)), ((), ())), preferred_element_type=jnp.float32))
    return jnp.stack(result).reshape(3, 3, 3, chans, chans)

def one_stream(args):
    frames_in, first, cot, kernel, bias = args
    frames, height, width, chans = frames_in.shape
    groups = chans // 4
    grouped = frames_in.astype(jnp.float32).reshape(frames, height * width, groups, 4)
    frame_sums = jnp.stack([lax.optimization_barrier(jnp.sum(grouped, axis=(1, 3))), lax.optimization_barrier(jnp.sum(grouped * grouped, axis=(1, 3)))], 1)
    place = jnp.arange(frames, dtype=jnp.int32)
    member = ((first[None, :] == first[:, None]) & (place[None, :] <= place[:, None])).astype(jnp.float32)
    sums = jnp.einsum('ts,sjg->tjg', member, frame_sums, precision=lax.Precision.HIGHEST)
    count = lax.optimization_barrier(jnp.sum(member, axis=1)) * (height * width * 4)
    mean = sums[:, 0] / count[:, None]
    var = sums[:, 1] / count[:, None] - mean * mean
    scale = lax.rsqrt(var + 1e-05)
    normed = ((grouped - mean[:, None, :, None]) * scale[:, None, :, None]).reshape(frames_in.shape).astype(jnp.bfloat16)
    extended = jnp.concatenate([jnp.zeros((2, height, width, chans), jnp.bfloat16), normed], 0)
    padded = jnp.pad(extended, ((0, 0), (1, 1), (1, 1), (0, 0)))
    valid = (place[:, None] - 2 + jnp.arange(3, dtype=jnp.int32)[None, :] >= first[:, None]).astype(jnp.float32)
    conv = conv_taps(padded, valid, kernel, bias)
    active = jax.nn.silu(conv).reshape(frames, height // 2, 2, width // 2, 2, chans)
    output = lax.optimization_barrier(jnp.mean(active, axis=(2, 4))).astype(jnp.bfloat16)
    spread = jnp.broadcast_to(cot.astype(jnp.float32)[:, :, None, :, None, :] * 0.25, (frames, height // 2, 2, width // 2, 2, chans))
    dconv = (spread.reshape(-1, chans) * slope(conv)).astype(jnp.bfloat16)
    return (output, tap_grads(padded, valid, dconv))

def reference(video, clip_first, kernel, bias, cotangent):

    def single(pair):
        return one_stream((pair[0], pair[1], pair[2], kernel, bias))
    outputs, grads = lax.map(single, (video, clip_first, cotangent))
    return (outputs, lax.optimization_barrier(jnp.sum(grads, axis=0)))
```

```python
import functools

import jax
import jax.numpy as jnp
from jax import lax
from jax.experimental import pallas as pl
from jax.experimental.pallas import tpu as pltpu
from jax.sharding import PartitionSpec as P

F32 = jnp.float32
BF16 = jnp.bfloat16
TILES = 27 * 4


def fused(
    nx,
    nz,
    ny,
    first_ref,
    bias_ref,
    video_hbm,
    kern_hbm,
    cot_hbm,
    down_ref,
    grad_hbm,
    vid,
    halo,
    kern,
    cot,
    xs,
    acc,
    spread,
    pool,
    dts,
    dtm,
    gath,
    grads,
    r_pair,
    part,
    r_plane,
    a32,
    a16,
    r_z,
    full,
    local_sem,
    halo_send,
    halo_recv,
    stat_send,
    stat_recv,
    pair_send,
    pair_recv,
    plane_send,
    plane_recv,
    z_send,
    z_recv,
    zg_send,
    zg_recv,
    pg_send,
    pg_recv,
    cg_send,
    cg_recv,
):
    _, frames, height, width, chans = video_hbm.shape
    half_h, half_w = height // 2, width // 2
    pixels = height * width
    n_plane = nx * ny
    n_tm = nx * nz
    slots = grads.shape[2]
    used = r_pair.shape[1]
    zt = slots // nz

    tm = lax.axis_index("tm")
    dp = lax.axis_index("dp")
    x, z = tm // nz, tm % nz
    y, core = dp // 2, dp % 2
    plane = x * ny + y

    def at(tm_to, dp_to):
        return {"tm": tm_to, "dp": dp_to}

    def plane_peer(q):
        return at((q // ny) * nz + z, (q % ny) * 2 + core)

    def z_peer(q):
        return at(x * nz + q, dp)

    sibling = at(tm, y * 2 + 1 - core)

    def remote(src, dst, send, recv, to):
        return pltpu.make_async_remote_copy(
            src_ref=src,
            dst_ref=dst,
            send_sem=send,
            recv_sem=recv,
            device_id=to,
            device_id_type=pl.DeviceIdType.MESH,
        )

    loads = [
        pltpu.make_async_copy(video_hbm.at[0], vid, local_sem.at[0]),
        pltpu.make_async_copy(cot_hbm.at[0], cot, local_sem.at[1]),
        pltpu.make_async_copy(kern_hbm, kern, local_sem.at[2]),
    ]
    for load in loads:
        load.start()

    barrier = pltpu.get_barrier_semaphore()
    peers = [sibling]
    peers += [at((tm + d) % n_tm, dp) for d in range(1, n_tm)]
    for d in range(1, n_plane):
        q = (plane + d) % n_plane
        peers.append(plane_peer(q))
    for peer in peers:
        pl.semaphore_signal(barrier, inc=1, device_id=peer, device_id_type=pl.DeviceIdType.MESH)

    loads[0].wait()
    rows = []
    for f in range(frames):
        value = vid[f].astype(F32)
        rows.append(jnp.sum(jnp.sum(value, axis=0), axis=0, keepdims=True))
        rows.append(jnp.sum(jnp.sum(value * value, axis=0), axis=0, keepdims=True))
    rows.append(jnp.zeros((4, chans), F32))
    stat = jnp.concatenate(rows, axis=0)
    lane = lax.broadcasted_iota(jnp.int32, (8, chans), 1)
    stat = stat + jnp.where(lane % 2 == 0, pltpu.roll(stat, chans - 1, 1), pltpu.roll(stat, 1, 1))
    stat = stat + jnp.where(lane % 4 < 2, pltpu.roll(stat, chans - 2, 1), pltpu.roll(stat, 2, 1))
    gath[tm] = stat

    pl.semaphore_wait(barrier, len(peers))

    following = at((tm + 1) % n_tm, dp)
    halos = [
        remote(video_hbm.at[0, f], halo.at[f], halo_send.at[f], halo_recv.at[f], following)
        for f in range(frames)
    ]
    stats = []
    for d in range(1, n_tm):
        stats.append(
            remote(
                gath.at[tm],
                gath.at[tm],
                stat_send.at[d],
                stat_recv.at[tm],
                at((tm + d) % n_tm, dp),
            )
        )
    for copy in stats:
        copy.start()
    halos[1].start()
    halos[0].start()

    loads[1].wait()
    for f in range(frames):
        for i in range(half_h):
            quarter = cot[f, i].astype(F32) * 0.25
            spread[f * half_h + i, pl.ds(0, half_w, stride=2), :] = quarter
            spread[f * half_h + i, pl.ds(1, half_w, stride=2), :] = quarter
    rim = jnp.zeros((width, 3 * chans), BF16)
    for s in range(4):
        xs[s, 0] = rim
        xs[s, height + 1] = rim
    blank = jnp.zeros((16, chans), BF16)
    for h in range(2):
        for j in range(TILES, n_plane * used):
            grads[h, j // used, j % used] = blank
    for j in range(used, slots):
        a32[j] = jnp.zeros((16, chans), F32)

    first0 = first_ref[0, 0]
    first1 = first_ref[0, 1]
    t0 = tm * frames
    loads[2].wait()

    for d in range(1, n_tm):
        q = (tm + d) % n_tm
        remote(
            gath.at[tm], gath.at[q], stat_send.at[d], stat_recv.at[q], at(q, dp)
        ).wait_recv()

    gathered = gath[...]
    row = lax.broadcasted_iota(jnp.int32, gathered.shape, 1)
    frame = lax.broadcasted_iota(jnp.int32, gathered.shape, 0) * frames + row // 2

    def moments(first, last):
        chosen = jnp.where((frame >= first) & (frame <= last) & (row < 4), gathered, 0.0)
        total = jnp.sum(chosen, axis=0)
        number = jnp.maximum((last - first + 1) * (pixels * 4), 1)
        count = jnp.full((1, chans), number, jnp.int32).astype(F32)
        mean = (total[0:1] + total[2:3]) / count
        var = (total[1:2] + total[3:4]) / count - mean * mean
        return mean, lax.rsqrt(var + 1e-05)

    col = lax.broadcasted_iota(jnp.int32, (width, chans), 0)

    def place(source, f, slot, mean, scale, keep):
        for r in range(height):
            value = (source[f, r].astype(F32) - mean) * scale
            if keep is not None:
                value = jnp.where(keep, value, 0.0)
            left = jnp.where(col == 0, 0.0, pltpu.roll(value, 1, 0))
            right = jnp.where(col == width - 1, 0.0, pltpu.roll(value, width - 1, 0))
            xs[slot, r + 1, :, 0:chans] = left.astype(BF16)
            xs[slot, r + 1, :, chans : 2 * chans] = value.astype(BF16)
            xs[slot, r + 1, :, 2 * chans : 3 * chans] = right.astype(BF16)

    same = jnp.full((1, chans), first1 <= t0, jnp.bool_).astype(F32)
    block = min(8, height)

    def patches(slot, r):
        parts = [xs[slot, r + dy : r + dy + block].reshape(block * width, 3 * chans) for dy in range(3)]
        return jnp.concatenate(parts, axis=1)

    def taps(k):
        return kern[k].reshape(9 * chans, chans)

    def dot(a, b):
        return jnp.dot(a, b, preferred_element_type=F32)

    place(vid, 0, 2, *moments(first0, t0), None)
    place(vid, 1, 3, *moments(first1, t0 + 1), None)
    for r in range(0, height, block):
        both = dot(patches(2, r), jnp.concatenate([taps(2), taps(1)], axis=1))
        own = dot(patches(3, r), taps(2))
        px = pl.ds(r * width, block * width)
        acc[0, px] = both[:, :chans]
        acc[1, px] = both[:, chans:] * same + own

    keep1 = jnp.full((1, chans), first0 <= t0 - 1, jnp.bool_)
    keep0 = jnp.full((1, chans), first0 <= t0 - 2, jnp.bool_)
    halos[1].wait_recv()
    place(halo, 1, 1, *moments(first0, t0 - 1), keep1)
    for r in range(0, height, block):
        both = dot(patches(1, r), jnp.concatenate([taps(1), taps(0)], axis=1))
        px = pl.ds(r * width, block * width)
        acc[0, px] += both[:, :chans]
        acc[1, px] += both[:, chans:] * same
    halos[0].wait_recv()
    place(halo, 0, 0, *moments(first0, t0 - 2), keep0)
    for r in range(0, height, block):
        px = pl.ds(r * width, block * width)
        acc[0, px] += dot(patches(0, r), taps(0))

    bias = bias_ref[...]
    for f in range(frames):
        for i in range(half_h):
            value = acc[f, i * 2 * width : (i + 1) * 2 * width] + bias
            logistic = 1.0 / (1.0 + jnp.exp(-value))
            active = value * logistic
            pool[f * half_h + i] = active[:width] + active[width:]
            slope = logistic * (1.0 + value * (1.0 - logistic))
            over = spread[f * half_h + i]
            dconv = jnp.concatenate([over, over], axis=0) * slope
            turned = dconv.T
            dts[f * chans : (f + 1) * chans, i * 2 * width : (i + 1) * 2 * width] = turned.astype(BF16)
            if f == 1:
                dtm[:, i * 2 * width : (i + 1) * 2 * width] = (turned * same[0:1, 0:1]).astype(BF16)
    for f in range(frames):
        for i in range(half_h):
            even = pool[f * half_h + i, pl.ds(0, half_w, stride=2), :]
            odd = pool[f * half_h + i, pl.ds(1, half_w, stride=2), :]
            down_ref[0, f, i] = ((even + odd) * 0.25).astype(BF16)

    for dy in range(3):
        shifted = [xs[s, dy : dy + height].reshape(pixels, 3 * chans) for s in range(4)]
        d0 = dts[0:chans]
        d1 = dts[chans : 2 * chans]
        two = jnp.concatenate([d0, dtm[...]], axis=0)
        r0 = dot(d0, shifted[0])
        r1 = dot(two, shifted[1])
        r2 = dot(two, shifted[2])
        r3 = dot(d1, shifted[3])
        sums = [r0 + r1[chans:], r1[:chans] + r2[chans:], r2[:chans] + r3]
        for k in range(3):
            for dx in range(3):
                tile = sums[k][:, dx * chans : (dx + 1) * chans].T.astype(BF16)
                tap = (k * 3 + dy) * 3 + dx
                for h in range(2):
                    for q in range(4):
                        j = tap * 4 + q
                        start = (h * 4 + q) * 16
                        grads[h, j // used, j % used] = tile[start : start + 16]

    swap = remote(grads.at[1 - core, :, pl.ds(0, used)], r_pair, pair_send.at[0], pair_recv.at[0], sibling)
    swap.start()
    swap.wait_recv()
    for o in range(n_plane):
        part[o] = (grads[core, o, 0:used].astype(F32) + r_pair[o].astype(F32)).astype(BF16)

    out_plane = []
    for d in range(1, n_plane):
        q = (plane + d) % n_plane
        out_plane.append(
            remote(part.at[q], r_plane.at[plane], plane_send.at[d], plane_recv.at[plane], plane_peer(q))
        )
    for copy in out_plane:
        copy.start()
    total = part[plane].astype(F32)
    for d in range(1, n_plane):
        q = (plane + n_plane - d) % n_plane
        remote(part.at[q], r_plane.at[q], plane_send.at[d], plane_recv.at[q], plane_peer(q)).wait_recv()
        total = total + r_plane[q].astype(F32)
    a32[0:used] = total
    a16[...] = a32[...].astype(BF16)

    out_z = []
    for d in range(1, nz):
        q = (z + d) % nz
        out_z.append(
            remote(a16.at[pl.ds(q * zt, zt)], r_z.at[z], z_send.at[d], z_recv.at[z], z_peer(q))
        )
    for copy in out_z:
        copy.start()
    total = a32[pl.ds(z * zt, zt)]
    for d in range(1, nz):
        q = (z + nz - d) % nz
        remote(a16.at[pl.ds(0, zt)], r_z.at[q], z_send.at[d], z_recv.at[q], z_peer(q)).wait_recv()
        total = total + r_z[q].astype(F32)
    full[core, plane, pl.ds(z * zt, zt)] = total.astype(BF16)

    mine = full.at[core, plane]
    out_zg = []
    for d in range(1, nz):
        q = (z + d) % nz
        own = mine.at[pl.ds(z * zt, zt)]
        out_zg.append(remote(own, own, zg_send.at[d], zg_recv.at[z], z_peer(q)))
    for copy in out_zg:
        copy.start()
    for d in range(1, nz):
        q = (z + nz - d) % nz
        theirs = mine.at[pl.ds(q * zt, zt)]
        remote(theirs, theirs, zg_send.at[d], zg_recv.at[q], z_peer(q)).wait_recv()

    out_pg = []
    for d in range(1, n_plane):
        q = (plane + d) % n_plane
        own = full.at[core, plane]
        out_pg.append(remote(own, own, pg_send.at[d], pg_recv.at[plane], plane_peer(q)))
    for copy in out_pg:
        copy.start()
    for d in range(1, n_plane):
        q = (plane + n_plane - d) % n_plane
        theirs = full.at[core, q]
        remote(theirs, theirs, pg_send.at[d], pg_recv.at[q], plane_peer(q)).wait_recv()

    give = remote(full.at[core], full.at[core], cg_send.at[0], cg_recv.at[0], sibling)
    give.start()
    keep = pltpu.make_async_copy(full.at[core], grad_hbm.at[core], local_sem.at[3])
    keep.start()
    remote(full.at[1 - core], full.at[1 - core], cg_send.at[0], cg_recv.at[0], sibling).wait_recv()
    take = pltpu.make_async_copy(full.at[1 - core], grad_hbm.at[1 - core], local_sem.at[4])
    take.start()

    for copy in halos + stats + [swap] + out_plane + out_z + out_zg + out_pg + [give]:
        copy.wait_send()
    keep.wait()
    take.wait()


def per_device(nx, nz, ny, video, clip_first, kernel, bias, cotangent):
    _, frames, height, width, chans = video.shape
    half_h, half_w = height // 2, width // 2
    n_plane, n_tm = nx * ny, nx * nz
    used = -(-TILES // n_plane)
    zt = -(-used // nz)
    slots = zt * nz
    any_space = pl.BlockSpec(memory_space=pl.ANY)
    vmem = pl.BlockSpec(memory_space=pltpu.VMEM)
    smem = pl.BlockSpec(memory_space=pltpu.SMEM)
    sem = pltpu.SemaphoreType.DMA
    down, grad = pl.pallas_call(
        functools.partial(fused, nx, nz, ny),
        out_shape=(
            jax.ShapeDtypeStruct(cotangent.shape, BF16),
            jax.ShapeDtypeStruct((2, n_plane, slots, 16, chans), BF16),
        ),
        in_specs=[smem, vmem, any_space, any_space, any_space],
        out_specs=(vmem, any_space),
        scratch_shapes=[
            pltpu.VMEM((frames, height, width, chans), BF16),
            pltpu.VMEM((frames, height, width, chans), BF16),
            pltpu.VMEM((3, 3, 3, chans, chans), BF16),
            pltpu.VMEM((frames, half_h, half_w, chans), BF16),
            pltpu.VMEM((4, height + 2, width, 3 * chans), BF16),
            pltpu.VMEM((frames, height * width, chans), F32),
            pltpu.VMEM((frames * half_h, width, chans), F32),
            pltpu.VMEM((frames * half_h, width, chans), F32),
            pltpu.VMEM((frames * chans, height * width), BF16),
            pltpu.VMEM((chans, height * width), BF16),
            pltpu.VMEM((n_tm, 8, chans), F32),
            pltpu.VMEM((2, n_plane, slots, 16, chans), BF16),
            pltpu.VMEM((n_plane, used, 16, chans), BF16),
            pltpu.VMEM((n_plane, used, 16, chans), BF16),
            pltpu.VMEM((n_plane, used, 16, chans), BF16),
            pltpu.VMEM((slots, 16, chans), F32),
            pltpu.VMEM((slots, 16, chans), BF16),
            pltpu.VMEM((nz, zt, 16, chans), BF16),
            pltpu.VMEM((2, n_plane, slots, 16, chans), BF16),
            sem((5,)),
            sem((2,)),
            sem((2,)),
            sem((n_tm,)),
            sem((n_tm,)),
            sem((1,)),
            sem((1,)),
            sem((n_plane,)),
            sem((n_plane,)),
            sem((nz,)),
            sem((nz,)),
            sem((nz,)),
            sem((nz,)),
            sem((n_plane,)),
            sem((n_plane,)),
            sem((1,)),
            sem((1,)),
        ],
        compiler_params=pltpu.CompilerParams(
            collective_id=0, has_side_effects=True, vmem_limit_bytes=48 * 1024 * 1024
        ),
    )(clip_first, bias.reshape(1, chans), video, kernel, cotangent)
    grad = grad[:, :, :used].reshape(2, n_plane * used, 16, chans)[:, :TILES]
    grad = grad.reshape(2, 27, chans // 2, chans).transpose(1, 0, 2, 3)
    return down, grad.reshape(3, 3, 3, chans, chans).astype(F32)


def solution(mesh):
    n_tm, n_dp = mesh.shape["tm"], mesh.shape["dp"]
    nz = 8 if n_tm == 32 else 2
    in_specs = (
        P("dp", "tm", None, None, None),
        P("dp", "tm"),
        P(),
        P(),
        P("dp", "tm", None, None, None),
    )
    out_specs = (P("dp", "tm", None, None, None), P())
    return jax.shard_map(
        functools.partial(per_device, n_tm // nz, nz, n_dp // 2),
        mesh=mesh,
        in_specs=in_specs,
        out_specs=out_specs,
        check_vma=False,
    )
```

```python
import functools

import jax
import jax.numpy as jnp
from jax import lax
from jax.experimental import pallas as pl
from jax.experimental.pallas import tpu as pltpu
from jax.sharding import PartitionSpec as P

F32 = jnp.float32
BF16 = jnp.bfloat16
HALF = 14 * 8


def fused(
    nx,
    nz,
    ny,
    first_hbm,
    bias_hbm,
    video_hbm,
    kern_hbm,
    cot_hbm,
    down_ref,
    grad_hbm,
    first_ref,
    bias_ref,
    vid,
    halo,
    kern,
    cot,
    xs,
    acc,
    spread,
    pool,
    dts,
    dtm,
    gath,
    grads,
    r_pair,
    part,
    r_plane,
    a32,
    a16,
    r_z,
    full,
    local_sem,
    keep_sem,
    halo_send,
    halo_recv,
    stat_send,
    stat_recv,
    pair_send,
    pair_recv,
    plane_send,
    plane_recv,
    z_send,
    z_recv,
    zg_send,
    zg_recv,
    pg_send,
    pg_recv,
    cg_send,
    cg_recv,
):
    _, frames, height, width, chans = video_hbm.shape
    half_h, half_w = height // 2, width // 2
    pixels = height * width
    n_plane = nx * ny
    n_tm = nx * nz
    used = HALF // n_plane
    zt = -(-used // nz)

    tm = lax.axis_index("tm")
    dp = lax.axis_index("dp")
    x, z = tm // nz, tm % nz
    y, core = dp // 2, dp % 2
    plane = x * ny + y

    def at(tm_to, dp_to):
        return {"tm": tm_to, "dp": dp_to}

    def plane_peer(q):
        return at((q // ny) * nz + z, (q % ny) * 2 + core)

    def z_peer(q):
        return at(x * nz + q, dp)

    sibling = at(tm, y * 2 + 1 - core)

    def remote(src, dst, send, recv, to):
        return pltpu.make_async_remote_copy(
            src_ref=src,
            dst_ref=dst,
            send_sem=send,
            recv_sem=recv,
            device_id=to,
            device_id_type=pl.DeviceIdType.MESH,
        )

    loads = [
        pltpu.make_async_copy(video_hbm.at[0], vid, local_sem.at[0]),
        pltpu.make_async_copy(cot_hbm.at[0], cot, local_sem.at[1]),
        pltpu.make_async_copy(kern_hbm, kern, local_sem.at[2]),
        pltpu.make_async_copy(first_hbm, first_ref, local_sem.at[3]),
        pltpu.make_async_copy(bias_hbm, bias_ref, local_sem.at[4]),
    ]
    for load in loads:
        load.start()

    barrier = pltpu.get_barrier_semaphore()
    peers = [sibling]
    peers += [at((tm + d) % n_tm, dp) for d in range(1, n_tm)]
    for d in range(1, n_plane):
        q = (plane + d) % n_plane
        peers.append(plane_peer(q))
    for peer in peers:
        pl.semaphore_signal(barrier, inc=1, device_id=peer, device_id_type=pl.DeviceIdType.MESH)

    loads[0].wait()
    rows = []
    for f in range(frames):
        value = vid[f].astype(F32)
        rows.append(jnp.sum(jnp.sum(value, axis=0), axis=0, keepdims=True))
        rows.append(jnp.sum(jnp.sum(value * value, axis=0), axis=0, keepdims=True))
    rows.append(jnp.zeros((4, chans), F32))
    stat = jnp.concatenate(rows, axis=0)
    lane = lax.broadcasted_iota(jnp.int32, (8, chans), 1)
    stat = stat + jnp.where(lane % 2 == 0, pltpu.roll(stat, chans - 1, 1), pltpu.roll(stat, 1, 1))
    stat = stat + jnp.where(lane % 4 < 2, pltpu.roll(stat, chans - 2, 1), pltpu.roll(stat, 2, 1))
    gath[tm] = stat

    pl.semaphore_wait(barrier, len(peers))

    following = at((tm + 1) % n_tm, dp)
    halos = [
        remote(video_hbm.at[0, f], halo.at[f], halo_send.at[f], halo_recv.at[f], following)
        for f in range(frames)
    ]
    stats = []
    for d in range(1, n_tm):
        stats.append(
            remote(
                gath.at[tm],
                gath.at[tm],
                stat_send.at[d],
                stat_recv.at[tm],
                at((tm + d) % n_tm, dp),
            )
        )
    for copy in stats:
        copy.start()
    halos[1].start()
    halos[0].start()

    loads[1].wait()
    for f in range(frames):
        for i in range(half_h):
            quarter = cot[f, i].astype(F32) * 0.25
            spread[f * half_h + i, pl.ds(0, half_w, stride=2), :] = quarter
            spread[f * half_h + i, pl.ds(1, half_w, stride=2), :] = quarter
    rim = jnp.zeros((width, 3 * chans), BF16)
    for s in range(4):
        xs[s, 0] = rim
        xs[s, height + 1] = rim
    blank = jnp.zeros((16, chans), BF16)
    for j in range(27 * 8, 2 * HALF):
        grads[j] = blank

    loads[3].wait()
    loads[4].wait()
    first0 = first_ref[0, 0]
    first1 = first_ref[0, 1]
    t0 = tm * frames
    loads[2].wait()

    for d in range(1, n_tm):
        q = (tm + d) % n_tm
        remote(
            gath.at[tm], gath.at[q], stat_send.at[d], stat_recv.at[q], at(q, dp)
        ).wait_recv()

    gathered = gath[...]
    row = lax.broadcasted_iota(jnp.int32, gathered.shape, 1)
    frame = lax.broadcasted_iota(jnp.int32, gathered.shape, 0) * frames + row // 2

    def moments(first, last):
        chosen = jnp.where((frame >= first) & (frame <= last) & (row < 4), gathered, 0.0)
        total = jnp.sum(chosen, axis=0)
        number = jnp.maximum((last - first + 1) * (pixels * 4), 1)
        count = jnp.full((1, chans), number, jnp.int32).astype(F32)
        mean = (total[0:1] + total[2:3]) / count
        var = (total[1:2] + total[3:4]) / count - mean * mean
        return mean, lax.rsqrt(var + 1e-05)

    col = lax.broadcasted_iota(jnp.int32, (width, chans), 0)

    def place(source, f, slot, mean, scale, keep):
        for r in range(height):
            value = (source[f, r].astype(F32) - mean) * scale
            if keep is not None:
                value = jnp.where(keep, value, 0.0)
            left = jnp.where(col == 0, 0.0, pltpu.roll(value, 1, 0))
            right = jnp.where(col == width - 1, 0.0, pltpu.roll(value, width - 1, 0))
            xs[slot, r + 1, :, 0:chans] = left.astype(BF16)
            xs[slot, r + 1, :, chans : 2 * chans] = value.astype(BF16)
            xs[slot, r + 1, :, 2 * chans : 3 * chans] = right.astype(BF16)

    same = jnp.full((1, chans), first1 <= t0, jnp.bool_).astype(F32)
    block = min(8, height)

    def patches(slot, r):
        parts = [xs[slot, r + dy : r + dy + block].reshape(block * width, 3 * chans) for dy in range(3)]
        return jnp.concatenate(parts, axis=1)

    def taps(k):
        return kern[k].reshape(9 * chans, chans)

    def dot(a, b):
        return jnp.dot(a, b, preferred_element_type=F32)

    place(vid, 0, 2, *moments(first0, t0), None)
    place(vid, 1, 3, *moments(first1, t0 + 1), None)
    for r in range(0, height, block):
        both = dot(patches(2, r), jnp.concatenate([taps(2), taps(1)], axis=1))
        own = dot(patches(3, r), taps(2))
        px = pl.ds(r * width, block * width)
        acc[0, px] = both[:, :chans]
        acc[1, px] = both[:, chans:] * same + own

    keep1 = jnp.full((1, chans), first0 <= t0 - 1, jnp.bool_)
    keep0 = jnp.full((1, chans), first0 <= t0 - 2, jnp.bool_)
    halos[1].wait_recv()
    place(halo, 1, 1, *moments(first0, t0 - 1), keep1)
    for r in range(0, height, block):
        both = dot(patches(1, r), jnp.concatenate([taps(1), taps(0)], axis=1))
        px = pl.ds(r * width, block * width)
        acc[0, px] += both[:, :chans]
        acc[1, px] += both[:, chans:] * same
    halos[0].wait_recv()
    place(halo, 0, 0, *moments(first0, t0 - 2), keep0)
    for r in range(0, height, block):
        px = pl.ds(r * width, block * width)
        acc[0, px] += dot(patches(0, r), taps(0))

    bias = bias_ref[...]
    for f in range(frames):
        for i in range(half_h):
            value = acc[f, i * 2 * width : (i + 1) * 2 * width] + bias
            logistic = 1.0 / (1.0 + jnp.exp(-value))
            active = value * logistic
            pool[f * half_h + i] = active[:width] + active[width:]
            slope = logistic * (1.0 + value * (1.0 - logistic))
            over = spread[f * half_h + i]
            dconv = jnp.concatenate([over, over], axis=0) * slope
            turned = dconv.T
            dts[f * chans : (f + 1) * chans, i * 2 * width : (i + 1) * 2 * width] = turned.astype(BF16)
            if f == 1:
                dtm[:, i * 2 * width : (i + 1) * 2 * width] = (turned * same[0:1, 0:1]).astype(BF16)
    for f in range(frames):
        for i in range(half_h):
            even = pool[f * half_h + i, pl.ds(0, half_w, stride=2), :]
            odd = pool[f * half_h + i, pl.ds(1, half_w, stride=2), :]
            down_ref[0, f, i] = ((even + odd) * 0.25).astype(BF16)

    for dy in range(3):
        shifted = [xs[s, dy : dy + height].reshape(pixels, 3 * chans) for s in range(4)]
        d0 = dts[0:chans]
        d1 = dts[chans : 2 * chans]
        two = jnp.concatenate([d0, dtm[...]], axis=0)
        r0 = dot(d0, shifted[0])
        r1 = dot(two, shifted[1])
        r2 = dot(two, shifted[2])
        r3 = dot(d1, shifted[3])
        sums = [r0 + r1[chans:], r1[:chans] + r2[chans:], r2[:chans] + r3]
        for k in range(3):
            for dx in range(3):
                tile = sums[k][:, dx * chans : (dx + 1) * chans].T.astype(BF16)
                spot = ((dy * 3 + k) * 3 + dx) * 8
                for q in range(8):
                    grads[spot + q] = tile[q * 16 : (q + 1) * 16]

    swap = remote(
        grads.at[pl.ds((1 - core) * HALF, HALF)], r_pair, pair_send.at[0], pair_recv.at[0], sibling
    )
    swap.start()
    swap.wait_recv()
    for o in range(n_plane):
        tiles = pl.ds(o * used, used)
        own = grads[pl.ds(core * HALF + o * used, used)].astype(F32)
        part[tiles] = (own + r_pair[tiles].astype(F32)).astype(BF16)

    def owned(q):
        return pl.ds(q * used, used)

    out_plane = []
    for d in range(1, n_plane):
        q = (plane + d) % n_plane
        out_plane.append(
            remote(
                part.at[owned(q)], r_plane.at[plane], plane_send.at[d], plane_recv.at[plane], plane_peer(q)
            )
        )
    for copy in out_plane:
        copy.start()
    total = part[owned(plane)].astype(F32)
    for d in range(1, n_plane):
        q = (plane + n_plane - d) % n_plane
        remote(
            part.at[owned(q)], r_plane.at[q], plane_send.at[d], plane_recv.at[q], plane_peer(q)
        ).wait_recv()
        total = total + r_plane[q].astype(F32)
    a32[...] = total
    a16[...] = total.astype(BF16)

    def owns(q):
        return q * zt < used

    def tiles_of(q):
        return pl.ds(core * HALF + plane * used + q * zt, zt)

    for d in range(1, nz):
        q = (z + d) % nz

        @pl.when(owns(q))
        def _():
            remote(
                a16.at[pl.ds(q * zt, zt)], r_z.at[z], z_send.at[d], z_recv.at[z], z_peer(q)
            ).start()

    @pl.when(owns(z))
    def _():
        total = a32[pl.ds(z * zt, zt)]
        for d in range(1, nz):
            q = (z + nz - d) % nz
            remote(a16.at[pl.ds(0, zt)], r_z.at[q], z_send.at[d], z_recv.at[q], z_peer(q)).wait_recv()
            total = total + r_z[q].astype(F32)
        full[tiles_of(z)] = total.astype(BF16)
        own = full.at[tiles_of(z)]
        for d in range(1, nz):
            q = (z + d) % nz
            remote(own, own, zg_send.at[d], zg_recv.at[z], z_peer(q)).start()

    for d in range(1, nz):
        q = (z + nz - d) % nz

        @pl.when(owns(q))
        def _():
            theirs = full.at[tiles_of(q)]
            remote(theirs, theirs, zg_send.at[d], zg_recv.at[q], z_peer(q)).wait_recv()

    def gathered_at(half, q):
        return full.at[pl.ds(half * HALF + q * used, used)]

    out_pg = []
    for d in range(1, n_plane):
        q = (plane + d) % n_plane
        own = gathered_at(core, plane)
        out_pg.append(remote(own, own, pg_send.at[d], pg_recv.at[plane], plane_peer(q)))
    for copy in out_pg:
        copy.start()
    for d in range(1, n_plane):
        q = (plane + n_plane - d) % n_plane
        theirs = gathered_at(core, q)
        remote(theirs, theirs, pg_send.at[d], pg_recv.at[q], plane_peer(q)).wait_recv()

    mine, other = full.at[pl.ds(core * HALF, HALF)], full.at[pl.ds((1 - core) * HALF, HALF)]
    give = remote(mine, mine, cg_send.at[0], cg_recv.at[0], sibling)
    give.start()
    remote(other, other, cg_send.at[0], cg_recv.at[0], sibling).wait_recv()
    keeps = []
    for dy in range(3):
        for k in range(3):
            keeps.append(
                pltpu.make_async_copy(
                    full.at[pl.ds((dy * 3 + k) * 24, 24)],
                    grad_hbm.at[pl.ds((k * 3 + dy) * 24, 24)],
                    keep_sem.at[dy * 3 + k],
                )
            )
    for copy in keeps:
        copy.start()

    for copy in halos + stats + [swap] + out_plane + out_pg + [give]:
        copy.wait_send()
    for d in range(1, nz):
        q = (z + d) % nz

        @pl.when(owns(q))
        def _():
            remote(
                a16.at[pl.ds(q * zt, zt)], r_z.at[z], z_send.at[d], z_recv.at[z], z_peer(q)
            ).wait_send()

    @pl.when(owns(z))
    def _():
        own = full.at[tiles_of(z)]
        for d in range(1, nz):
            q = (z + d) % nz
            remote(own, own, zg_send.at[d], zg_recv.at[z], z_peer(q)).wait_send()

    for copy in keeps:
        copy.wait()


def per_device(nx, nz, ny, video, clip_first, kernel, bias, cotangent):
    _, frames, height, width, chans = video.shape
    half_h, half_w = height // 2, width // 2
    n_plane, n_tm = nx * ny, nx * nz
    used = HALF // n_plane
    zt = -(-used // nz)
    any_space = pl.BlockSpec(memory_space=pl.ANY)
    vmem = pl.BlockSpec(memory_space=pltpu.VMEM)
    sem = pltpu.SemaphoreType.DMA
    down, grad = pl.pallas_call(
        functools.partial(fused, nx, nz, ny),
        out_shape=(
            jax.ShapeDtypeStruct(cotangent.shape, BF16),
            jax.ShapeDtypeStruct((27 * 8, 16, chans), BF16),
        ),
        in_specs=[any_space] * 5,
        out_specs=(vmem, any_space),
        scratch_shapes=[
            pltpu.SMEM(clip_first.shape, jnp.int32),
            pltpu.VMEM((1, chans), F32),
            pltpu.VMEM((frames, height, width, chans), BF16),
            pltpu.VMEM((frames, height, width, chans), BF16),
            pltpu.VMEM((3, 3, 3, chans, chans), BF16),
            pltpu.VMEM((frames, half_h, half_w, chans), BF16),
            pltpu.VMEM((4, height + 2, width, 3 * chans), BF16),
            pltpu.VMEM((frames, height * width, chans), F32),
            pltpu.VMEM((frames * half_h, width, chans), F32),
            pltpu.VMEM((frames * half_h, width, chans), F32),
            pltpu.VMEM((frames * chans, height * width), BF16),
            pltpu.VMEM((chans, height * width), BF16),
            pltpu.VMEM((n_tm, 8, chans), F32),
            pltpu.VMEM((2 * HALF, 16, chans), BF16),
            pltpu.VMEM((HALF, 16, chans), BF16),
            pltpu.VMEM((HALF, 16, chans), BF16),
            pltpu.VMEM((n_plane, used, 16, chans), BF16),
            pltpu.VMEM((used, 16, chans), F32),
            pltpu.VMEM((used, 16, chans), BF16),
            pltpu.VMEM((nz, zt, 16, chans), BF16),
            pltpu.VMEM((2 * HALF, 16, chans), BF16),
            sem((5,)),
            sem((9,)),
            sem((2,)),
            sem((2,)),
            sem((n_tm,)),
            sem((n_tm,)),
            sem((1,)),
            sem((1,)),
            sem((n_plane,)),
            sem((n_plane,)),
            sem((nz,)),
            sem((nz,)),
            sem((nz,)),
            sem((nz,)),
            sem((n_plane,)),
            sem((n_plane,)),
            sem((1,)),
            sem((1,)),
        ],
        compiler_params=pltpu.CompilerParams(
            collective_id=0, has_side_effects=True, vmem_limit_bytes=62 * 1024 * 1024
        ),
    )(clip_first, bias.reshape(1, chans), video, kernel, cotangent)
    return down, grad.reshape(3, 3, 3, chans, chans).astype(F32)


def solution(mesh):
    n_tm, n_dp = mesh.shape["tm"], mesh.shape["dp"]
    nz = 8 if n_tm == 32 else 2
    in_specs = (
        P("dp", "tm", None, None, None),
        P("dp", "tm"),
        P(),
        P(),
        P("dp", "tm", None, None, None),
    )
    out_specs = (P("dp", "tm", None, None, None), P())
    return jax.shard_map(
        functools.partial(per_device, n_tm // nz, nz, n_dp // 2),
        mesh=mesh,
        in_specs=in_specs,
        out_specs=out_specs,
        check_vma=False,
    )
```

```python
import functools

import jax
import jax.numpy as jnp
from jax import lax
from jax.experimental import pallas as pl
from jax.experimental.pallas import tpu as pltpu
from jax.sharding import PartitionSpec as P

F32 = jnp.float32
BF16 = jnp.bfloat16
HALF = 28 * 4
CHUNK = 9 * 4


def fused(
    nx,
    nz,
    ny,
    sa,
    sb,
    first_hbm,
    bias_hbm,
    video_hbm,
    kern_hbm,
    cot_hbm,
    down_hbm,
    grad_hbm,
    first_ref,
    bias_ref,
    vid,
    halo,
    kern,
    cot,
    xs,
    acc,
    spread,
    pool,
    down,
    dts,
    gath,
    grads,
    r_pair,
    part,
    r1a,
    r1b,
    s1a,
    s1b,
    r2a,
    r2b,
    s2a,
    s2b,
    r3a,
    r3b,
    full,
    local_sem,
    near_send,
    near_recv,
    stat_send,
    stat_recv,
    pair_send,
    pair_recv,
    a1_send,
    a1_recv,
    b1_send,
    b1_recv,
    a2_send,
    a2_recv,
    b2_send,
    b2_recv,
    a3_send,
    a3_recv,
    b3_send,
    b3_recv,
    a4_send,
    a4_recv,
    b4_send,
    b4_recv,
    a5_send,
    a5_recv,
    b5_send,
    b5_recv,
    a6_send,
    a6_recv,
    b6_send,
    b6_recv,
):
    _, frames, height, width, chans = video_hbm.shape
    half_h, half_w = height // 2, width // 2
    pixels = height * width
    n_tm = nx * nz
    n_a = nx * ny * sa

    tm = lax.axis_index("tm")
    dp = lax.axis_index("dp")
    x, z = tm // nz, tm % nz
    y, core = dp // 2, dp % 2

    def at(tm_to, dp_to):
        return {"tm": tm_to, "dp": dp_to}

    def x_peer(q):
        return at(q * nz + z, dp)

    def y_peer(q):
        return at(tm, q * 2 + core)

    def z_peer(q):
        return at(x * nz + q, dp)

    sibling = at(tm, y * 2 + 1 - core)
    right = at((tm + 1) % n_tm, dp)
    left = at((tm + n_tm - 1) % n_tm, dp)

    def remote(src, dst, send, recv, to):
        return pltpu.make_async_remote_copy(
            src_ref=src,
            dst_ref=dst,
            send_sem=send,
            recv_sem=recv,
            device_id=to,
            device_id_type=pl.DeviceIdType.MESH,
        )

    loads = [
        pltpu.make_async_copy(video_hbm.at[0], vid, local_sem.at[0]),
        pltpu.make_async_copy(first_hbm, first_ref, local_sem.at[1]),
        pltpu.make_async_copy(cot_hbm.at[0, 1], cot.at[0], local_sem.at[2]),
        pltpu.make_async_copy(bias_hbm, bias_ref, local_sem.at[3]),
        pltpu.make_async_copy(kern_hbm, kern, local_sem.at[4]),
    ]
    for load in loads:
        load.start()

    barrier = pltpu.get_barrier_semaphore()
    peers = [at((tm + d) % n_tm, dp) for d in range(1, n_tm)]
    peers += [y_peer((y + d) % ny) for d in range(1, ny)]
    peers += [sibling]
    for peer in peers:
        pl.semaphore_signal(barrier, inc=1, device_id=peer, device_id_type=pl.DeviceIdType.MESH)

    loads[0].wait()
    loads[1].wait()
    rows = []
    for f in range(frames):
        value = vid[f].astype(F32)
        rows.append(jnp.sum(jnp.sum(value, axis=0), axis=0, keepdims=True))
        rows.append(jnp.sum(jnp.sum(value * value, axis=0), axis=0, keepdims=True))
    rows.append(jnp.zeros((4, chans), F32))
    stat = jnp.concatenate(rows, axis=0)
    lane8 = lax.broadcasted_iota(jnp.int32, (8, chans), 1)
    stat = stat + jnp.where(lane8 % 2 == 0, pltpu.roll(stat, chans - 1, 1), pltpu.roll(stat, 1, 1))
    stat = stat + jnp.where(lane8 % 4 < 2, pltpu.roll(stat, chans - 2, 1), pltpu.roll(stat, 2, 1))
    lane = lax.broadcasted_iota(jnp.int32, (1, chans), 1)
    low = jnp.where(lane % 2 == 0, stat[0:1], stat[1:2])
    high = jnp.where(lane % 2 == 0, stat[2:3], stat[3:4])
    first0 = jnp.full((1, chans), first_ref[0, 0], jnp.int32)
    first1 = jnp.full((1, chans), first_ref[0, 1], jnp.int32)
    gath[tm, 0:1] = jnp.where(lane % 4 < 2, low, high)
    gath[tm, 1:2] = first0.astype(F32)

    pl.semaphore_wait(barrier, len(peers))

    near = [
        remote(video_hbm.at[0, 1], halo.at[0], near_send.at[0], near_recv.at[0], right),
        remote(video_hbm.at[0, 0], halo.at[1], near_send.at[1], near_recv.at[1], left),
        remote(cot_hbm.at[0, 0], cot.at[1], near_send.at[2], near_recv.at[2], left),
    ]
    for d in range(1, n_tm):
        remote(gath.at[tm], gath.at[tm], stat_send.at[0], stat_recv.at[0], at((tm + d) % n_tm, dp)).start()
    for copy in near:
        copy.start()

    rim = jnp.zeros((width, 3 * chans), BF16)
    for s in range(4):
        xs[s, 0] = rim
        xs[s, height + 1] = rim
    for h in range(2):
        for j in range(27 * 4, HALF):
            grads[h * HALF + j] = jnp.zeros((16, chans), BF16)

    def widen(f):
        for i in range(half_h):
            quarter = cot[f, i].astype(F32) * 0.25
            spread[f * half_h + i, pl.ds(0, half_w, stride=2), :] = quarter
            spread[f * half_h + i, pl.ds(1, half_w, stride=2), :] = quarter

    loads[2].wait()
    widen(0)
    loads[3].wait()
    loads[4].wait()

    others = gath.at[pl.ds(0, n_tm - 1)]
    remote(others, others, stat_send.at[0], stat_recv.at[0], right).wait_recv()

    t0 = tm * frames
    t2 = (t0 + 2) % (n_tm * frames)
    first2 = gath[(tm + 1) % n_tm, 1:2].astype(jnp.int32)
    gathered = gath[...]
    frame = lax.broadcasted_iota(jnp.int32, gathered.shape, 0) * frames
    frame = frame + lax.broadcasted_iota(jnp.int32, gathered.shape, 2) % 4 // 2

    def moments(first, last):
        chosen = jnp.where((frame >= first[None]) & (frame <= last), gathered, 0.0)
        total = jnp.sum(chosen, axis=0)[0:1]
        count = jnp.maximum((last + 1 - first) * (pixels * 4), 1).astype(F32)
        total = total + jnp.where(lane % 4 < 2, pltpu.roll(total, chans - 2, 1), pltpu.roll(total, 2, 1))
        mean = jnp.where(lane % 2 == 0, total, pltpu.roll(total, 1, 1)) / count
        var = jnp.where(lane % 2 == 1, total, pltpu.roll(total, chans - 1, 1)) / count - mean * mean
        return mean, lax.rsqrt(var + 1e-05)

    col = lax.broadcasted_iota(jnp.int32, (width, chans), 0)

    def place(source, f, slot, mean, scale, keep):
        for r in range(height):
            value = (source[f, r].astype(F32) - mean) * scale
            if keep is not None:
                value = jnp.where(keep, value, 0.0)
            before = jnp.where(col == 0, 0.0, pltpu.roll(value, 1, 0))
            after = jnp.where(col == width - 1, 0.0, pltpu.roll(value, width - 1, 0))
            xs[slot, r + 1, :, 0:chans] = before.astype(BF16)
            xs[slot, r + 1, :, chans : 2 * chans] = value.astype(BF16)
            xs[slot, r + 1, :, 2 * chans : 3 * chans] = after.astype(BF16)

    def flag(condition):
        return jnp.where(condition, 1.0, 0.0)

    t0_t1 = flag(first1 <= t0)
    t0_t2 = flag(first2 <= t2 - 2)
    t1_t2 = flag(first2 <= t2 - 1)
    block = min(8, height)

    def patches(slot, r):
        parts = [xs[slot, r + dy : r + dy + block].reshape(block * width, 3 * chans) for dy in range(3)]
        return jnp.concatenate(parts, axis=1)

    def taps(k):
        return kern[k].reshape(9 * chans, chans)

    def dot(a, b):
        return jnp.dot(a, b, preferred_element_type=F32)

    place(vid, 0, 1, *moments(first0, t0), None)
    place(vid, 1, 2, *moments(first1, t0 + 1), None)
    for r in range(0, height, block):
        px = pl.ds(r * width, block * width)
        one = dot(patches(1, r), jnp.concatenate([taps(1), taps(0)], axis=1))
        two = dot(patches(2, r), jnp.concatenate([taps(2), taps(1)], axis=1))
        acc[0, px] = one[:, :chans] * t0_t1 + two[:, :chans]
        acc[1, px] = one[:, chans:] * t0_t2 + two[:, chans:] * t1_t2

    bias = bias_ref[...]

    def finish_conv(f, slot, k):
        for r in range(0, height, block):
            last = dot(patches(slot, r), taps(k))
            for m in range(block // 2):
                i = r // 2 + m
                px = slice(i * 2 * width, (i + 1) * 2 * width)
                value = acc[f, px] + last[m * 2 * width : (m + 1) * 2 * width] + bias
                logistic = 1.0 / (1.0 + jnp.exp(-value))
                active = value * logistic
                pool[f * half_h + i] = active[:width] + active[width:]
                slope = logistic * (1.0 + value * (1.0 - logistic))
                over = spread[f * half_h + i]
                dconv = jnp.concatenate([over, over], axis=0) * slope
                dts[f * chans : (f + 1) * chans, px] = dconv.T.astype(BF16)
        for i in range(half_h):
            even = pool[f * half_h + i, pl.ds(0, half_w, stride=2), :]
            odd = pool[f * half_h + i, pl.ds(1, half_w, stride=2), :]
            down[f, i] = ((even + odd) * 0.25).astype(BF16)

    near[0].wait_recv()
    place(halo, 0, 0, *moments(first1, t0 - 1), first1 <= t0 - 1)
    finish_conv(0, 0, 0)
    near[2].wait_recv()
    widen(1)
    near[1].wait_recv()
    place(halo, 1, 3, *moments(first2, t2), None)
    finish_conv(1, 3, 2)
    out_far = remote(down.at[1], down_hbm.at[0, 0], near_send.at[3], near_recv.at[3], right)
    out_near = pltpu.make_async_copy(down.at[0], down_hbm.at[0, 1], local_sem.at[5])
    out_far.start()
    out_near.start()

    sends = near + [out_far]

    def pair(c):
        tiles = pl.ds(c * CHUNK, CHUNK if c < 2 else HALF - 2 * CHUNK)
        src = grads.at[pl.ds((1 - core) * HALF + tiles.start, tiles.size)]
        return remote(src, r_pair.at[tiles], pair_send.at[c], pair_recv.at[c], sibling)

    def join_pair(c):
        pair(c).wait_recv()
        tiles = pl.ds(c * CHUNK, CHUNK if c < 2 else HALF - 2 * CHUNK)
        own = grads[pl.ds(core * HALF + tiles.start, tiles.size)].astype(F32)
        part[tiles] = (own + r_pair[tiles].astype(F32)).astype(BF16)

    def first_a(q):
        src = part.at[pl.ds(q * nx * sa, nx * sa)]
        return remote(src, r1a.at[y], a1_send.at[q], a1_recv.at[y], y_peer(q))

    def first_b(q):
        src = part.at[pl.ds(n_a + q * ny * sb, ny * sb)]
        return remote(src, r1b.at[x], b1_send.at[q], b1_recv.at[x], x_peer(q))

    def go(make, me, owners):
        for q in owners:

            @pl.when(q != me)
            def _():
                make(q).start()

    def a_ready(done):
        return [q for q in range(ny) if (q + 1) * nx * sa <= done]

    started = []
    for dy in range(3):
        shifted = [xs[s, dy : dy + height].reshape(pixels, 3 * chans) for s in range(4)]
        both = dts[...]
        r0 = dot(both[:chans], shifted[0])
        r1 = dot(both, shifted[1])
        r2 = dot(both, shifted[2])
        r3 = dot(both[chans:], shifted[3])
        m01, m02, m12 = t0_t1[:, 0:1], t0_t2[:, 0:1], t1_t2[:, 0:1]
        sums = [r0 + r1[chans:] * m02, r1[:chans] * m01 + r2[chans:] * m12, r2[:chans] + r3]
        for k in range(3):
            for dx in range(3):
                tile = sums[k][:, dx * chans : (dx + 1) * chans].T.astype(BF16)
                spot = ((dy * 3 + k) * 3 + dx) * 4
                for h in range(2):
                    for q in range(4):
                        start = (h * 4 + q) * 16
                        grads[h * HALF + spot + q] = tile[start : start + 16]
        sends.append(pair(dy))
        sends[-1].start()
        if dy > 0:
            join_pair(dy - 1)
            ready = [q for q in a_ready(dy * CHUNK) if q not in started]
            go(first_a, y, ready)
            started += ready
    join_pair(2)
    go(first_a, y, [q for q in range(ny) if q not in started])
    go(first_b, x, range(nx))

    def exchange(n, me, src_of, dst, send, recv, peer):
        copies = []
        for d in range(1, n):
            q = (me + d) % n
            copies.append(remote(src_of(q), dst.at[me], send.at[d], recv.at[me], peer(q)))
        return copies

    def arrived(n, me, dst, send, recv, peer):
        for d in range(1, n):
            q = (me + n - d) % n
            remote(dst.at[q], dst.at[q], send.at[d], recv.at[q], peer(q)).wait_recv()

    def summed(n, me, own, dst):
        total = own.astype(F32)
        for d in range(1, n):
            total = total + dst[(me + n - d) % n].astype(F32)
        return total.astype(BF16)

    arrived(ny, y, r1a, a1_send, a1_recv, y_peer)
    s1a[...] = summed(ny, y, part[pl.ds(y * nx * sa, nx * sa)], r1a)
    copies = exchange(nx, x, lambda q: s1a.at[pl.ds(q * sa, sa)], r2a, a2_send, a2_recv, x_peer)
    arrived_b = functools.partial(arrived, nx, x, r1b, b1_send, b1_recv, x_peer)
    for copy in copies:
        copy.start()
    sends += copies
    arrived_b()
    s1b[...] = summed(nx, x, part[pl.ds(n_a + x * ny * sb, ny * sb)], r1b)
    copies = exchange(ny, y, lambda q: s1b.at[pl.ds(q * sb, sb)], r2b, b2_send, b2_recv, y_peer)
    for copy in copies:
        copy.start()
    sends += copies

    arrived(nx, x, r2a, a2_send, a2_recv, x_peer)
    s2a[...] = summed(nx, x, s1a[pl.ds(x * sa, sa)], r2a)
    copies = exchange(nz, z, lambda q: s2a, r3a, a3_send, a3_recv, z_peer)
    for copy in copies:
        copy.start()
    sends += copies
    arrived(ny, y, r2b, b2_send, b2_recv, y_peer)
    s2b[...] = summed(ny, y, s1b[pl.ds(y * sb, sb)], r2b)
    copies = exchange(nz, z, lambda q: s2b, r3b, b3_send, b3_recv, z_peer)
    for copy in copies:
        copy.start()
    sends += copies

    base = core * HALF

    def a_line(q):
        return full.at[pl.ds(base + q * nx * sa, nx * sa)]

    def b_line(q):
        return full.at[pl.ds(base + n_a + q * ny * sb, ny * sb)]

    def a_piece(q):
        return full.at[pl.ds(base + (y * nx + q) * sa, sa)]

    def b_piece(q):
        return full.at[pl.ds(base + n_a + (x * ny + q) * sb, sb)]

    def spread_out(n, me, piece, send, recv, peer):
        copies = []
        for d in range(1, n):
            q = (me + d) % n
            copies.append(remote(piece(me), piece(me), send.at[d], recv.at[me], peer(q)))
            copies[-1].start()
        return copies

    def collected(n, me, piece, send, recv, peer, then=None):
        for d in range(1, n):
            q = (me + n - d) % n
            remote(piece(q), piece(q), send.at[d], recv.at[q], peer(q)).wait_recv()
            if then is not None:
                then(q)

    arrived(nz, z, r3a, a3_send, a3_recv, z_peer)
    full[pl.ds(base + (y * nx + x) * sa, sa)] = summed(nz, z, s2a[...], r3a)
    sends += spread_out(nx, x, a_piece, a4_send, a4_recv, x_peer)
    arrived(nz, z, r3b, b3_send, b3_recv, z_peer)
    full[pl.ds(base + n_a + (x * ny + y) * sb, sb)] = summed(nz, z, s2b[...], r3b)
    sends += spread_out(ny, y, b_piece, b4_send, b4_recv, y_peer)

    def give_a(q):
        sends.append(remote(a_line(q), a_line(q), a6_send.at[q], a6_recv.at[q], sibling))
        sends[-1].start()

    def give_b(q):
        sends.append(remote(b_line(q), b_line(q), b6_send.at[q], b6_recv.at[q], sibling))
        sends[-1].start()

    collected(nx, x, a_piece, a4_send, a4_recv, x_peer)
    sends += spread_out(ny, y, a_line, a5_send, a5_recv, y_peer)
    give_a(y)
    collected(ny, y, b_piece, b4_send, b4_recv, y_peer)
    sends += spread_out(nx, x, b_line, b5_send, b5_recv, x_peer)
    give_b(x)
    collected(ny, y, a_line, a5_send, a5_recv, y_peer, give_a)
    collected(nx, x, b_line, b5_send, b5_recv, x_peer, give_b)
    mine = pltpu.make_async_copy(
        full.at[pl.ds(base, HALF)], grad_hbm.at[pl.ds(base, HALF)], local_sem.at[6]
    )
    mine.start()
    base = (1 - core) * HALF
    for q in range(ny):
        remote(a_line(q), a_line(q), a6_send.at[q], a6_recv.at[q], sibling).wait_recv()
    for q in range(nx):
        remote(b_line(q), b_line(q), b6_send.at[q], b6_recv.at[q], sibling).wait_recv()
    theirs = pltpu.make_async_copy(
        full.at[pl.ds(base, HALF)], grad_hbm.at[pl.ds(base, HALF)], local_sem.at[7]
    )
    theirs.start()

    remote(others, others, stat_send.at[0], stat_recv.at[0], right).wait_send()
    for copy in sends:
        copy.wait_send()
    for make, me, n in ((first_a, y, ny), (first_b, x, nx)):
        for q in range(n):

            @pl.when(q != me)
            def _():
                make(q).wait_send()

    out_far.wait_recv()
    out_near.wait()
    mine.wait()
    theirs.wait()


def widen_result(grad_hbm, down_hbm, grad_out, down_out, tiles, wide, sems):
    pass_on = pltpu.make_async_copy(down_hbm, down_out, sems.at[0])
    loads = []
    for dy in range(3):
        for h in range(2):
            span = pl.ds(h * HALF + dy * CHUNK, CHUNK)
            loads.append(pltpu.make_async_copy(grad_hbm.at[span], tiles.at[span], sems.at[1 + dy * 2 + h]))
    for load in loads:
        load.start()
    pass_on.start()
    stores = []
    for dy in range(3):
        for h in range(2):
            loads[dy * 2 + h].wait()
        for k in range(3):
            tap = k * 9 + dy * 3
            for dx in range(3):
                for h in range(2):
                    for q in range(4):
                        spot = h * HALF + ((dy * 3 + k) * 3 + dx) * 4 + q
                        start = (h * 4 + q) * 16
                        wide[tap + dx, start : start + 16] = tiles[spot].astype(F32)
            group = pl.ds(tap, 3)
            stores.append(pltpu.make_async_copy(wide.at[group], grad_out.at[group], sems.at[7 + dy * 3 + k]))
            stores[-1].start()
    for store in stores:
        store.wait()
    pass_on.wait()


def per_device(nx, nz, ny, video, clip_first, kernel, bias, cotangent):
    _, frames, height, width, chans = video.shape
    half_h, half_w = height // 2, width // 2
    n_tm = nx * nz
    owned = HALF // (nx * ny)
    sa, sb = owned - owned // 2, owned // 2
    any_space = pl.BlockSpec(memory_space=pl.ANY)
    sem = pltpu.SemaphoreType.DMA

    def tiles(*shape):
        return pltpu.VMEM((*shape, 16, chans), BF16)

    def both(n):
        return [sem((n,)), sem((n,))]

    down, grad = pl.pallas_call(
        functools.partial(fused, nx, nz, ny, sa, sb),
        out_shape=(
            jax.ShapeDtypeStruct(cotangent.shape, BF16),
            jax.ShapeDtypeStruct((2 * HALF, 16, chans), BF16),
        ),
        in_specs=[any_space] * 5,
        out_specs=(any_space, any_space),
        scratch_shapes=[
            pltpu.SMEM(clip_first.shape, jnp.int32),
            pltpu.VMEM((1, chans), F32),
            pltpu.VMEM((frames, height, width, chans), BF16),
            pltpu.VMEM((frames, height, width, chans), BF16),
            pltpu.VMEM((3, 3, 3, chans, chans), BF16),
            pltpu.VMEM((frames, half_h, half_w, chans), BF16),
            pltpu.VMEM((4, height + 2, width, 3 * chans), BF16),
            pltpu.VMEM((frames, height * width, chans), F32),
            pltpu.VMEM((frames * half_h, width, chans), F32),
            pltpu.VMEM((frames * half_h, width, chans), F32),
            pltpu.VMEM((frames, half_h, half_w, chans), BF16),
            pltpu.VMEM((frames * chans, height * width), BF16),
            pltpu.VMEM((n_tm, 2, chans), F32),
            tiles(2 * HALF),
            tiles(HALF),
            tiles(HALF),
            tiles(ny, nx * sa),
            tiles(nx, ny * sb),
            tiles(nx * sa),
            tiles(ny * sb),
            tiles(nx, sa),
            tiles(ny, sb),
            tiles(sa),
            tiles(sb),
            tiles(nz, sa),
            tiles(nz, sb),
            tiles(2 * HALF),
            sem((8,)),
            *both(4),
            *both(1),
            *both(3),
            *both(ny),
            *both(nx),
            *both(nx),
            *both(ny),
            *both(nz),
            *both(nz),
            *both(nx),
            *both(ny),
            *both(ny),
            *both(nx),
            *both(ny),
            *both(nx),
        ],
        compiler_params=pltpu.CompilerParams(
            collective_id=0, has_side_effects=True, vmem_limit_bytes=62 * 1024 * 1024
        ),
    )(clip_first, bias.reshape(1, chans), video, kernel, cotangent)
    grad, down = pl.pallas_call(
        widen_result,
        out_shape=(
            jax.ShapeDtypeStruct((27, chans, chans), F32),
            jax.ShapeDtypeStruct(cotangent.shape, BF16),
        ),
        in_specs=[any_space] * 2,
        out_specs=(any_space, any_space),
        scratch_shapes=[
            tiles(2 * HALF),
            pltpu.VMEM((27, chans, chans), F32),
            sem((16,)),
        ],
        compiler_params=pltpu.CompilerParams(vmem_limit_bytes=62 * 1024 * 1024),
    )(grad, down)
    return down, grad.reshape(3, 3, 3, chans, chans)


def solution(mesh):
    n_tm, n_dp = mesh.shape["tm"], mesh.shape["dp"]
    nz = 8 if n_tm == 32 else 2
    in_specs = (
        P("dp", "tm", None, None, None),
        P("dp", "tm"),
        P(),
        P(),
        P("dp", "tm", None, None, None),
    )
    out_specs = (P("dp", "tm", None, None, None), P())
    return jax.shard_map(
        functools.partial(per_device, n_tm // nz, nz, n_dp // 2),
        mesh=mesh,
        in_specs=in_specs,
        out_specs=out_specs,
        check_vma=False,
    )
```

```python
import functools

import jax
import jax.numpy as jnp
from jax import lax
from jax.experimental import pallas as pl
from jax.experimental.pallas import tpu as pltpu
from jax.sharding import PartitionSpec as P

F32 = jnp.float32
BF16 = jnp.bfloat16
HALF = 28 * 4
CHUNK = 9 * 4


def fused(
    nx,
    nz,
    ny,
    sa,
    sb,
    first_hbm,
    bias_hbm,
    video_hbm,
    kern_hbm,
    cot_hbm,
    down_hbm,
    grad_hbm,
    first_ref,
    bias_ref,
    vid,
    halo,
    kern,
    cot,
    xs,
    acc,
    spread,
    pool,
    down,
    dts,
    gath,
    grads,
    r_pair,
    part,
    r1a,
    r1b,
    s1a,
    s1b,
    r2a,
    r2b,
    s2a,
    s2b,
    r3a,
    r3b,
    full,
    local_sem,
    sent,
    near_recv,
    pair_recv,
    stage,
    line_a,
    line_b,
):
    _, frames, height, width, chans = video_hbm.shape
    half_h, half_w = height // 2, width // 2
    pixels = height * width
    n_tm = nx * nz
    n_a = nx * ny * sa

    tm = lax.axis_index("tm")
    dp = lax.axis_index("dp")
    x, z = tm // nz, tm % nz
    y, core = dp // 2, dp % 2

    def at(tm_to, dp_to):
        return {"tm": tm_to, "dp": dp_to}

    def x_peer(q):
        return at(q * nz + z, dp)

    def y_peer(q):
        return at(tm, q * 2 + core)

    def z_peer(q):
        return at(x * nz + q, dp)

    sibling = at(tm, y * 2 + 1 - core)
    right = at((tm + 1) % n_tm, dp)
    left = at((tm + n_tm - 1) % n_tm, dp)

    def remote(src, dst, send, recv, to):
        return pltpu.make_async_remote_copy(
            src_ref=src,
            dst_ref=dst,
            send_sem=send,
            recv_sem=recv,
            device_id=to,
            device_id_type=pl.DeviceIdType.MESH,
        )

    loads = [
        pltpu.make_async_copy(video_hbm.at[0], vid, local_sem.at[0]),
        pltpu.make_async_copy(first_hbm, first_ref, local_sem.at[1]),
        pltpu.make_async_copy(cot_hbm.at[0, 1], cot.at[0], local_sem.at[2]),
        pltpu.make_async_copy(bias_hbm, bias_ref, local_sem.at[3]),
        pltpu.make_async_copy(kern_hbm, kern, local_sem.at[4]),
    ]
    for load in loads:
        load.start()

    barrier = pltpu.get_barrier_semaphore()
    peers = [at((tm + d) % n_tm, dp) for d in range(1, n_tm)]
    peers += [y_peer((y + d) % ny) for d in range(1, ny)]
    peers += [sibling]
    for peer in peers:
        pl.semaphore_signal(barrier, inc=1, device_id=peer, device_id_type=pl.DeviceIdType.MESH)

    loads[0].wait()
    loads[1].wait()
    rows = []
    for f in range(frames):
        value = vid[f].astype(F32)
        rows.append(jnp.sum(jnp.sum(value, axis=0), axis=0, keepdims=True))
        rows.append(jnp.sum(jnp.sum(value * value, axis=0), axis=0, keepdims=True))
    rows.append(jnp.zeros((4, chans), F32))
    stat = jnp.concatenate(rows, axis=0)
    lane8 = lax.broadcasted_iota(jnp.int32, (8, chans), 1)
    stat = stat + jnp.where(lane8 % 2 == 0, pltpu.roll(stat, chans - 1, 1), pltpu.roll(stat, 1, 1))
    stat = stat + jnp.where(lane8 % 4 < 2, pltpu.roll(stat, chans - 2, 1), pltpu.roll(stat, 2, 1))
    lane = lax.broadcasted_iota(jnp.int32, (1, chans), 1)
    low = jnp.where(lane % 2 == 0, stat[0:1], stat[1:2])
    high = jnp.where(lane % 2 == 0, stat[2:3], stat[3:4])
    first0 = jnp.full((1, chans), first_ref[0, 0], jnp.int32)
    first1 = jnp.full((1, chans), first_ref[0, 1], jnp.int32)
    gath[tm, 0:1] = jnp.where(lane % 4 < 2, low, high)
    gath[tm, 1:2] = first0.astype(F32)

    pl.semaphore_wait(barrier, len(peers))

    near = [
        remote(video_hbm.at[0, 1], halo.at[0], sent.at[0], near_recv.at[0], right),
        remote(video_hbm.at[0, 0], halo.at[1], sent.at[0], near_recv.at[1], left),
        remote(cot_hbm.at[0, 0], cot.at[1], sent.at[0], near_recv.at[2], left),
    ]
    for copy in near[:2]:
        copy.start()
    for d in range(1, n_tm):
        remote(gath.at[tm], gath.at[tm], sent.at[4], stage.at[0], at((tm + d) % n_tm, dp)).start()
    near[2].start()

    rim = jnp.zeros((width, 3 * chans), BF16)
    for s in range(4):
        xs[s, 0] = rim
        xs[s, height + 1] = rim
    for h in range(2):
        for j in range(27 * 4, HALF):
            grads[h * HALF + j] = jnp.zeros((16, chans), BF16)

    def widen(f):
        for i in range(half_h):
            quarter = cot[f, i].astype(F32) * 0.25
            spread[f * half_h + i, pl.ds(0, half_w, stride=2), :] = quarter
            spread[f * half_h + i, pl.ds(1, half_w, stride=2), :] = quarter

    loads[2].wait()
    widen(0)
    loads[3].wait()
    loads[4].wait()

    others = gath.at[pl.ds(0, n_tm - 1)]
    remote(others, others, sent.at[4], stage.at[0], right).wait_recv()

    t0 = tm * frames
    t2 = (t0 + 2) % (n_tm * frames)
    first2 = gath[(tm + 1) % n_tm, 1:2].astype(jnp.int32)
    gathered = gath[...]
    frame = lax.broadcasted_iota(jnp.int32, gathered.shape, 0) * frames
    frame = frame + lax.broadcasted_iota(jnp.int32, gathered.shape, 2) % 4 // 2

    def moments(first, last):
        chosen = jnp.where((frame >= first[None]) & (frame <= last), gathered, 0.0)
        total = jnp.sum(chosen, axis=0)[0:1]
        count = jnp.maximum((last + 1 - first) * (pixels * 4), 1).astype(F32)
        total = total + jnp.where(lane % 4 < 2, pltpu.roll(total, chans - 2, 1), pltpu.roll(total, 2, 1))
        mean = jnp.where(lane % 2 == 0, total, pltpu.roll(total, 1, 1)) / count
        var = jnp.where(lane % 2 == 1, total, pltpu.roll(total, chans - 1, 1)) / count - mean * mean
        return mean, lax.rsqrt(var + 1e-05)

    col = lax.broadcasted_iota(jnp.int32, (width, chans), 0)

    def place(source, f, slot, mean, scale, keep):
        for r in range(height):
            value = (source[f, r].astype(F32) - mean) * scale
            if keep is not None:
                value = jnp.where(keep, value, 0.0)
            before = jnp.where(col == 0, 0.0, pltpu.roll(value, 1, 0))
            after = jnp.where(col == width - 1, 0.0, pltpu.roll(value, width - 1, 0))
            xs[slot, r + 1, :, 0:chans] = before.astype(BF16)
            xs[slot, r + 1, :, chans : 2 * chans] = value.astype(BF16)
            xs[slot, r + 1, :, 2 * chans : 3 * chans] = after.astype(BF16)

    def flag(condition):
        return jnp.where(condition, 1.0, 0.0)

    t0_t1 = flag(first1 <= t0)
    t0_t2 = flag(first2 <= t2 - 2)
    t1_t2 = flag(first2 <= t2 - 1)
    block = min(8, height)

    def patches(slot, r):
        parts = [xs[slot, r + dy : r + dy + block].reshape(block * width, 3 * chans) for dy in range(3)]
        return jnp.concatenate(parts, axis=1)

    def taps(k):
        return kern[k].reshape(9 * chans, chans)

    def dot(a, b):
        return jnp.dot(a, b, preferred_element_type=F32)

    place(vid, 0, 1, *moments(first0, t0), None)
    place(vid, 1, 2, *moments(first1, t0 + 1), None)
    for r in range(0, height, block):
        px = pl.ds(r * width, block * width)
        one = dot(patches(1, r), jnp.concatenate([taps(1), taps(0)], axis=1))
        two = dot(patches(2, r), jnp.concatenate([taps(2), taps(1)], axis=1))
        acc[0, px] = one[:, :chans] * t0_t1 + two[:, :chans]
        acc[1, px] = one[:, chans:] * t0_t2 + two[:, chans:] * t1_t2

    bias = bias_ref[...]

    def finish_conv(f, slot, k):
        for r in range(0, height, block):
            last = dot(patches(slot, r), taps(k))
            for m in range(block // 2):
                i = r // 2 + m
                px = slice(i * 2 * width, (i + 1) * 2 * width)
                value = acc[f, px] + last[m * 2 * width : (m + 1) * 2 * width] + bias
                logistic = 1.0 / (1.0 + jnp.exp(-value))
                active = value * logistic
                pool[f * half_h + i] = active[:width] + active[width:]
                slope = logistic * (1.0 + value * (1.0 - logistic))
                over = spread[f * half_h + i]
                dconv = jnp.concatenate([over, over], axis=0) * slope
                dts[f * chans : (f + 1) * chans, px] = dconv.T.astype(BF16)
        for i in range(half_h):
            even = pool[f * half_h + i, pl.ds(0, half_w, stride=2), :]
            odd = pool[f * half_h + i, pl.ds(1, half_w, stride=2), :]
            down[f, i] = ((even + odd) * 0.25).astype(BF16)

    near[0].wait_recv()
    place(halo, 0, 0, *moments(first1, t0 - 1), first1 <= t0 - 1)
    finish_conv(0, 0, 0)
    near[2].wait_recv()
    widen(1)
    near[1].wait_recv()
    place(halo, 1, 3, *moments(first2, t2), None)
    finish_conv(1, 3, 2)
    out_far = remote(down.at[1], down_hbm.at[0, 0], sent.at[0], near_recv.at[3], right)
    out_near = pltpu.make_async_copy(down.at[0], down_hbm.at[0, 1], local_sem.at[5])
    out_far.start()
    out_near.start()


    def pair(c):
        tiles = pl.ds(c * CHUNK, CHUNK if c < 2 else HALF - 2 * CHUNK)
        src = grads.at[pl.ds((1 - core) * HALF + tiles.start, tiles.size)]
        return remote(src, r_pair.at[tiles], sent.at[1], pair_recv.at[c], sibling)

    def join_pair(c):
        pair(c).wait_recv()
        tiles = pl.ds(c * CHUNK, CHUNK if c < 2 else HALF - 2 * CHUNK)
        own = grads[pl.ds(core * HALF + tiles.start, tiles.size)].astype(F32)
        part[tiles] = (own + r_pair[tiles].astype(F32)).astype(BF16)

    def first_a(q):
        src = part.at[pl.ds(q * nx * sa, nx * sa)]
        return remote(src, r1a.at[y], sent.at[1], stage.at[1], y_peer(q))

    def first_b(q):
        src = part.at[pl.ds(n_a + q * ny * sb, ny * sb)]
        return remote(src, r1b.at[x], sent.at[1], stage.at[2], x_peer(q))

    def go(make, me, owners):
        for q in owners:

            @pl.when(q != me)
            def _():
                make(q).start()

    def a_ready(done):
        return [q for q in range(ny) if (q + 1) * nx * sa <= done]

    started = []
    for dy in range(3):
        shifted = [xs[s, dy : dy + height].reshape(pixels, 3 * chans) for s in range(4)]
        both = dts[...]
        r0 = dot(both[:chans], shifted[0])
        r1 = dot(both, shifted[1])
        r2 = dot(both, shifted[2])
        r3 = dot(both[chans:], shifted[3])
        m01, m02, m12 = t0_t1[:, 0:1], t0_t2[:, 0:1], t1_t2[:, 0:1]
        sums = [r0 + r1[chans:] * m02, r1[:chans] * m01 + r2[chans:] * m12, r2[:chans] + r3]
        for k in range(3):
            for dx in range(3):
                tile = sums[k][:, dx * chans : (dx + 1) * chans].T.astype(BF16)
                spot = ((dy * 3 + k) * 3 + dx) * 4
                for h in range(2):
                    for q in range(4):
                        start = (h * 4 + q) * 16
                        grads[h * HALF + spot + q] = tile[start : start + 16]
        pair(dy).start()
        if dy > 0:
            join_pair(dy - 1)
            ready = [q for q in a_ready(dy * CHUNK) if q not in started]
            go(first_a, y, ready)
            started += ready
    join_pair(2)
    go(first_a, y, [q for q in range(ny) if q not in started])
    go(first_b, x, range(nx))

    def exchange(n, me, src_of, dst, place, peer):
        for d in range(1, n):
            q = (me + d) % n
            remote(src_of(q), dst.at[me], sent.at[2], stage.at[place], peer(q)).start()

    def arrived(n, dst, place):
        rows = dst.at[pl.ds(0, n - 1)]
        remote(rows, rows, sent.at[2], stage.at[place], sibling).wait_recv()

    def summed(n, me, own, dst):
        total = own.astype(F32)
        for d in range(1, n):
            total = total + dst[(me + n - d) % n].astype(F32)
        return total.astype(BF16)

    arrived(ny, r1a, 1)
    s1a[...] = summed(ny, y, part[pl.ds(y * nx * sa, nx * sa)], r1a)
    exchange(nx, x, lambda q: s1a.at[pl.ds(q * sa, sa)], r2a, 3, x_peer)
    arrived(nx, r1b, 2)
    s1b[...] = summed(nx, x, part[pl.ds(n_a + x * ny * sb, ny * sb)], r1b)
    exchange(ny, y, lambda q: s1b.at[pl.ds(q * sb, sb)], r2b, 4, y_peer)

    arrived(nx, r2a, 3)
    s2a[...] = summed(nx, x, s1a[pl.ds(x * sa, sa)], r2a)
    exchange(nz, z, lambda q: s2a, r3a, 5, z_peer)
    arrived(ny, r2b, 4)
    s2b[...] = summed(ny, y, s1b[pl.ds(y * sb, sb)], r2b)
    exchange(nz, z, lambda q: s2b, r3b, 6, z_peer)

    base = core * HALF

    def a_line(q, start=base):
        return full.at[pl.ds(start + q * nx * sa, nx * sa)]

    def b_line(q, start=base):
        return full.at[pl.ds(start + n_a + q * ny * sb, ny * sb)]

    def spread_out(n, me, piece, group, recv, peer):
        for d in range(1, n):
            remote(piece, piece, sent.at[group], recv, peer((me + d) % n)).start()

    def some(tiles):
        return full.at[pl.ds(0, tiles)]

    arrived(nz, r3a, 5)
    a_piece = full.at[pl.ds(base + (y * nx + x) * sa, sa)]
    a_piece[...] = summed(nz, z, s2a[...], r3a)
    spread_out(nx, x, a_piece, 2, stage.at[7], x_peer)
    arrived(nz, r3b, 6)
    b_piece = full.at[pl.ds(base + n_a + (x * ny + y) * sb, sb)]
    b_piece[...] = summed(nz, z, s2b[...], r3b)
    spread_out(ny, y, b_piece, 2, stage.at[8], y_peer)

    def give_a(q):
        remote(a_line(q), a_line(q), sent.at[3], stage.at[9], sibling).start()

    def give_b(q):
        remote(b_line(q), b_line(q), sent.at[3], stage.at[10], sibling).start()

    remote(some((nx - 1) * sa), some((nx - 1) * sa), sent.at[2], stage.at[7], sibling).wait_recv()
    spread_out(ny, y, a_line(y), 3, line_a.at[y], y_peer)
    give_a(y)
    remote(some((ny - 1) * sb), some((ny - 1) * sb), sent.at[2], stage.at[8], sibling).wait_recv()
    spread_out(nx, x, b_line(x), 3, line_b.at[x], x_peer)
    give_b(x)
    for d in range(1, ny):
        q = (y + ny - d) % ny
        remote(a_line(q), a_line(q), sent.at[3], line_a.at[q], sibling).wait_recv()
        give_a(q)
    for d in range(1, nx):
        q = (x + nx - d) % nx
        remote(b_line(q), b_line(q), sent.at[3], line_b.at[q], sibling).wait_recv()
        give_b(q)

    def write(start, size, place):
        tiles = pl.ds(start, size)
        copy = pltpu.make_async_copy(full.at[tiles], grad_hbm.at[tiles], local_sem.at[place])
        copy.start()
        return copy

    writes = [write(base, HALF, 6)]
    base = (1 - core) * HALF
    remote(some(n_a), some(n_a), sent.at[3], stage.at[9], sibling).wait_recv()
    writes.append(write(base, n_a, 7))
    remote(some(HALF - n_a), some(HALF - n_a), sent.at[3], stage.at[10], sibling).wait_recv()
    writes.append(write(base + n_a, HALF - n_a, 8))

    remote(others, others, sent.at[4], stage.at[0], right).wait_send()
    lines = (ny - 1) * nx * sa + (nx - 1) * ny * sb
    pieces = 2 * ((nx - 1) * sa + (ny - 1) * sb) + (nz - 1) * (sa + sb)
    frames_out = frames * (pixels + half_h * half_w) // 16
    for group, tiles in ((0, frames_out), (1, HALF + lines), (2, pieces), (3, HALF + lines)):
        remote(some(tiles), some(tiles), sent.at[group], stage.at[0], sibling).wait_send()

    out_far.wait_recv()
    out_near.wait()
    for copy in writes:
        copy.wait()


def widen_result(grad_hbm, down_hbm, grad_out, down_out, tiles, wide, down, sems):
    take = pltpu.make_async_copy(down_hbm, down, sems.at[0])
    pass_on = pltpu.make_async_copy(down, down_out, sems.at[0])
    loads = []
    for dy in range(3):
        for h in range(2):
            span = pl.ds(h * HALF + dy * CHUNK, CHUNK)
            loads.append(pltpu.make_async_copy(grad_hbm.at[span], tiles.at[span], sems.at[1 + dy * 2 + h]))
    for load in loads:
        load.start()
    take.start()
    stores = []
    for dy in range(3):
        for h in range(2):
            loads[dy * 2 + h].wait()
        for k in range(3):
            tap = k * 9 + dy * 3
            for dx in range(3):
                for h in range(2):
                    for q in range(4):
                        spot = h * HALF + ((dy * 3 + k) * 3 + dx) * 4 + q
                        start = (h * 4 + q) * 16
                        wide[tap + dx, start : start + 16] = tiles[spot].astype(F32)
            group = pl.ds(tap, 3)
            stores.append(pltpu.make_async_copy(wide.at[group], grad_out.at[group], sems.at[7 + dy * 3 + k]))
            stores[-1].start()
    take.wait()
    pass_on.start()
    for store in stores:
        store.wait()
    pass_on.wait()


def per_device(nx, nz, ny, video, clip_first, kernel, bias, cotangent):
    _, frames, height, width, chans = video.shape
    half_h, half_w = height // 2, width // 2
    n_tm = nx * nz
    owned = HALF // (nx * ny)
    sa, sb = owned - owned // 2, owned // 2
    any_space = pl.BlockSpec(memory_space=pl.ANY)
    sem = pltpu.SemaphoreType.DMA

    def tiles(*shape):
        return pltpu.VMEM((*shape, 16, chans), BF16)

    down, grad = pl.pallas_call(
        functools.partial(fused, nx, nz, ny, sa, sb),
        out_shape=(
            jax.ShapeDtypeStruct(cotangent.shape, BF16),
            jax.ShapeDtypeStruct((2 * HALF, 16, chans), BF16),
        ),
        in_specs=[any_space] * 5,
        out_specs=(any_space, any_space),
        scratch_shapes=[
            pltpu.SMEM(clip_first.shape, jnp.int32),
            pltpu.VMEM((1, chans), F32),
            pltpu.VMEM((frames, height, width, chans), BF16),
            pltpu.VMEM((frames, height, width, chans), BF16),
            pltpu.VMEM((3, 3, 3, chans, chans), BF16),
            pltpu.VMEM((frames, half_h, half_w, chans), BF16),
            pltpu.VMEM((4, height + 2, width, 3 * chans), BF16),
            pltpu.VMEM((frames, height * width, chans), F32),
            pltpu.VMEM((frames * half_h, width, chans), F32),
            pltpu.VMEM((frames * half_h, width, chans), F32),
            pltpu.VMEM((frames, half_h, half_w, chans), BF16),
            pltpu.VMEM((frames * chans, height * width), BF16),
            pltpu.VMEM((n_tm, 2, chans), F32),
            tiles(2 * HALF),
            tiles(HALF),
            tiles(HALF),
            tiles(ny, nx * sa),
            tiles(nx, ny * sb),
            tiles(nx * sa),
            tiles(ny * sb),
            tiles(nx, sa),
            tiles(ny, sb),
            tiles(sa),
            tiles(sb),
            tiles(nz, sa),
            tiles(nz, sb),
            tiles(2 * HALF),
            sem((9,)),
            sem((5,)),
            sem((4,)),
            sem((3,)),
            sem((11,)),
            sem((ny,)),
            sem((nx,)),
        ],
        compiler_params=pltpu.CompilerParams(
            collective_id=0, has_side_effects=True, vmem_limit_bytes=62 * 1024 * 1024
        ),
    )(clip_first, bias.reshape(1, chans), video, kernel, cotangent)
    grad, down = pl.pallas_call(
        widen_result,
        out_shape=(
            jax.ShapeDtypeStruct((27, chans, chans), F32),
            jax.ShapeDtypeStruct(cotangent.shape, BF16),
        ),
        in_specs=[any_space] * 2,
        out_specs=(any_space, any_space),
        scratch_shapes=[
            tiles(2 * HALF),
            pltpu.VMEM((27, chans, chans), F32),
            pltpu.VMEM(cotangent.shape, BF16),
            sem((16,)),
        ],
        compiler_params=pltpu.CompilerParams(vmem_limit_bytes=62 * 1024 * 1024),
    )(grad, down)
    return down, grad.reshape(3, 3, 3, chans, chans)


def solution(mesh):
    n_tm, n_dp = mesh.shape["tm"], mesh.shape["dp"]
    nz = 8 if n_tm == 32 else 2
    in_specs = (
        P("dp", "tm", None, None, None),
        P("dp", "tm"),
        P(),
        P(),
        P("dp", "tm", None, None, None),
    )
    out_specs = (P("dp", "tm", None, None, None), P())
    return jax.shard_map(
        functools.partial(per_device, n_tm // nz, nz, n_dp // 2),
        mesh=mesh,
        in_specs=in_specs,
        out_specs=out_specs,
        check_vma=False,
    )
```

```python
import functools

import jax
import jax.numpy as jnp
from jax import lax
from jax.experimental import pallas as pl
from jax.experimental.pallas import tpu as pltpu
from jax.sharding import PartitionSpec as P

F32 = jnp.float32
BF16 = jnp.bfloat16
HALF = 28 * 4
CHUNK = 9 * 4


def fused(
    nx,
    nz,
    ny,
    sa,
    sb,
    first_hbm,
    bias_hbm,
    video_hbm,
    kern_hbm,
    cot_hbm,
    down_hbm,
    grad_hbm,
    first_ref,
    bias_ref,
    vid,
    halo,
    kern,
    cot,
    xs,
    acc,
    spread,
    pool,
    down,
    dts,
    gath,
    grads,
    r_pair,
    part,
    r1a,
    r1b,
    s1a,
    s1b,
    r2a,
    r2b,
    s2a,
    s2b,
    r3a,
    r3b,
    full,
    local_sem,
    sent,
    near_recv,
    pair_recv,
    stage,
    line_a,
    line_b,
):
    _, frames, height, width, chans = video_hbm.shape
    half_h, half_w = height // 2, width // 2
    pixels = height * width
    n_tm = nx * nz
    n_a = nx * ny * sa

    tm = lax.axis_index("tm")
    dp = lax.axis_index("dp")
    x, z = tm // nz, tm % nz
    y, core = dp // 2, dp % 2

    def at(tm_to, dp_to):
        return {"tm": tm_to, "dp": dp_to}

    def x_peer(q):
        return at(q * nz + z, dp)

    def y_peer(q):
        return at(tm, q * 2 + core)

    def z_peer(q):
        return at(x * nz + q, dp)

    sibling = at(tm, y * 2 + 1 - core)
    right = at((tm + 1) % n_tm, dp)
    left = at((tm + n_tm - 1) % n_tm, dp)

    def remote(src, dst, send, recv, to):
        return pltpu.make_async_remote_copy(
            src_ref=src,
            dst_ref=dst,
            send_sem=send,
            recv_sem=recv,
            device_id=to,
            device_id_type=pl.DeviceIdType.MESH,
        )

    loads = [
        pltpu.make_async_copy(video_hbm.at[0], vid, local_sem.at[0]),
        pltpu.make_async_copy(first_hbm, first_ref, local_sem.at[1]),
        pltpu.make_async_copy(cot_hbm.at[0, 1], cot.at[0], local_sem.at[2]),
        pltpu.make_async_copy(bias_hbm, bias_ref, local_sem.at[3]),
        pltpu.make_async_copy(kern_hbm, kern, local_sem.at[4]),
    ]
    for load in loads:
        load.start()

    barrier = pltpu.get_barrier_semaphore()
    peers = [at((tm + d) % n_tm, dp) for d in range(1, n_tm)]
    peers += [y_peer((y + d) % ny) for d in range(1, ny)]
    peers += [sibling]
    for peer in peers:
        pl.semaphore_signal(barrier, inc=1, device_id=peer, device_id_type=pl.DeviceIdType.MESH)

    loads[0].wait()
    loads[1].wait()
    rows = []
    for f in range(frames):
        value = vid[f].astype(F32)
        rows.append(jnp.sum(jnp.sum(value, axis=0), axis=0, keepdims=True))
        rows.append(jnp.sum(jnp.sum(value * value, axis=0), axis=0, keepdims=True))
    rows.append(jnp.zeros((4, chans), F32))
    stat = jnp.concatenate(rows, axis=0)
    lane8 = lax.broadcasted_iota(jnp.int32, (8, chans), 1)
    stat = stat + jnp.where(lane8 % 2 == 0, pltpu.roll(stat, chans - 1, 1), pltpu.roll(stat, 1, 1))
    stat = stat + jnp.where(lane8 % 4 < 2, pltpu.roll(stat, chans - 2, 1), pltpu.roll(stat, 2, 1))
    lane = lax.broadcasted_iota(jnp.int32, (1, chans), 1)
    low = jnp.where(lane % 2 == 0, stat[0:1], stat[1:2])
    high = jnp.where(lane % 2 == 0, stat[2:3], stat[3:4])
    first0 = jnp.full((1, chans), first_ref[0, 0], jnp.int32)
    first1 = jnp.full((1, chans), first_ref[0, 1], jnp.int32)
    gath[tm, 0:1] = jnp.where(lane % 4 < 2, low, high)
    gath[tm, 1:2] = first0.astype(F32)

    pl.semaphore_wait(barrier, len(peers))

    near = [
        remote(video_hbm.at[0, 1], halo.at[0], sent.at[0], near_recv.at[0], right),
        remote(video_hbm.at[0, 0], halo.at[1], sent.at[0], near_recv.at[1], left),
        remote(cot_hbm.at[0, 0], cot.at[1], sent.at[0], near_recv.at[2], left),
    ]
    for d in range(1, n_tm):
        remote(gath.at[tm], gath.at[tm], sent.at[4], stage.at[0], at((tm + d) % n_tm, dp)).start()
    for copy in near:
        copy.start()

    rim = jnp.zeros((width, 3 * chans), BF16)
    for s in range(4):
        xs[s, 0] = rim
        xs[s, height + 1] = rim
    for h in range(2):
        for j in range(27 * 4, HALF):
            grads[h * HALF + j] = jnp.zeros((16, chans), BF16)

    def widen(f):
        for i in range(half_h):
            quarter = cot[f, i].astype(F32) * 0.25
            spread[f * half_h + i, pl.ds(0, half_w, stride=2), :] = quarter
            spread[f * half_h + i, pl.ds(1, half_w, stride=2), :] = quarter

    loads[2].wait()
    widen(0)
    loads[3].wait()
    loads[4].wait()

    others = gath.at[pl.ds(0, n_tm - 1)]
    remote(others, others, sent.at[4], stage.at[0], right).wait_recv()

    t0 = tm * frames
    t2 = (t0 + 2) % (n_tm * frames)
    first2 = gath[(tm + 1) % n_tm, 1:2].astype(jnp.int32)
    gathered = gath[...]
    frame = lax.broadcasted_iota(jnp.int32, gathered.shape, 0) * frames
    frame = frame + lax.broadcasted_iota(jnp.int32, gathered.shape, 2) % 4 // 2

    def moments(first, last):
        chosen = jnp.where((frame >= first[None]) & (frame <= last), gathered, 0.0)
        total = jnp.sum(chosen, axis=0)[0:1]
        count = jnp.maximum((last + 1 - first) * (pixels * 4), 1).astype(F32)
        total = total + jnp.where(lane % 4 < 2, pltpu.roll(total, chans - 2, 1), pltpu.roll(total, 2, 1))
        mean = jnp.where(lane % 2 == 0, total, pltpu.roll(total, 1, 1)) / count
        var = jnp.where(lane % 2 == 1, total, pltpu.roll(total, chans - 1, 1)) / count - mean * mean
        return mean, lax.rsqrt(var + 1e-05)

    col = lax.broadcasted_iota(jnp.int32, (width, chans), 0)

    def place(source, f, slot, mean, scale, keep):
        for r in range(height):
            value = (source[f, r].astype(F32) - mean) * scale
            if keep is not None:
                value = jnp.where(keep, value, 0.0)
            before = jnp.where(col == 0, 0.0, pltpu.roll(value, 1, 0))
            after = jnp.where(col == width - 1, 0.0, pltpu.roll(value, width - 1, 0))
            xs[slot, r + 1, :, 0:chans] = before.astype(BF16)
            xs[slot, r + 1, :, chans : 2 * chans] = value.astype(BF16)
            xs[slot, r + 1, :, 2 * chans : 3 * chans] = after.astype(BF16)

    def flag(condition):
        return jnp.where(condition, 1.0, 0.0)

    t0_t1 = flag(first1 <= t0)
    t0_t2 = flag(first2 <= t2 - 2)
    t1_t2 = flag(first2 <= t2 - 1)
    block = min(8, height)

    def patches(slot, r):
        parts = [xs[slot, r + dy : r + dy + block].reshape(block * width, 3 * chans) for dy in range(3)]
        return jnp.concatenate(parts, axis=1)

    def taps(k):
        return kern[k].reshape(9 * chans, chans)

    def dot(a, b):
        return jnp.dot(a, b, preferred_element_type=F32)

    place(vid, 0, 1, *moments(first0, t0), None)
    place(vid, 1, 2, *moments(first1, t0 + 1), None)
    for r in range(0, height, block):
        px = pl.ds(r * width, block * width)
        one = dot(patches(1, r), jnp.concatenate([taps(1), taps(0)], axis=1))
        two = dot(patches(2, r), jnp.concatenate([taps(2), taps(1)], axis=1))
        acc[0, px] = one[:, :chans] * t0_t1 + two[:, :chans]
        acc[1, px] = one[:, chans:] * t0_t2 + two[:, chans:] * t1_t2

    bias = bias_ref[...]

    def finish_conv(f, slot, k):
        for r in range(0, height, block):
            last = dot(patches(slot, r), taps(k))
            for m in range(block // 2):
                i = r // 2 + m
                px = slice(i * 2 * width, (i + 1) * 2 * width)
                value = acc[f, px] + last[m * 2 * width : (m + 1) * 2 * width] + bias
                logistic = 1.0 / (1.0 + jnp.exp(-value))
                active = value * logistic
                pool[f * half_h + i] = active[:width] + active[width:]
                slope = logistic * (1.0 + value * (1.0 - logistic))
                over = spread[f * half_h + i]
                dconv = jnp.concatenate([over, over], axis=0) * slope
                dts[f * chans : (f + 1) * chans, px] = dconv.T.astype(BF16)
        for i in range(half_h):
            even = pool[f * half_h + i, pl.ds(0, half_w, stride=2), :]
            odd = pool[f * half_h + i, pl.ds(1, half_w, stride=2), :]
            down[f, i] = ((even + odd) * 0.25).astype(BF16)

    near[0].wait_recv()
    place(halo, 0, 0, *moments(first1, t0 - 1), first1 <= t0 - 1)
    finish_conv(0, 0, 0)
    near[2].wait_recv()
    widen(1)
    near[1].wait_recv()
    place(halo, 1, 3, *moments(first2, t2), None)
    finish_conv(1, 3, 2)
    out_far = remote(down.at[1], down_hbm.at[0, 0], sent.at[0], near_recv.at[3], right)
    out_near = pltpu.make_async_copy(down.at[0], down_hbm.at[0, 1], local_sem.at[5])
    out_far.start()
    out_near.start()


    def pair(c):
        tiles = pl.ds(c * CHUNK, CHUNK if c < 2 else HALF - 2 * CHUNK)
        src = grads.at[pl.ds((1 - core) * HALF + tiles.start, tiles.size)]
        return remote(src, r_pair.at[tiles], sent.at[1], pair_recv.at[c], sibling)

    def join_pair(c):
        pair(c).wait_recv()
        tiles = pl.ds(c * CHUNK, CHUNK if c < 2 else HALF - 2 * CHUNK)
        own = grads[pl.ds(core * HALF + tiles.start, tiles.size)].astype(F32)
        part[tiles] = (own + r_pair[tiles].astype(F32)).astype(BF16)

    def first_a(q):
        src = part.at[pl.ds(q * nx * sa, nx * sa)]
        return remote(src, r1a.at[y], sent.at[1], stage.at[1], y_peer(q))

    def first_b(q):
        src = part.at[pl.ds(n_a + q * ny * sb, ny * sb)]
        return remote(src, r1b.at[x], sent.at[1], stage.at[2], x_peer(q))

    def go(make, me, owners):
        for q in owners:

            @pl.when(q != me)
            def _():
                make(q).start()

    def a_ready(done):
        return [q for q in range(ny) if (q + 1) * nx * sa <= done]

    started = []
    for dy in range(3):
        shifted = [xs[s, dy : dy + height].reshape(pixels, 3 * chans) for s in range(4)]
        both = dts[...]
        r0 = dot(both[:chans], shifted[0])
        r1 = dot(both, shifted[1])
        r2 = dot(both, shifted[2])
        r3 = dot(both[chans:], shifted[3])
        m01, m02, m12 = t0_t1[:, 0:1], t0_t2[:, 0:1], t1_t2[:, 0:1]
        sums = [r0 + r1[chans:] * m02, r1[:chans] * m01 + r2[chans:] * m12, r2[:chans] + r3]
        for k in range(3):
            for dx in range(3):
                tile = sums[k][:, dx * chans : (dx + 1) * chans].T.astype(BF16)
                spot = ((dy * 3 + k) * 3 + dx) * 4
                for h in range(2):
                    for q in range(4):
                        start = (h * 4 + q) * 16
                        grads[h * HALF + spot + q] = tile[start : start + 16]
        pair(dy).start()
        if dy > 0:
            join_pair(dy - 1)
            ready = [q for q in a_ready(dy * CHUNK) if q not in started]
            go(first_a, y, ready)
            started += ready
    join_pair(2)
    go(first_a, y, [q for q in range(ny) if q not in started])
    go(first_b, x, range(nx))

    def exchange(n, me, src_of, dst, place, peer):
        for d in range(1, n):
            q = (me + d) % n
            remote(src_of(q), dst.at[me], sent.at[2], stage.at[place], peer(q)).start()

    def arrived(n, dst, place):
        rows = dst.at[pl.ds(0, n - 1)]
        remote(rows, rows, sent.at[2], stage.at[place], sibling).wait_recv()

    def summed(n, me, own, dst):
        total = own.astype(F32)
        for d in range(1, n):
            total = total + dst[(me + n - d) % n].astype(F32)
        return total.astype(BF16)

    arrived(ny, r1a, 1)
    s1a[...] = summed(ny, y, part[pl.ds(y * nx * sa, nx * sa)], r1a)
    exchange(nx, x, lambda q: s1a.at[pl.ds(q * sa, sa)], r2a, 3, x_peer)
    arrived(nx, r1b, 2)
    s1b[...] = summed(nx, x, part[pl.ds(n_a + x * ny * sb, ny * sb)], r1b)
    exchange(ny, y, lambda q: s1b.at[pl.ds(q * sb, sb)], r2b, 4, y_peer)

    arrived(nx, r2a, 3)
    s2a[...] = summed(nx, x, s1a[pl.ds(x * sa, sa)], r2a)
    exchange(nz, z, lambda q: s2a, r3a, 5, z_peer)
    arrived(ny, r2b, 4)
    s2b[...] = summed(ny, y, s1b[pl.ds(y * sb, sb)], r2b)
    exchange(nz, z, lambda q: s2b, r3b, 6, z_peer)

    base = core * HALF

    def a_line(q, start=base):
        return full.at[pl.ds(start + q * nx * sa, nx * sa)]

    def b_line(q, start=base):
        return full.at[pl.ds(start + n_a + q * ny * sb, ny * sb)]

    def spread_out(n, me, piece, group, recv, peer):
        for d in range(1, n):
            remote(piece, piece, sent.at[group], recv, peer((me + d) % n)).start()

    def some(tiles):
        return full.at[pl.ds(0, tiles)]

    arrived(nz, r3a, 5)
    a_piece = full.at[pl.ds(base + (y * nx + x) * sa, sa)]
    a_piece[...] = summed(nz, z, s2a[...], r3a)
    spread_out(nx, x, a_piece, 2, stage.at[7], x_peer)
    arrived(nz, r3b, 6)
    b_piece = full.at[pl.ds(base + n_a + (x * ny + y) * sb, sb)]
    b_piece[...] = summed(nz, z, s2b[...], r3b)
    spread_out(ny, y, b_piece, 2, stage.at[8], y_peer)

    def give_a(q):
        remote(a_line(q), a_line(q), sent.at[3], stage.at[9], sibling).start()

    def give_b(q):
        remote(b_line(q), b_line(q), sent.at[3], stage.at[10], sibling).start()

    remote(some((nx - 1) * sa), some((nx - 1) * sa), sent.at[2], stage.at[7], sibling).wait_recv()
    spread_out(ny, y, a_line(y), 3, line_a.at[y], y_peer)
    give_a(y)
    remote(some((ny - 1) * sb), some((ny - 1) * sb), sent.at[2], stage.at[8], sibling).wait_recv()
    spread_out(nx, x, b_line(x), 3, line_b.at[x], x_peer)
    give_b(x)
    for d in range(1, ny):
        q = (y + ny - d) % ny
        remote(a_line(q), a_line(q), sent.at[3], line_a.at[q], sibling).wait_recv()
        give_a(q)
    for d in range(1, nx):
        q = (x + nx - d) % nx
        remote(b_line(q), b_line(q), sent.at[3], line_b.at[q], sibling).wait_recv()
        give_b(q)

    def write(start, size, place):
        tiles = pl.ds(start, size)
        copy = pltpu.make_async_copy(full.at[tiles], grad_hbm.at[tiles], local_sem.at[place])
        copy.start()
        return copy

    writes = [write(base, HALF, 6)]
    base = (1 - core) * HALF
    remote(some(n_a), some(n_a), sent.at[3], stage.at[9], sibling).wait_recv()
    writes.append(write(base, n_a, 7))
    remote(some(HALF - n_a), some(HALF - n_a), sent.at[3], stage.at[10], sibling).wait_recv()
    writes.append(write(base + n_a, HALF - n_a, 8))

    remote(others, others, sent.at[4], stage.at[0], right).wait_send()
    lines = (ny - 1) * nx * sa + (nx - 1) * ny * sb
    pieces = 2 * ((nx - 1) * sa + (ny - 1) * sb) + (nz - 1) * (sa + sb)
    frames_out = frames * (pixels + half_h * half_w) // 16
    for group, tiles in ((0, frames_out), (1, HALF + lines), (2, pieces), (3, HALF + lines)):
        remote(some(tiles), some(tiles), sent.at[group], stage.at[0], sibling).wait_send()

    out_far.wait_recv()
    out_near.wait()
    for copy in writes:
        copy.wait()


def widen_result(grad_hbm, down_hbm, grad_out, down_out, tiles, wide, down, sems):
    take = pltpu.make_async_copy(down_hbm, down, sems.at[0])
    pass_on = pltpu.make_async_copy(down, down_out, sems.at[0])
    loads = []
    for dy in range(3):
        for h in range(2):
            span = pl.ds(h * HALF + dy * CHUNK, CHUNK)
            loads.append(pltpu.make_async_copy(grad_hbm.at[span], tiles.at[span], sems.at[1 + dy * 2 + h]))
    for load in loads:
        load.start()
    take.start()
    stores = []
    for dy in range(3):
        for h in range(2):
            loads[dy * 2 + h].wait()
        for k in range(3):
            tap = k * 9 + dy * 3
            for dx in range(3):
                for h in range(2):
                    for q in range(4):
                        spot = h * HALF + ((dy * 3 + k) * 3 + dx) * 4 + q
                        start = (h * 4 + q) * 16
                        wide[tap + dx, start : start + 16] = tiles[spot].astype(F32)
            group = pl.ds(tap, 3)
            stores.append(pltpu.make_async_copy(wide.at[group], grad_out.at[group], sems.at[7 + dy * 3 + k]))
            stores[-1].start()
    take.wait()
    pass_on.start()
    for store in stores:
        store.wait()
    pass_on.wait()


def per_device(nx, nz, ny, video, clip_first, kernel, bias, cotangent):
    _, frames, height, width, chans = video.shape
    half_h, half_w = height // 2, width // 2
    n_tm = nx * nz
    owned = HALF // (nx * ny)
    sa, sb = owned - owned // 2, owned // 2
    any_space = pl.BlockSpec(memory_space=pl.ANY)
    sem = pltpu.SemaphoreType.DMA

    def tiles(*shape):
        return pltpu.VMEM((*shape, 16, chans), BF16)

    down, grad = pl.pallas_call(
        functools.partial(fused, nx, nz, ny, sa, sb),
        out_shape=(
            jax.ShapeDtypeStruct(cotangent.shape, BF16),
            jax.ShapeDtypeStruct((2 * HALF, 16, chans), BF16),
        ),
        in_specs=[any_space] * 5,
        out_specs=(any_space, any_space),
        scratch_shapes=[
            pltpu.SMEM(clip_first.shape, jnp.int32),
            pltpu.VMEM((1, chans), F32),
            pltpu.VMEM((frames, height, width, chans), BF16),
            pltpu.VMEM((frames, height, width, chans), BF16),
            pltpu.VMEM((3, 3, 3, chans, chans), BF16),
            pltpu.VMEM((frames, half_h, half_w, chans), BF16),
            pltpu.VMEM((4, height + 2, width, 3 * chans), BF16),
            pltpu.VMEM((frames, height * width, chans), F32),
            pltpu.VMEM((frames * half_h, width, chans), F32),
            pltpu.VMEM((frames * half_h, width, chans), F32),
            pltpu.VMEM((frames, half_h, half_w, chans), BF16),
            pltpu.VMEM((frames * chans, height * width), BF16),
            pltpu.VMEM((n_tm, 2, chans), F32),
            tiles(2 * HALF),
            tiles(HALF),
            tiles(HALF),
            tiles(ny, nx * sa),
            tiles(nx, ny * sb),
            tiles(nx * sa),
            tiles(ny * sb),
            tiles(nx, sa),
            tiles(ny, sb),
            tiles(sa),
            tiles(sb),
            tiles(nz, sa),
            tiles(nz, sb),
            tiles(2 * HALF),
            sem((9,)),
            sem((5,)),
            sem((4,)),
            sem((3,)),
            sem((11,)),
            sem((ny,)),
            sem((nx,)),
        ],
        compiler_params=pltpu.CompilerParams(
            collective_id=0, has_side_effects=True, vmem_limit_bytes=62 * 1024 * 1024
        ),
    )(clip_first, bias.reshape(1, chans), video, kernel, cotangent)
    grad, down = pl.pallas_call(
        widen_result,
        out_shape=(
            jax.ShapeDtypeStruct((27, chans, chans), F32),
            jax.ShapeDtypeStruct(cotangent.shape, BF16),
        ),
        in_specs=[any_space] * 2,
        out_specs=(any_space, any_space),
        scratch_shapes=[
            tiles(2 * HALF),
            pltpu.VMEM((27, chans, chans), F32),
            pltpu.VMEM(cotangent.shape, BF16),
            sem((16,)),
        ],
        compiler_params=pltpu.CompilerParams(vmem_limit_bytes=62 * 1024 * 1024),
    )(grad, down)
    return down, grad.reshape(3, 3, 3, chans, chans)


def solution(mesh):
    n_tm, n_dp = mesh.shape["tm"], mesh.shape["dp"]
    nz = 8 if n_tm == 32 else 2
    in_specs = (
        P("dp", "tm", None, None, None),
        P("dp", "tm"),
        P(),
        P(),
        P("dp", "tm", None, None, None),
    )
    out_specs = (P("dp", "tm", None, None, None), P())
    return jax.shard_map(
        functools.partial(per_device, n_tm // nz, nz, n_dp // 2),
        mesh=mesh,
        in_specs=in_specs,
        out_specs=out_specs,
        check_vma=False,
    )
```

```python
import functools

import jax
import jax.numpy as jnp
from jax import lax
from jax.experimental import pallas as pl
from jax.experimental.pallas import tpu as pltpu
from jax.sharding import PartitionSpec as P

F32 = jnp.float32
BF16 = jnp.bfloat16
HALF = 28 * 4
CHUNK = 9 * 4


def fused(
    nx,
    nz,
    ny,
    sa,
    sb,
    first_hbm,
    bias_hbm,
    video_hbm,
    kern_hbm,
    cot_hbm,
    down_hbm,
    grad_hbm,
    first_ref,
    bias_ref,
    vid,
    halo,
    kern,
    cot,
    xs,
    acc,
    spread,
    pool,
    down,
    dts,
    gath,
    grads,
    r_pair,
    part,
    r1a,
    r1b,
    s1a,
    s1b,
    r2a,
    r2b,
    s2a,
    s2b,
    r3a,
    r3b,
    full,
    local_sem,
    sent,
    near_recv,
    pair_recv,
    stage,
    line_a,
    line_b,
):
    _, frames, height, width, chans = video_hbm.shape
    half_h, half_w = height // 2, width // 2
    pixels = height * width
    n_tm = nx * nz
    n_a = nx * ny * sa
    za = nx * sa // nz

    tm = lax.axis_index("tm")
    dp = lax.axis_index("dp")
    x, z = tm // nz, tm % nz
    y, core = dp // 2, dp % 2

    def at(tm_to, dp_to):
        return {"tm": tm_to, "dp": dp_to}

    def x_peer(q):
        return at(q * nz + z, dp)

    def y_peer(q):
        return at(tm, q * 2 + core)

    def z_peer(q):
        return at(x * nz + q, dp)

    sibling = at(tm, y * 2 + 1 - core)
    right = at((tm + 1) % n_tm, dp)
    left = at((tm + n_tm - 1) % n_tm, dp)

    def remote(src, dst, send, recv, to):
        return pltpu.make_async_remote_copy(
            src_ref=src,
            dst_ref=dst,
            send_sem=send,
            recv_sem=recv,
            device_id=to,
            device_id_type=pl.DeviceIdType.MESH,
        )

    loads = [
        pltpu.make_async_copy(video_hbm.at[0], vid, local_sem.at[0]),
        pltpu.make_async_copy(first_hbm, first_ref, local_sem.at[1]),
        pltpu.make_async_copy(cot_hbm.at[0, 1], cot.at[0], local_sem.at[2]),
        pltpu.make_async_copy(bias_hbm, bias_ref, local_sem.at[3]),
        pltpu.make_async_copy(kern_hbm, kern, local_sem.at[4]),
    ]
    for load in loads:
        load.start()

    barrier = pltpu.get_barrier_semaphore()
    peers = [z_peer((z + d) % nz) for d in range(1, nz)]
    peers += [x_peer((x + d) % nx) for d in range(1, nx)]
    peers += [y_peer((y + d) % ny) for d in range(1, ny)]
    peers += [left, right, sibling]
    for peer in peers:
        pl.semaphore_signal(barrier, inc=1, device_id=peer, device_id_type=pl.DeviceIdType.MESH)

    loads[0].wait()
    loads[1].wait()
    rows = []
    for f in range(frames):
        value = vid[f].astype(F32)
        rows.append(jnp.sum(jnp.sum(value, axis=0), axis=0, keepdims=True))
        rows.append(jnp.sum(jnp.sum(value * value, axis=0), axis=0, keepdims=True))
    rows.append(jnp.zeros((4, chans), F32))
    stat = jnp.concatenate(rows, axis=0)
    lane8 = lax.broadcasted_iota(jnp.int32, (8, chans), 1)
    stat = stat + jnp.where(lane8 % 2 == 0, pltpu.roll(stat, chans - 1, 1), pltpu.roll(stat, 1, 1))
    stat = stat + jnp.where(lane8 % 4 < 2, pltpu.roll(stat, chans - 2, 1), pltpu.roll(stat, 2, 1))
    lane = lax.broadcasted_iota(jnp.int32, (1, chans), 1)
    low = jnp.where(lane % 2 == 0, stat[0:1], stat[1:2])
    high = jnp.where(lane % 2 == 0, stat[2:3], stat[3:4])
    first0 = jnp.full((1, chans), first_ref[0, 0], jnp.int32)
    first1 = jnp.full((1, chans), first_ref[0, 1], jnp.int32)
    gath[tm, 0:1] = jnp.where(lane % 4 < 2, low, high)
    gath[tm, 1:2] = first0.astype(F32)

    pl.semaphore_wait(barrier, len(peers))

    near = [
        remote(video_hbm.at[0, 1], halo.at[0], sent.at[0], near_recv.at[0], right),
        remote(video_hbm.at[0, 0], halo.at[1], sent.at[0], near_recv.at[1], left),
        remote(cot_hbm.at[0, 0], cot.at[1], sent.at[0], near_recv.at[2], left),
    ]
    for d in range(1, nz):
        remote(gath.at[tm], gath.at[tm], sent.at[4], stage.at[0], z_peer((z + d) % nz)).start()
    for copy in near:
        copy.start()

    rim = jnp.zeros((width, 3 * chans), BF16)
    for s in range(4):
        xs[s, 0] = rim
        xs[s, height + 1] = rim
    for h in range(2):
        for j in range(27 * 4, HALF):
            grads[h * HALF + j] = jnp.zeros((16, chans), BF16)

    def widen(f):
        for i in range(half_h):
            quarter = cot[f, i].astype(F32) * 0.25
            spread[f * half_h + i, pl.ds(0, half_w, stride=2), :] = quarter
            spread[f * half_h + i, pl.ds(1, half_w, stride=2), :] = quarter

    loads[2].wait()
    widen(0)
    loads[3].wait()
    loads[4].wait()

    others = gath.at[pl.ds(0, nz - 1)]
    remote(others, others, sent.at[4], stage.at[0], right).wait_recv()
    line = gath.at[pl.ds(x * nz, nz)]
    for d in range(1, nx):
        remote(line, line, sent.at[4], stage.at[11], x_peer((x + d) % nx)).start()
    others = gath.at[pl.ds(0, (nx - 1) * nz)]
    remote(others, others, sent.at[4], stage.at[11], right).wait_recv()

    t0 = tm * frames
    t2 = (t0 + 2) % (n_tm * frames)
    first2 = gath[(tm + 1) % n_tm, 1:2].astype(jnp.int32)
    gathered = gath[...]
    frame = lax.broadcasted_iota(jnp.int32, gathered.shape, 0) * frames
    frame = frame + lax.broadcasted_iota(jnp.int32, gathered.shape, 2) % 4 // 2

    def moments(first, last):
        chosen = jnp.where((frame >= first[None]) & (frame <= last), gathered, 0.0)
        total = jnp.sum(chosen, axis=0)[0:1]
        count = jnp.maximum((last + 1 - first) * (pixels * 4), 1).astype(F32)
        total = total + jnp.where(lane % 4 < 2, pltpu.roll(total, chans - 2, 1), pltpu.roll(total, 2, 1))
        mean = jnp.where(lane % 2 == 0, total, pltpu.roll(total, 1, 1)) / count
        var = jnp.where(lane % 2 == 1, total, pltpu.roll(total, chans - 1, 1)) / count - mean * mean
        return mean, lax.rsqrt(var + 1e-05)

    col = lax.broadcasted_iota(jnp.int32, (width, chans), 0)

    def place(source, f, slot, mean, scale, keep):
        for r in range(height):
            value = (source[f, r].astype(F32) - mean) * scale
            if keep is not None:
                value = jnp.where(keep, value, 0.0)
            before = jnp.where(col == 0, 0.0, pltpu.roll(value, 1, 0))
            after = jnp.where(col == width - 1, 0.0, pltpu.roll(value, width - 1, 0))
            xs[slot, r + 1, :, 0:chans] = before.astype(BF16)
            xs[slot, r + 1, :, chans : 2 * chans] = value.astype(BF16)
            xs[slot, r + 1, :, 2 * chans : 3 * chans] = after.astype(BF16)

    def flag(condition):
        return jnp.where(condition, 1.0, 0.0)

    t0_t1 = flag(first1 <= t0)
    t0_t2 = flag(first2 <= t2 - 2)
    t1_t2 = flag(first2 <= t2 - 1)
    block = min(8, height)

    def patches(slot, r):
        parts = [xs[slot, r + dy : r + dy + block].reshape(block * width, 3 * chans) for dy in range(3)]
        return jnp.concatenate(parts, axis=1)

    def taps(k):
        return kern[k].reshape(9 * chans, chans)

    def dot(a, b):
        return jnp.dot(a, b, preferred_element_type=F32)

    place(vid, 0, 1, *moments(first0, t0), None)
    place(vid, 1, 2, *moments(first1, t0 + 1), None)
    for r in range(0, height, block):
        px = pl.ds(r * width, block * width)
        one = dot(patches(1, r), jnp.concatenate([taps(1), taps(0)], axis=1))
        two = dot(patches(2, r), jnp.concatenate([taps(2), taps(1)], axis=1))
        acc[0, px] = one[:, :chans] * t0_t1 + two[:, :chans]
        acc[1, px] = one[:, chans:] * t0_t2 + two[:, chans:] * t1_t2

    bias = bias_ref[...]

    def finish_conv(f, slot, k):
        for r in range(0, height, block):
            last = dot(patches(slot, r), taps(k))
            for m in range(block // 2):
                i = r // 2 + m
                px = slice(i * 2 * width, (i + 1) * 2 * width)
                value = acc[f, px] + last[m * 2 * width : (m + 1) * 2 * width] + bias
                logistic = 1.0 / (1.0 + jnp.exp(-value))
                active = value * logistic
                pool[f * half_h + i] = active[:width] + active[width:]
                slope = logistic * (1.0 + value * (1.0 - logistic))
                over = spread[f * half_h + i]
                dconv = jnp.concatenate([over, over], axis=0) * slope
                dts[f * chans : (f + 1) * chans, px] = dconv.T.astype(BF16)
        for i in range(half_h):
            even = pool[f * half_h + i, pl.ds(0, half_w, stride=2), :]
            odd = pool[f * half_h + i, pl.ds(1, half_w, stride=2), :]
            down[f, i] = ((even + odd) * 0.25).astype(BF16)

    near[0].wait_recv()
    place(halo, 0, 0, *moments(first1, t0 - 1), first1 <= t0 - 1)
    finish_conv(0, 0, 0)
    near[2].wait_recv()
    widen(1)
    near[1].wait_recv()
    place(halo, 1, 3, *moments(first2, t2), None)
    finish_conv(1, 3, 2)
    out_far = remote(down.at[1], down_hbm.at[0, 0], sent.at[0], near_recv.at[3], right)
    out_near = pltpu.make_async_copy(down.at[0], down_hbm.at[0, 1], local_sem.at[5])
    out_far.start()
    out_near.start()


    def pair(c):
        tiles = pl.ds(c * CHUNK, CHUNK if c < 2 else HALF - 2 * CHUNK)
        src = grads.at[pl.ds((1 - core) * HALF + tiles.start, tiles.size)]
        return remote(src, r_pair.at[tiles], sent.at[1], pair_recv.at[c], sibling)

    def join_pair(c):
        pair(c).wait_recv()
        tiles = pl.ds(c * CHUNK, CHUNK if c < 2 else HALF - 2 * CHUNK)
        own = grads[pl.ds(core * HALF + tiles.start, tiles.size)].astype(F32)
        part[tiles] = (own + r_pair[tiles].astype(F32)).astype(BF16)

    def first_a(q):
        src = part.at[pl.ds(q * nx * sa, nx * sa)]
        return remote(src, r1a.at[y], sent.at[1], stage.at[1], y_peer(q))

    def first_b(q):
        src = part.at[pl.ds(n_a + q * ny * sb, ny * sb)]
        return remote(src, r1b.at[x], sent.at[1], stage.at[2], x_peer(q))

    def go(make, me, owners):
        for q in owners:

            @pl.when(q != me)
            def _():
                make(q).start()

    def a_ready(done):
        return [q for q in range(ny) if (q + 1) * nx * sa <= done]

    started = []
    for dy in range(3):
        shifted = [xs[s, dy : dy + height].reshape(pixels, 3 * chans) for s in range(4)]
        both = dts[...]
        r0 = dot(both[:chans], shifted[0])
        r1 = dot(both, shifted[1])
        r2 = dot(both, shifted[2])
        r3 = dot(both[chans:], shifted[3])
        m01, m02, m12 = t0_t1[:, 0:1], t0_t2[:, 0:1], t1_t2[:, 0:1]
        sums = [r0 + r1[chans:] * m02, r1[:chans] * m01 + r2[chans:] * m12, r2[:chans] + r3]
        for k in range(3):
            for dx in range(3):
                tile = sums[k][:, dx * chans : (dx + 1) * chans].T.astype(BF16)
                spot = ((dy * 3 + k) * 3 + dx) * 4
                for h in range(2):
                    for q in range(4):
                        start = (h * 4 + q) * 16
                        grads[h * HALF + spot + q] = tile[start : start + 16]
        pair(dy).start()
        if dy > 0:
            join_pair(dy - 1)
            ready = [q for q in a_ready(dy * CHUNK) if q not in started]
            go(first_a, y, ready)
            started += ready
    join_pair(2)
    go(first_a, y, [q for q in range(ny) if q not in started])
    go(first_b, x, range(nx))

    def exchange(n, me, src_of, dst, place, peer):
        for d in range(1, n):
            q = (me + d) % n
            remote(src_of(q), dst.at[me], sent.at[2], stage.at[place], peer(q)).start()

    def arrived(n, dst, place):
        rows = dst.at[pl.ds(0, n - 1)]
        remote(rows, rows, sent.at[2], stage.at[place], sibling).wait_recv()

    def summed(n, me, own, dst):
        total = own.astype(F32)
        for d in range(1, n):
            total = total + dst[(me + n - d) % n].astype(F32)
        return total.astype(BF16)

    arrived(ny, r1a, 1)
    s1a[...] = summed(ny, y, part[pl.ds(y * nx * sa, nx * sa)], r1a)
    exchange(nz, z, lambda q: s1a.at[pl.ds(q * za, za)], r2a, 3, z_peer)
    arrived(nx, r1b, 2)
    s1b[...] = summed(nx, x, part[pl.ds(n_a + x * ny * sb, ny * sb)], r1b)
    exchange(ny, y, lambda q: s1b.at[pl.ds(q * sb, sb)], r2b, 4, y_peer)

    arrived(nz, r2a, 3)
    s2a[...] = summed(nz, z, s1a[pl.ds(z * za, za)], r2a)
    exchange(nx, x, lambda q: s2a, r3a, 5, x_peer)
    arrived(ny, r2b, 4)
    s2b[...] = summed(ny, y, s1b[pl.ds(y * sb, sb)], r2b)
    exchange(nz, z, lambda q: s2b, r3b, 6, z_peer)

    base = core * HALF

    def a_line(q, start=base):
        return full.at[pl.ds(start + q * nx * sa, nx * sa)]

    def b_line(q, start=base):
        return full.at[pl.ds(start + n_a + q * ny * sb, ny * sb)]

    def spread_out(n, me, piece, group, recv, peer):
        for d in range(1, n):
            remote(piece, piece, sent.at[group], recv, peer((me + d) % n)).start()

    def some(tiles):
        return full.at[pl.ds(0, tiles)]

    arrived(nx, r3a, 5)
    a_piece = full.at[pl.ds(base + y * nx * sa + z * za, za)]
    a_piece[...] = summed(nx, x, s2a[...], r3a)
    spread_out(nz, z, a_piece, 2, stage.at[7], z_peer)
    arrived(nz, r3b, 6)
    b_piece = full.at[pl.ds(base + n_a + (x * ny + y) * sb, sb)]
    b_piece[...] = summed(nz, z, s2b[...], r3b)
    spread_out(ny, y, b_piece, 2, stage.at[8], y_peer)

    def give_a(q):
        remote(a_line(q), a_line(q), sent.at[3], stage.at[9], sibling).start()

    def give_b(q):
        remote(b_line(q), b_line(q), sent.at[3], stage.at[10], sibling).start()

    remote(some((nz - 1) * za), some((nz - 1) * za), sent.at[2], stage.at[7], sibling).wait_recv()
    spread_out(ny, y, a_line(y), 3, line_a.at[y], y_peer)
    give_a(y)
    remote(some((ny - 1) * sb), some((ny - 1) * sb), sent.at[2], stage.at[8], sibling).wait_recv()
    spread_out(nx, x, b_line(x), 3, line_b.at[x], x_peer)
    give_b(x)
    for d in range(1, ny):
        q = (y + ny - d) % ny
        remote(a_line(q), a_line(q), sent.at[3], line_a.at[q], sibling).wait_recv()
        give_a(q)
    for d in range(1, nx):
        q = (x + nx - d) % nx
        remote(b_line(q), b_line(q), sent.at[3], line_b.at[q], sibling).wait_recv()
        give_b(q)

    def write(start, size, place):
        tiles = pl.ds(start, size)
        copy = pltpu.make_async_copy(full.at[tiles], grad_hbm.at[tiles], local_sem.at[place])
        copy.start()
        return copy

    writes = [write(base, HALF, 6)]
    base = (1 - core) * HALF
    remote(some(n_a), some(n_a), sent.at[3], stage.at[9], sibling).wait_recv()
    writes.append(write(base, n_a, 7))
    remote(some(HALF - n_a), some(HALF - n_a), sent.at[3], stage.at[10], sibling).wait_recv()
    writes.append(write(base + n_a, HALF - n_a, 8))

    others = gath.at[pl.ds(0, n_tm - 1)]
    remote(others, others, sent.at[4], stage.at[0], right).wait_send()
    lines = (ny - 1) * nx * sa + (nx - 1) * ny * sb
    pieces = 2 * ((nz - 1) * za + (ny - 1) * sb) + (nx - 1) * za + (nz - 1) * sb
    frames_out = frames * (pixels + half_h * half_w) // 16
    for group, tiles in ((0, frames_out), (1, HALF + lines), (2, pieces), (3, HALF + lines)):
        remote(some(tiles), some(tiles), sent.at[group], stage.at[0], sibling).wait_send()

    out_far.wait_recv()
    out_near.wait()
    for copy in writes:
        copy.wait()


def widen_result(grad_hbm, down_hbm, grad_out, down_out, tiles, wide, down, sems):
    take = pltpu.make_async_copy(down_hbm, down, sems.at[0])
    pass_on = pltpu.make_async_copy(down, down_out, sems.at[0])
    loads = []
    for dy in range(3):
        for h in range(2):
            span = pl.ds(h * HALF + dy * CHUNK, CHUNK)
            loads.append(pltpu.make_async_copy(grad_hbm.at[span], tiles.at[span], sems.at[1 + dy * 2 + h]))
    for load in loads:
        load.start()
    take.start()
    stores = []
    for dy in range(3):
        for h in range(2):
            loads[dy * 2 + h].wait()
        for k in range(3):
            tap = k * 9 + dy * 3
            for dx in range(3):
                for h in range(2):
                    for q in range(4):
                        spot = h * HALF + ((dy * 3 + k) * 3 + dx) * 4 + q
                        start = (h * 4 + q) * 16
                        wide[tap + dx, start : start + 16] = tiles[spot].astype(F32)
            group = pl.ds(tap, 3)
            stores.append(pltpu.make_async_copy(wide.at[group], grad_out.at[group], sems.at[7 + dy * 3 + k]))
            stores[-1].start()
    take.wait()
    pass_on.start()
    for store in stores:
        store.wait()
    pass_on.wait()


def per_device(nx, nz, ny, video, clip_first, kernel, bias, cotangent):
    _, frames, height, width, chans = video.shape
    half_h, half_w = height // 2, width // 2
    n_tm = nx * nz
    owned = HALF // (nx * ny)
    sa, sb = owned - owned // 2, owned // 2
    any_space = pl.BlockSpec(memory_space=pl.ANY)
    sem = pltpu.SemaphoreType.DMA

    def tiles(*shape):
        return pltpu.VMEM((*shape, 16, chans), BF16)

    down, grad = pl.pallas_call(
        functools.partial(fused, nx, nz, ny, sa, sb),
        out_shape=(
            jax.ShapeDtypeStruct(cotangent.shape, BF16),
            jax.ShapeDtypeStruct((2 * HALF, 16, chans), BF16),
        ),
        in_specs=[any_space] * 5,
        out_specs=(any_space, any_space),
        scratch_shapes=[
            pltpu.SMEM(clip_first.shape, jnp.int32),
            pltpu.VMEM((1, chans), F32),
            pltpu.VMEM((frames, height, width, chans), BF16),
            pltpu.VMEM((frames, height, width, chans), BF16),
            pltpu.VMEM((3, 3, 3, chans, chans), BF16),
            pltpu.VMEM((frames, half_h, half_w, chans), BF16),
            pltpu.VMEM((4, height + 2, width, 3 * chans), BF16),
            pltpu.VMEM((frames, height * width, chans), F32),
            pltpu.VMEM((frames * half_h, width, chans), F32),
            pltpu.VMEM((frames * half_h, width, chans), F32),
            pltpu.VMEM((frames, half_h, half_w, chans), BF16),
            pltpu.VMEM((frames * chans, height * width), BF16),
            pltpu.VMEM((n_tm, 2, chans), F32),
            tiles(2 * HALF),
            tiles(HALF),
            tiles(HALF),
            tiles(ny, nx * sa),
            tiles(nx, ny * sb),
            tiles(nx * sa),
            tiles(ny * sb),
            tiles(nz, nx * sa // nz),
            tiles(ny, sb),
            tiles(nx * sa // nz),
            tiles(sb),
            tiles(nx, nx * sa // nz),
            tiles(nz, sb),
            tiles(2 * HALF),
            sem((9,)),
            sem((5,)),
            sem((4,)),
            sem((3,)),
            sem((12,)),
            sem((ny,)),
            sem((nx,)),
        ],
        compiler_params=pltpu.CompilerParams(
            collective_id=0, has_side_effects=True, vmem_limit_bytes=62 * 1024 * 1024
        ),
    )(clip_first, bias.reshape(1, chans), video, kernel, cotangent)
    grad, down = pl.pallas_call(
        widen_result,
        out_shape=(
            jax.ShapeDtypeStruct((27, chans, chans), F32),
            jax.ShapeDtypeStruct(cotangent.shape, BF16),
        ),
        in_specs=[any_space] * 2,
        out_specs=(any_space, any_space),
        scratch_shapes=[
            tiles(2 * HALF),
            pltpu.VMEM((27, chans, chans), F32),
            pltpu.VMEM(cotangent.shape, BF16),
            sem((16,)),
        ],
        compiler_params=pltpu.CompilerParams(vmem_limit_bytes=62 * 1024 * 1024),
    )(grad, down)
    return down, grad.reshape(3, 3, 3, chans, chans)


def solution(mesh):
    n_tm, n_dp = mesh.shape["tm"], mesh.shape["dp"]
    nz = 8 if n_tm == 32 else 2
    in_specs = (
        P("dp", "tm", None, None, None),
        P("dp", "tm"),
        P(),
        P(),
        P("dp", "tm", None, None, None),
    )
    out_specs = (P("dp", "tm", None, None, None), P())
    return jax.shard_map(
        functools.partial(per_device, n_tm // nz, nz, n_dp // 2),
        mesh=mesh,
        in_specs=in_specs,
        out_specs=out_specs,
        check_vma=False,
    )
```

```python
import functools

import jax
import jax.numpy as jnp
from jax import lax
from jax.experimental import pallas as pl
from jax.experimental.pallas import tpu as pltpu
from jax.sharding import PartitionSpec as P

F32 = jnp.float32
BF16 = jnp.bfloat16
HALF = 28 * 4
CHUNK = 9 * 4


def fused(
    nx,
    nz,
    ny,
    sa,
    sb,
    first_hbm,
    bias_hbm,
    video_hbm,
    kern_hbm,
    cot_hbm,
    down_hbm,
    grad_hbm,
    first_ref,
    bias_ref,
    vid,
    halo,
    kern,
    cot,
    xs,
    acc,
    spread,
    pool,
    down,
    dcs,
    gath,
    grads,
    r_pair,
    part,
    r1a,
    r1b,
    s1a,
    s1b,
    r2a,
    r2b,
    s2a,
    s2b,
    r3a,
    r3b,
    full,
    local_sem,
    sent,
    near_recv,
    pair_recv,
    stage,
    line_a,
    line_b,
):
    _, frames, height, width, chans = video_hbm.shape
    half_h, half_w = height // 2, width // 2
    pixels = height * width
    n_tm = nx * nz
    n_a = nx * ny * sa
    za = nx * sa // nz

    tm = lax.axis_index("tm")
    dp = lax.axis_index("dp")
    x, z = tm // nz, tm % nz
    y, core = dp // 2, dp % 2

    def at(tm_to, dp_to):
        return {"tm": tm_to, "dp": dp_to}

    def x_peer(q):
        return at(q * nz + z, dp)

    def y_peer(q):
        return at(tm, q * 2 + core)

    def z_peer(q):
        return at(x * nz + q, dp)

    sibling = at(tm, y * 2 + 1 - core)
    right = at((tm + 1) % n_tm, dp)
    left = at((tm + n_tm - 1) % n_tm, dp)

    def remote(src, dst, send, recv, to):
        return pltpu.make_async_remote_copy(
            src_ref=src,
            dst_ref=dst,
            send_sem=send,
            recv_sem=recv,
            device_id=to,
            device_id_type=pl.DeviceIdType.MESH,
        )

    loads = [
        pltpu.make_async_copy(video_hbm.at[0], vid, local_sem.at[0]),
        pltpu.make_async_copy(first_hbm, first_ref, local_sem.at[1]),
        pltpu.make_async_copy(cot_hbm.at[0, 1], cot.at[0], local_sem.at[2]),
        pltpu.make_async_copy(bias_hbm, bias_ref, local_sem.at[3]),
        pltpu.make_async_copy(kern_hbm, kern, local_sem.at[4]),
    ]
    for load in loads:
        load.start()

    barrier = pltpu.get_barrier_semaphore()
    peers = [at((tm + d) % n_tm, dp) for d in range(1, n_tm)]
    peers += [y_peer((y + d) % ny) for d in range(1, ny)]
    peers += [sibling]
    for peer in peers:
        pl.semaphore_signal(barrier, inc=1, device_id=peer, device_id_type=pl.DeviceIdType.MESH)

    loads[0].wait()
    loads[1].wait()
    rows = []
    for f in range(frames):
        value = vid[f].astype(F32)
        rows.append(jnp.sum(jnp.sum(value, axis=0), axis=0, keepdims=True))
        rows.append(jnp.sum(jnp.sum(value * value, axis=0), axis=0, keepdims=True))
    rows.append(jnp.zeros((4, chans), F32))
    stat = jnp.concatenate(rows, axis=0)
    lane8 = lax.broadcasted_iota(jnp.int32, (8, chans), 1)
    stat = stat + jnp.where(lane8 % 2 == 0, pltpu.roll(stat, chans - 1, 1), pltpu.roll(stat, 1, 1))
    stat = stat + jnp.where(lane8 % 4 < 2, pltpu.roll(stat, chans - 2, 1), pltpu.roll(stat, 2, 1))
    lane = lax.broadcasted_iota(jnp.int32, (1, chans), 1)
    low = jnp.where(lane % 2 == 0, stat[0:1], stat[1:2])
    high = jnp.where(lane % 2 == 0, stat[2:3], stat[3:4])
    first0 = jnp.full((1, chans), first_ref[0, 0], jnp.int32)
    first1 = jnp.full((1, chans), first_ref[0, 1], jnp.int32)
    gath[tm, 0:1] = jnp.where(lane % 4 < 2, low, high)
    gath[tm, 1:2] = first0.astype(F32)

    pl.semaphore_wait(barrier, len(peers))

    parts = 4
    step = height // parts
    edges = [0] + [c * step + 1 for c in range(1, parts)] + [height]
    spans = [pl.ds(start, end - start) for start, end in zip(edges[:-1], edges[1:])]
    near = []
    for c, span in enumerate(spans):
        near += [
            remote(video_hbm.at[0, 1, span], halo.at[0, span], sent.at[0], near_recv.at[2 * c], right),
            remote(video_hbm.at[0, 0, span], halo.at[1, span], sent.at[0], near_recv.at[2 * c + 1], left),
        ]
    near_cot = remote(cot_hbm.at[0, 0], cot.at[1], sent.at[0], near_recv.at[2 * parts], left)
    for d in range(1, n_tm):
        remote(gath.at[tm], gath.at[tm], sent.at[4], stage.at[0], at((tm + d) % n_tm, dp)).start()
    near_cot.start()
    for copy in near:
        copy.start()

    rim = jnp.zeros((width, 3 * chans), BF16)
    for s in range(4):
        xs[s, 0] = rim
        xs[s, height + 1] = rim
    for h in range(2):
        for j in range(27 * 4, HALF):
            grads[h * HALF + j] = jnp.zeros((16, chans), BF16)

    def widen(f):
        for i in range(half_h):
            quarter = cot[f, i].astype(F32) * 0.25
            spread[f * half_h + i, pl.ds(0, half_w, stride=2), :] = quarter
            spread[f * half_h + i, pl.ds(1, half_w, stride=2), :] = quarter

    loads[2].wait()
    widen(0)
    loads[3].wait()
    loads[4].wait()

    others = gath.at[pl.ds(0, n_tm - 1)]
    remote(others, others, sent.at[4], stage.at[0], right).wait_recv()

    t0 = tm * frames
    t2 = (t0 + 2) % (n_tm * frames)
    first2 = gath[(tm + 1) % n_tm, 1:2].astype(jnp.int32)
    gathered = gath[...]
    frame = lax.broadcasted_iota(jnp.int32, gathered.shape, 0) * frames
    frame = frame + lax.broadcasted_iota(jnp.int32, gathered.shape, 2) % 4 // 2

    def moments(first, last):
        chosen = jnp.where((frame >= first[None]) & (frame <= last), gathered, 0.0)
        total = jnp.sum(chosen, axis=0)[0:1]
        count = jnp.maximum((last + 1 - first) * (pixels * 4), 1).astype(F32)
        total = total + jnp.where(lane % 4 < 2, pltpu.roll(total, chans - 2, 1), pltpu.roll(total, 2, 1))
        mean = jnp.where(lane % 2 == 0, total, pltpu.roll(total, 1, 1)) / count
        var = jnp.where(lane % 2 == 1, total, pltpu.roll(total, chans - 1, 1)) / count - mean * mean
        return mean, lax.rsqrt(var + 1e-05)

    col = lax.broadcasted_iota(jnp.int32, (width, chans), 0)

    def place(source, f, slot, mean, scale, keep, span):
        for r in range(span.start, span.start + span.size):
            value = (source[f, r].astype(F32) - mean) * scale
            if keep is not None:
                value = jnp.where(keep, value, 0.0)
            before = jnp.where(col == 0, 0.0, pltpu.roll(value, 1, 0))
            after = jnp.where(col == width - 1, 0.0, pltpu.roll(value, width - 1, 0))
            xs[slot, r + 1, :, 0:chans] = before.astype(BF16)
            xs[slot, r + 1, :, chans : 2 * chans] = value.astype(BF16)
            xs[slot, r + 1, :, 2 * chans : 3 * chans] = after.astype(BF16)

    def flag(condition):
        return jnp.where(condition, 1.0, 0.0)

    t0_t1 = flag(first1 <= t0)
    t0_t2 = flag(first2 <= t2 - 2)
    t1_t2 = flag(first2 <= t2 - 1)
    block = min(8, height)

    def patches(slot, r, rows):
        shifts = [xs[slot, r + dy : r + dy + rows].reshape(rows * width, 3 * chans) for dy in range(3)]
        return jnp.concatenate(shifts, axis=1)

    def taps(k):
        return kern[k].reshape(9 * chans, chans)

    def dot(a, b):
        return jnp.dot(a, b, preferred_element_type=F32)

    rows = pl.ds(0, height)
    place(vid, 0, 1, *moments(first0, t0), None, rows)
    place(vid, 1, 2, *moments(first1, t0 + 1), None, rows)
    for r in range(0, height, block):
        px = pl.ds(r * width, block * width)
        one = dot(patches(1, r, block), jnp.concatenate([taps(1), taps(0)], axis=1))
        two = dot(patches(2, r, block), jnp.concatenate([taps(2), taps(1)], axis=1))
        acc[0, px] = one[:, :chans] * t0_t1 + two[:, :chans]
        acc[1, px] = one[:, chans:] * t0_t2 + two[:, chans:] * t1_t2

    bias = bias_ref[...]

    def finish_conv(f, slot, k, r):
        last = dot(patches(slot, r, step), taps(k))
        for m in range(step // 2):
            i = r // 2 + m
            px = slice(i * 2 * width, (i + 1) * 2 * width)
            value = acc[f, px] + last[m * 2 * width : (m + 1) * 2 * width] + bias
            logistic = 1.0 / (1.0 + jnp.exp(-value))
            active = value * logistic
            pool[f * half_h + i] = active[:width] + active[width:]
            slope = logistic * (1.0 + value * (1.0 - logistic))
            over = spread[f * half_h + i]
            dconv = jnp.concatenate([over, over], axis=0) * slope
            dcs[px, f * chans : (f + 1) * chans] = dconv.astype(BF16)
        for i in range(r // 2, (r + step) // 2):
            even = pool[f * half_h + i, pl.ds(0, half_w, stride=2), :]
            odd = pool[f * half_h + i, pl.ds(1, half_w, stride=2), :]
            down[f, i] = ((even + odd) * 0.25).astype(BF16)

    earlier = (*moments(first1, t0 - 1), first1 <= t0 - 1)
    later = (*moments(first2, t2), None)
    near_cot.wait_recv()
    widen(1)
    for c, span in enumerate(spans):
        near[2 * c].wait_recv()
        near[2 * c + 1].wait_recv()
        place(halo, 0, 0, *earlier, span)
        place(halo, 1, 3, *later, span)
        finish_conv(0, 0, 0, c * step)
        finish_conv(1, 3, 2, c * step)
    out_far = remote(down.at[1], down_hbm.at[0, 0], sent.at[0], near_recv.at[2 * parts + 1], right)
    out_near = pltpu.make_async_copy(down.at[0], down_hbm.at[0, 1], local_sem.at[5])
    out_far.start()
    out_near.start()


    def pair(c):
        tiles = pl.ds(c * CHUNK, CHUNK if c < 2 else HALF - 2 * CHUNK)
        src = grads.at[pl.ds((1 - core) * HALF + tiles.start, tiles.size)]
        return remote(src, r_pair.at[tiles], sent.at[1], pair_recv.at[c], sibling)

    def join_pair(c):
        pair(c).wait_recv()
        tiles = pl.ds(c * CHUNK, CHUNK if c < 2 else HALF - 2 * CHUNK)
        own = grads[pl.ds(core * HALF + tiles.start, tiles.size)].astype(F32)
        part[tiles] = (own + r_pair[tiles].astype(F32)).astype(BF16)

    def first_a(q):
        src = part.at[pl.ds(q * nx * sa, nx * sa)]
        return remote(src, r1a.at[y], sent.at[1], stage.at[1], y_peer(q))

    def first_b(q):
        src = part.at[pl.ds(n_a + q * ny * sb, ny * sb)]
        return remote(src, r1b.at[x], sent.at[1], stage.at[2], x_peer(q))

    def go(make, me, owners):
        for q in owners:

            @pl.when(q != me)
            def _():
                make(q).start()

    def a_ready(done):
        return [q for q in range(ny) if (q + 1) * nx * sa <= done]

    def tap_dot(a, b):
        return lax.dot_general(a, b, (((0,), (0,)), ((), ())), preferred_element_type=F32)

    started = []
    for dy in range(3):
        shifted = [xs[s, dy : dy + height].reshape(pixels, 3 * chans) for s in range(4)]
        both = dcs[...]
        r0 = tap_dot(shifted[0], both[:, :chans])
        r1 = tap_dot(shifted[1], both)
        r2 = tap_dot(shifted[2], both)
        r3 = tap_dot(shifted[3], both[:, chans:])
        sums = [
            r0 + r1[:, chans:] * t0_t2,
            r1[:, :chans] * t0_t1 + r2[:, chans:] * t1_t2,
            r2[:, :chans] + r3,
        ]
        for k in range(3):
            for dx in range(3):
                tile = sums[k][dx * chans : (dx + 1) * chans].astype(BF16)
                spot = ((dy * 3 + k) * 3 + dx) * 4
                for h in range(2):
                    for q in range(4):
                        start = (h * 4 + q) * 16
                        grads[h * HALF + spot + q] = tile[start : start + 16]
        pair(dy).start()
        if dy > 0:
            join_pair(dy - 1)
            ready = [q for q in a_ready(dy * CHUNK) if q not in started]
            go(first_a, y, ready)
            started += ready
    join_pair(2)
    go(first_a, y, [q for q in range(ny) if q not in started])
    go(first_b, x, range(nx))

    def exchange(n, me, src_of, dst, place, peer):
        for d in range(1, n):
            q = (me + d) % n
            remote(src_of(q), dst.at[me], sent.at[2], stage.at[place], peer(q)).start()

    def arrived(n, dst, place):
        rows = dst.at[pl.ds(0, n - 1)]
        remote(rows, rows, sent.at[2], stage.at[place], sibling).wait_recv()

    def summed(n, me, own, dst):
        total = own.astype(F32)
        for d in range(1, n):
            total = total + dst[(me + n - d) % n].astype(F32)
        return total.astype(BF16)

    arrived(ny, r1a, 1)
    s1a[...] = summed(ny, y, part[pl.ds(y * nx * sa, nx * sa)], r1a)
    exchange(nz, z, lambda q: s1a.at[pl.ds(q * za, za)], r2a, 3, z_peer)
    arrived(nx, r1b, 2)
    s1b[...] = summed(nx, x, part[pl.ds(n_a + x * ny * sb, ny * sb)], r1b)
    exchange(ny, y, lambda q: s1b.at[pl.ds(q * sb, sb)], r2b, 4, y_peer)

    arrived(nz, r2a, 3)
    s2a[...] = summed(nz, z, s1a[pl.ds(z * za, za)], r2a)
    exchange(nx, x, lambda q: s2a, r3a, 5, x_peer)
    arrived(ny, r2b, 4)
    s2b[...] = summed(ny, y, s1b[pl.ds(y * sb, sb)], r2b)
    exchange(nz, z, lambda q: s2b, r3b, 6, z_peer)

    base = core * HALF

    def a_line(q, start=base):
        return full.at[pl.ds(start + q * nx * sa, nx * sa)]

    def b_line(q, start=base):
        return full.at[pl.ds(start + n_a + q * ny * sb, ny * sb)]

    def spread_out(n, me, piece, group, recv, peer):
        for d in range(1, n):
            remote(piece, piece, sent.at[group], recv, peer((me + d) % n)).start()

    def some(tiles):
        return full.at[pl.ds(0, tiles)]

    arrived(nx, r3a, 5)
    a_piece = full.at[pl.ds(base + y * nx * sa + z * za, za)]
    a_piece[...] = summed(nx, x, s2a[...], r3a)
    spread_out(nz, z, a_piece, 2, stage.at[7], z_peer)
    arrived(nz, r3b, 6)
    b_piece = full.at[pl.ds(base + n_a + (x * ny + y) * sb, sb)]
    b_piece[...] = summed(nz, z, s2b[...], r3b)
    spread_out(ny, y, b_piece, 2, stage.at[8], y_peer)

    def give_a(q):
        remote(a_line(q), a_line(q), sent.at[3], stage.at[9], sibling).start()

    def give_b(q):
        remote(b_line(q), b_line(q), sent.at[3], stage.at[10], sibling).start()

    remote(some((nz - 1) * za), some((nz - 1) * za), sent.at[2], stage.at[7], sibling).wait_recv()
    spread_out(ny, y, a_line(y), 3, line_a.at[y], y_peer)
    give_a(y)
    remote(some((ny - 1) * sb), some((ny - 1) * sb), sent.at[2], stage.at[8], sibling).wait_recv()
    spread_out(nx, x, b_line(x), 3, line_b.at[x], x_peer)
    give_b(x)
    for d in range(1, ny):
        q = (y + ny - d) % ny
        remote(a_line(q), a_line(q), sent.at[3], line_a.at[q], sibling).wait_recv()
        give_a(q)
    for d in range(1, nx):
        q = (x + nx - d) % nx
        remote(b_line(q), b_line(q), sent.at[3], line_b.at[q], sibling).wait_recv()
        give_b(q)

    def write(start, size, place):
        tiles = pl.ds(start, size)
        copy = pltpu.make_async_copy(full.at[tiles], grad_hbm.at[tiles], local_sem.at[place])
        copy.start()
        return copy

    writes = [write(base, HALF, 6)]
    base = (1 - core) * HALF
    remote(some(n_a), some(n_a), sent.at[3], stage.at[9], sibling).wait_recv()
    writes.append(write(base, n_a, 7))
    remote(some(HALF - n_a), some(HALF - n_a), sent.at[3], stage.at[10], sibling).wait_recv()
    writes.append(write(base + n_a, HALF - n_a, 8))

    remote(others, others, sent.at[4], stage.at[0], right).wait_send()
    lines = (ny - 1) * nx * sa + (nx - 1) * ny * sb
    pieces = 2 * ((nz - 1) * za + (ny - 1) * sb) + (nx - 1) * za + (nz - 1) * sb
    frames_out = frames * (pixels + half_h * half_w) // 16
    for group, tiles in ((0, frames_out), (1, HALF + lines), (2, pieces), (3, HALF + lines)):
        remote(some(tiles), some(tiles), sent.at[group], stage.at[0], sibling).wait_send()

    out_far.wait_recv()
    out_near.wait()
    for copy in writes:
        copy.wait()


def widen_result(grad_hbm, down_hbm, grad_out, down_out, tiles, wide, down, sems):
    take = pltpu.make_async_copy(down_hbm, down, sems.at[0])
    pass_on = pltpu.make_async_copy(down, down_out, sems.at[0])
    loads = []
    for dy in range(3):
        for h in range(2):
            span = pl.ds(h * HALF + dy * CHUNK, CHUNK)
            loads.append(pltpu.make_async_copy(grad_hbm.at[span], tiles.at[span], sems.at[1 + dy * 2 + h]))
    for load in loads:
        load.start()
    take.start()
    stores = []
    for dy in range(3):
        for h in range(2):
            loads[dy * 2 + h].wait()
        for k in range(3):
            tap = k * 9 + dy * 3
            for dx in range(3):
                for h in range(2):
                    for q in range(4):
                        spot = h * HALF + ((dy * 3 + k) * 3 + dx) * 4 + q
                        start = (h * 4 + q) * 16
                        wide[tap + dx, start : start + 16] = tiles[spot].astype(F32)
            group = pl.ds(tap, 3)
            stores.append(pltpu.make_async_copy(wide.at[group], grad_out.at[group], sems.at[7 + dy * 3 + k]))
            stores[-1].start()
    take.wait()
    pass_on.start()
    for store in stores:
        store.wait()
    pass_on.wait()


def per_device(nx, nz, ny, video, clip_first, kernel, bias, cotangent):
    _, frames, height, width, chans = video.shape
    half_h, half_w = height // 2, width // 2
    n_tm = nx * nz
    owned = HALF // (nx * ny)
    sa, sb = owned - owned // 2, owned // 2
    any_space = pl.BlockSpec(memory_space=pl.ANY)
    sem = pltpu.SemaphoreType.DMA

    def tiles(*shape):
        return pltpu.VMEM((*shape, 16, chans), BF16)

    down, grad = pl.pallas_call(
        functools.partial(fused, nx, nz, ny, sa, sb),
        out_shape=(
            jax.ShapeDtypeStruct(cotangent.shape, BF16),
            jax.ShapeDtypeStruct((2 * HALF, 16, chans), BF16),
        ),
        in_specs=[any_space] * 5,
        out_specs=(any_space, any_space),
        scratch_shapes=[
            pltpu.SMEM(clip_first.shape, jnp.int32),
            pltpu.VMEM((1, chans), F32),
            pltpu.VMEM((frames, height, width, chans), BF16),
            pltpu.VMEM((frames, height, width, chans), BF16),
            pltpu.VMEM((3, 3, 3, chans, chans), BF16),
            pltpu.VMEM((frames, half_h, half_w, chans), BF16),
            pltpu.VMEM((4, height + 2, width, 3 * chans), BF16),
            pltpu.VMEM((frames, height * width, chans), F32),
            pltpu.VMEM((frames * half_h, width, chans), F32),
            pltpu.VMEM((frames * half_h, width, chans), F32),
            pltpu.VMEM((frames, half_h, half_w, chans), BF16),
            pltpu.VMEM((height * width, frames * chans), BF16),
            pltpu.VMEM((n_tm, 2, chans), F32),
            tiles(2 * HALF),
            tiles(HALF),
            tiles(HALF),
            tiles(ny, nx * sa),
            tiles(nx, ny * sb),
            tiles(nx * sa),
            tiles(ny * sb),
            tiles(nz, nx * sa // nz),
            tiles(ny, sb),
            tiles(nx * sa // nz),
            tiles(sb),
            tiles(nx, nx * sa // nz),
            tiles(nz, sb),
            tiles(2 * HALF),
            sem((9,)),
            sem((5,)),
            sem((10,)),
            sem((3,)),
            sem((12,)),
            sem((ny,)),
            sem((nx,)),
        ],
        compiler_params=pltpu.CompilerParams(
            collective_id=0, has_side_effects=True, vmem_limit_bytes=62 * 1024 * 1024
        ),
    )(clip_first, bias.reshape(1, chans), video, kernel, cotangent)
    grad, down = pl.pallas_call(
        widen_result,
        out_shape=(
            jax.ShapeDtypeStruct((27, chans, chans), F32),
            jax.ShapeDtypeStruct(cotangent.shape, BF16),
        ),
        in_specs=[any_space] * 2,
        out_specs=(any_space, any_space),
        scratch_shapes=[
            tiles(2 * HALF),
            pltpu.VMEM((27, chans, chans), F32),
            pltpu.VMEM(cotangent.shape, BF16),
            sem((16,)),
        ],
        compiler_params=pltpu.CompilerParams(vmem_limit_bytes=62 * 1024 * 1024),
    )(grad, down)
    return down, grad.reshape(3, 3, 3, chans, chans)


def solution(mesh):
    n_tm, n_dp = mesh.shape["tm"], mesh.shape["dp"]
    nz = 8 if n_tm == 32 else 2
    in_specs = (
        P("dp", "tm", None, None, None),
        P("dp", "tm"),
        P(),
        P(),
        P("dp", "tm", None, None, None),
    )
    out_specs = (P("dp", "tm", None, None, None), P())
    return jax.shard_map(
        functools.partial(per_device, n_tm // nz, nz, n_dp // 2),
        mesh=mesh,
        in_specs=in_specs,
        out_specs=out_specs,
        check_vma=False,
    )
```

```python
import functools

import jax
import jax.numpy as jnp
from jax import lax
from jax.experimental import pallas as pl
from jax.experimental.pallas import tpu as pltpu
from jax.sharding import PartitionSpec as P

F32 = jnp.float32
BF16 = jnp.bfloat16
HALF = 28 * 4
CHUNK = 9 * 4


def fused(
    nx,
    nz,
    ny,
    sa,
    sb,
    first_hbm,
    bias_hbm,
    video_hbm,
    kern_hbm,
    cot_hbm,
    down_hbm,
    grad_hbm,
    first_ref,
    bias_ref,
    vid,
    halo,
    kern,
    cot,
    xs,
    acc,
    spread,
    pool,
    down,
    dcs,
    gath,
    grads,
    r_pair,
    part,
    r1a,
    r1b,
    s1a,
    s1b,
    r2a,
    r2b,
    s2a,
    s2b,
    r3a,
    r3b,
    full,
    local_sem,
    sent,
    near_recv,
    pair_recv,
    stage,
    line_a,
    line_b,
    lines_out,
):
    _, frames, height, width, chans = video_hbm.shape
    half_h, half_w = height // 2, width // 2
    pixels = height * width
    n_tm = nx * nz
    n_a = nx * ny * sa
    za = nx * sa // nz

    tm = lax.axis_index("tm")
    dp = lax.axis_index("dp")
    x, z = tm // nz, tm % nz
    y, core = dp // 2, dp % 2

    def at(tm_to, dp_to):
        return {"tm": tm_to, "dp": dp_to}

    def x_peer(q):
        return at(q * nz + z, dp)

    def y_peer(q):
        return at(tm, q * 2 + core)

    def z_peer(q):
        return at(x * nz + q, dp)

    def far_first(n):
        return sorted(range(1, n), key=lambda d: -min(d, n - d))

    sibling = at(tm, y * 2 + 1 - core)
    right = at((tm + 1) % n_tm, dp)
    left = at((tm + n_tm - 1) % n_tm, dp)

    def remote(src, dst, send, recv, to):
        return pltpu.make_async_remote_copy(
            src_ref=src,
            dst_ref=dst,
            send_sem=send,
            recv_sem=recv,
            device_id=to,
            device_id_type=pl.DeviceIdType.MESH,
        )

    loads = [
        pltpu.make_async_copy(video_hbm.at[0], vid, local_sem.at[0]),
        pltpu.make_async_copy(first_hbm, first_ref, local_sem.at[1]),
        pltpu.make_async_copy(cot_hbm.at[0, 1], cot.at[0], local_sem.at[2]),
        pltpu.make_async_copy(bias_hbm, bias_ref, local_sem.at[3]),
        pltpu.make_async_copy(kern_hbm, kern, local_sem.at[4]),
    ]
    for load in loads:
        load.start()

    barrier = pltpu.get_barrier_semaphore()
    peers = [at((tm + d) % n_tm, dp) for d in range(1, n_tm)]
    peers += [y_peer((y + d) % ny) for d in range(1, ny)]
    peers += [sibling]
    for peer in peers:
        pl.semaphore_signal(barrier, inc=1, device_id=peer, device_id_type=pl.DeviceIdType.MESH)

    loads[0].wait()
    loads[1].wait()
    rows = []
    for f in range(frames):
        value = vid[f].astype(F32)
        rows.append(jnp.sum(jnp.sum(value, axis=0), axis=0, keepdims=True))
        rows.append(jnp.sum(jnp.sum(value * value, axis=0), axis=0, keepdims=True))
    rows.append(jnp.zeros((4, chans), F32))
    stat = jnp.concatenate(rows, axis=0)
    lane8 = lax.broadcasted_iota(jnp.int32, (8, chans), 1)
    stat = stat + jnp.where(lane8 % 2 == 0, pltpu.roll(stat, chans - 1, 1), pltpu.roll(stat, 1, 1))
    stat = stat + jnp.where(lane8 % 4 < 2, pltpu.roll(stat, chans - 2, 1), pltpu.roll(stat, 2, 1))
    lane = lax.broadcasted_iota(jnp.int32, (1, chans), 1)
    low = jnp.where(lane % 2 == 0, stat[0:1], stat[1:2])
    high = jnp.where(lane % 2 == 0, stat[2:3], stat[3:4])
    first0 = jnp.full((1, chans), first_ref[0, 0], jnp.int32)
    first1 = jnp.full((1, chans), first_ref[0, 1], jnp.int32)
    gath[tm, 0:1] = jnp.where(lane % 4 < 2, low, high)
    gath[tm, 1:2] = first0.astype(F32)

    pl.semaphore_wait(barrier, len(peers))

    parts = 4
    step = height // parts
    edges = [0] + [c * step + 1 for c in range(1, parts)] + [height]
    spans = [pl.ds(start, end - start) for start, end in zip(edges[:-1], edges[1:])]
    near = []
    for c, span in enumerate(spans):
        near += [
            remote(video_hbm.at[0, 1, span], halo.at[0, span], sent.at[0], near_recv.at[2 * c], right),
            remote(video_hbm.at[0, 0, span], halo.at[1, span], sent.at[0], near_recv.at[2 * c + 1], left),
        ]
    near_cot = remote(cot_hbm.at[0, 0], cot.at[1], sent.at[0], near_recv.at[2 * parts], left)
    for d in range(1, n_tm):
        remote(gath.at[tm], gath.at[tm], sent.at[4], stage.at[0], at((tm + d) % n_tm, dp)).start()
    near_cot.start()
    for copy in near:
        copy.start()

    rim = jnp.zeros((width, 3 * chans), BF16)
    for s in range(4):
        xs[s, 0] = rim
        xs[s, height + 1] = rim
    for h in range(2):
        for j in range(27 * 4, HALF):
            grads[h * HALF + j] = jnp.zeros((16, chans), BF16)

    def widen(f):
        for i in range(half_h):
            quarter = cot[f, i].astype(F32) * 0.25
            spread[f * half_h + i, pl.ds(0, half_w, stride=2), :] = quarter
            spread[f * half_h + i, pl.ds(1, half_w, stride=2), :] = quarter

    loads[2].wait()
    widen(0)
    loads[3].wait()
    loads[4].wait()

    others = gath.at[pl.ds(0, n_tm - 1)]
    remote(others, others, sent.at[4], stage.at[0], right).wait_recv()

    t0 = tm * frames
    t2 = (t0 + 2) % (n_tm * frames)
    first2 = gath[(tm + 1) % n_tm, 1:2].astype(jnp.int32)
    gathered = gath[...]
    frame = lax.broadcasted_iota(jnp.int32, gathered.shape, 0) * frames
    frame = frame + lax.broadcasted_iota(jnp.int32, gathered.shape, 2) % 4 // 2

    def moments(first, last):
        chosen = jnp.where((frame >= first[None]) & (frame <= last), gathered, 0.0)
        total = jnp.sum(chosen, axis=0)[0:1]
        count = jnp.maximum((last + 1 - first) * (pixels * 4), 1).astype(F32)
        total = total + jnp.where(lane % 4 < 2, pltpu.roll(total, chans - 2, 1), pltpu.roll(total, 2, 1))
        mean = jnp.where(lane % 2 == 0, total, pltpu.roll(total, 1, 1)) / count
        var = jnp.where(lane % 2 == 1, total, pltpu.roll(total, chans - 1, 1)) / count - mean * mean
        return mean, lax.rsqrt(var + 1e-05)

    col = lax.broadcasted_iota(jnp.int32, (width, chans), 0)

    def place(source, f, slot, mean, scale, keep, span):
        for r in range(span.start, span.start + span.size):
            value = (source[f, r].astype(F32) - mean) * scale
            if keep is not None:
                value = jnp.where(keep, value, 0.0)
            before = jnp.where(col == 0, 0.0, pltpu.roll(value, 1, 0))
            after = jnp.where(col == width - 1, 0.0, pltpu.roll(value, width - 1, 0))
            xs[slot, r + 1, :, 0:chans] = before.astype(BF16)
            xs[slot, r + 1, :, chans : 2 * chans] = value.astype(BF16)
            xs[slot, r + 1, :, 2 * chans : 3 * chans] = after.astype(BF16)

    def flag(condition):
        return jnp.where(condition, 1.0, 0.0)

    t0_t1 = flag(first1 <= t0)
    t0_t2 = flag(first2 <= t2 - 2)
    t1_t2 = flag(first2 <= t2 - 1)
    block = min(8, height)

    def patches(slot, r, rows):
        shifts = [xs[slot, r + dy : r + dy + rows].reshape(rows * width, 3 * chans) for dy in range(3)]
        return jnp.concatenate(shifts, axis=1)

    def taps(k):
        return kern[k].reshape(9 * chans, chans)

    def dot(a, b):
        return jnp.dot(a, b, preferred_element_type=F32)

    rows = pl.ds(0, height)
    place(vid, 0, 1, *moments(first0, t0), None, rows)
    place(vid, 1, 2, *moments(first1, t0 + 1), None, rows)
    for r in range(0, height, block):
        px = pl.ds(r * width, block * width)
        one = dot(patches(1, r, block), jnp.concatenate([taps(1), taps(0)], axis=1))
        two = dot(patches(2, r, block), jnp.concatenate([taps(2), taps(1)], axis=1))
        acc[0, px] = one[:, :chans] * t0_t1 + two[:, :chans]
        acc[1, px] = one[:, chans:] * t0_t2 + two[:, chans:] * t1_t2

    bias = bias_ref[...]

    def finish_conv(f, slot, k, r):
        last = dot(patches(slot, r, step), taps(k))
        for m in range(step // 2):
            i = r // 2 + m
            px = slice(i * 2 * width, (i + 1) * 2 * width)
            value = acc[f, px] + last[m * 2 * width : (m + 1) * 2 * width] + bias
            logistic = 1.0 / (1.0 + jnp.exp(-value))
            active = value * logistic
            pool[f * half_h + i] = active[:width] + active[width:]
            slope = logistic * (1.0 + value * (1.0 - logistic))
            over = spread[f * half_h + i]
            dconv = jnp.concatenate([over, over], axis=0) * slope
            dcs[px, f * chans : (f + 1) * chans] = dconv.astype(BF16)
        for i in range(r // 2, (r + step) // 2):
            even = pool[f * half_h + i, pl.ds(0, half_w, stride=2), :]
            odd = pool[f * half_h + i, pl.ds(1, half_w, stride=2), :]
            down[f, i] = ((even + odd) * 0.25).astype(BF16)

    earlier = (*moments(first1, t0 - 1), first1 <= t0 - 1)
    later = (*moments(first2, t2), None)
    near_cot.wait_recv()
    widen(1)
    for c, span in enumerate(spans):
        near[2 * c].wait_recv()
        near[2 * c + 1].wait_recv()
        place(halo, 0, 0, *earlier, span)
        place(halo, 1, 3, *later, span)
        finish_conv(0, 0, 0, c * step)
        finish_conv(1, 3, 2, c * step)
    out_far = remote(down.at[1], down_hbm.at[0, 0], sent.at[0], near_recv.at[2 * parts + 1], right)
    out_near = pltpu.make_async_copy(down.at[0], down_hbm.at[0, 1], local_sem.at[5])
    out_far.start()
    out_near.start()


    def pair(c):
        tiles = pl.ds(c * CHUNK, CHUNK if c < 2 else HALF - 2 * CHUNK)
        src = grads.at[pl.ds((1 - core) * HALF + tiles.start, tiles.size)]
        return remote(src, r_pair.at[tiles], sent.at[1], pair_recv.at[c], sibling)

    def join_pair(c):
        pair(c).wait_recv()
        tiles = pl.ds(c * CHUNK, CHUNK if c < 2 else HALF - 2 * CHUNK)
        own = grads[pl.ds(core * HALF + tiles.start, tiles.size)].astype(F32)
        part[tiles] = (own + r_pair[tiles].astype(F32)).astype(BF16)

    def first_a(q):
        src = part.at[pl.ds(q * nx * sa, nx * sa)]
        return remote(src, r1a.at[y], sent.at[1], stage.at[1], y_peer(q))

    def first_b(q):
        src = part.at[pl.ds(n_a + q * ny * sb, ny * sb)]
        return remote(src, r1b.at[x], sent.at[1], stage.at[2], x_peer(q))

    def go(make, me, owners):
        for q in owners:

            @pl.when(q != me)
            def _():
                make(q).start()

    def a_ready(done):
        return [q for q in range(ny) if (q + 1) * nx * sa <= done]

    def tap_dot(a, b):
        return lax.dot_general(a, b, (((0,), (0,)), ((), ())), preferred_element_type=F32)

    started = []
    for dy in range(3):
        shifted = [xs[s, dy : dy + height].reshape(pixels, 3 * chans) for s in range(4)]
        both = dcs[...]
        r0 = tap_dot(shifted[0], both[:, :chans])
        r1 = tap_dot(shifted[1], both)
        r2 = tap_dot(shifted[2], both)
        r3 = tap_dot(shifted[3], both[:, chans:])
        sums = [
            r0 + r1[:, chans:] * t0_t2,
            r1[:, :chans] * t0_t1 + r2[:, chans:] * t1_t2,
            r2[:, :chans] + r3,
        ]
        for k in range(3):
            for dx in range(3):
                tile = sums[k][dx * chans : (dx + 1) * chans].astype(BF16)
                spot = ((dy * 3 + k) * 3 + dx) * 4
                for h in range(2):
                    for q in range(4):
                        start = (h * 4 + q) * 16
                        grads[h * HALF + spot + q] = tile[start : start + 16]
        pair(dy).start()
        if dy > 0:
            join_pair(dy - 1)
            ready = [q for q in a_ready(dy * CHUNK) if q not in started]
            go(first_a, y, ready)
            started += ready
    join_pair(2)
    go(first_a, y, [q for q in range(ny) if q not in started])
    go(first_b, x, range(nx))

    def exchange(n, me, src_of, dst, place, peer):
        for d in far_first(n):
            q = (me + d) % n
            remote(src_of(q), dst.at[me], sent.at[2], stage.at[place], peer(q)).start()

    def arrived(n, dst, place):
        rows = dst.at[pl.ds(0, n - 1)]
        remote(rows, rows, sent.at[2], stage.at[place], sibling).wait_recv()

    def summed(n, me, own, dst):
        total = own.astype(F32)
        for d in range(1, n):
            total = total + dst[(me + n - d) % n].astype(F32)
        return total.astype(BF16)

    arrived(ny, r1a, 1)
    s1a[...] = summed(ny, y, part[pl.ds(y * nx * sa, nx * sa)], r1a)
    exchange(nz, z, lambda q: s1a.at[pl.ds(q * za, za)], r2a, 3, z_peer)
    arrived(nx, r1b, 2)
    s1b[...] = summed(nx, x, part[pl.ds(n_a + x * ny * sb, ny * sb)], r1b)
    exchange(ny, y, lambda q: s1b.at[pl.ds(q * sb, sb)], r2b, 4, y_peer)

    arrived(nz, r2a, 3)
    s2a[...] = summed(nz, z, s1a[pl.ds(z * za, za)], r2a)
    exchange(nx, x, lambda q: s2a, r3a, 5, x_peer)
    arrived(ny, r2b, 4)
    s2b[...] = summed(ny, y, s1b[pl.ds(y * sb, sb)], r2b)
    exchange(nz, z, lambda q: s2b, r3b, 6, z_peer)

    base = core * HALF

    def a_line(q, start=base):
        return full.at[pl.ds(start + q * nx * sa, nx * sa)]

    def b_line(q, start=base):
        return full.at[pl.ds(start + n_a + q * ny * sb, ny * sb)]

    def spread_out(n, me, piece, group, recv, peer):
        for d in far_first(n):
            remote(piece, piece, sent.at[group], recv, peer((me + d) % n)).start()

    def some(tiles):
        return full.at[pl.ds(0, tiles)]

    arrived(nx, r3a, 5)
    a_piece = full.at[pl.ds(base + y * nx * sa + z * za, za)]
    a_piece[...] = summed(nx, x, s2a[...], r3a)
    spread_out(nz, z, a_piece, 2, stage.at[7], z_peer)
    arrived(nz, r3b, 6)
    b_piece = full.at[pl.ds(base + n_a + (x * ny + y) * sb, sb)]
    b_piece[...] = summed(nz, z, s2b[...], r3b)
    spread_out(ny, y, b_piece, 2, stage.at[8], y_peer)

    def give(tiles, place):
        remote(full.at[tiles], grad_hbm.at[tiles], sent.at[3], stage.at[9], sibling).start()
        copy = pltpu.make_async_copy(full.at[tiles], grad_hbm.at[tiles], lines_out.at[place])
        copy.start()
        writes.append(copy)

    writes = []

    def give_a(q):
        give(pl.ds(base + q * nx * sa, nx * sa), len(writes))

    def give_b(q):
        give(pl.ds(base + n_a + q * ny * sb, ny * sb), len(writes))

    remote(some((nz - 1) * za), some((nz - 1) * za), sent.at[2], stage.at[7], sibling).wait_recv()
    spread_out(ny, y, a_line(y), 3, line_a.at[y], y_peer)
    give_a(y)
    remote(some((ny - 1) * sb), some((ny - 1) * sb), sent.at[2], stage.at[8], sibling).wait_recv()
    spread_out(nx, x, b_line(x), 3, line_b.at[x], x_peer)
    give_b(x)
    for d in reversed(far_first(ny)):
        q = (y + ny - d) % ny
        remote(a_line(q), a_line(q), sent.at[3], line_a.at[q], sibling).wait_recv()
        give_a(q)
    for d in reversed(far_first(nx)):
        q = (x + nx - d) % nx
        remote(b_line(q), b_line(q), sent.at[3], line_b.at[q], sibling).wait_recv()
        give_b(q)

    remote(others, others, sent.at[4], stage.at[0], right).wait_send()
    lines = (ny - 1) * nx * sa + (nx - 1) * ny * sb
    pieces = 2 * ((nz - 1) * za + (ny - 1) * sb) + (nx - 1) * za + (nz - 1) * sb
    frames_out = frames * (pixels + half_h * half_w) // 16
    for group, tiles in ((0, frames_out), (1, HALF + lines), (2, pieces), (3, HALF + lines)):
        remote(some(tiles), some(tiles), sent.at[group], stage.at[0], sibling).wait_send()

    theirs = grad_hbm.at[pl.ds((1 - core) * HALF, HALF)]
    remote(theirs, theirs, sent.at[3], stage.at[9], sibling).wait_recv()
    out_far.wait_recv()
    out_near.wait()
    for copy in writes:
        copy.wait()


def widen_result(grad_hbm, down_hbm, grad_out, down_out, tiles, wide, down, sems):
    take = pltpu.make_async_copy(down_hbm, down, sems.at[0])
    pass_on = pltpu.make_async_copy(down, down_out, sems.at[0])
    loads = []
    for dy in range(3):
        for h in range(2):
            span = pl.ds(h * HALF + dy * CHUNK, CHUNK)
            loads.append(pltpu.make_async_copy(grad_hbm.at[span], tiles.at[span], sems.at[1 + dy * 2 + h]))
    for load in loads:
        load.start()
    take.start()
    stores = []
    for dy in range(3):
        for h in range(2):
            loads[dy * 2 + h].wait()
        for k in range(3):
            tap = k * 9 + dy * 3
            for dx in range(3):
                for h in range(2):
                    for q in range(4):
                        spot = h * HALF + ((dy * 3 + k) * 3 + dx) * 4 + q
                        start = (h * 4 + q) * 16
                        wide[tap + dx, start : start + 16] = tiles[spot].astype(F32)
            group = pl.ds(tap, 3)
            stores.append(pltpu.make_async_copy(wide.at[group], grad_out.at[group], sems.at[7 + dy * 3 + k]))
            stores[-1].start()
    take.wait()
    pass_on.start()
    for store in stores:
        store.wait()
    pass_on.wait()


def per_device(nx, nz, ny, video, clip_first, kernel, bias, cotangent):
    _, frames, height, width, chans = video.shape
    half_h, half_w = height // 2, width // 2
    n_tm = nx * nz
    owned = HALF // (nx * ny)
    sa, sb = owned - owned // 2, owned // 2
    any_space = pl.BlockSpec(memory_space=pl.ANY)
    sem = pltpu.SemaphoreType.DMA

    def tiles(*shape):
        return pltpu.VMEM((*shape, 16, chans), BF16)

    down, grad = pl.pallas_call(
        functools.partial(fused, nx, nz, ny, sa, sb),
        out_shape=(
            jax.ShapeDtypeStruct(cotangent.shape, BF16),
            jax.ShapeDtypeStruct((2 * HALF, 16, chans), BF16),
        ),
        in_specs=[any_space] * 5,
        out_specs=(any_space, any_space),
        scratch_shapes=[
            pltpu.SMEM(clip_first.shape, jnp.int32),
            pltpu.VMEM((1, chans), F32),
            pltpu.VMEM((frames, height, width, chans), BF16),
            pltpu.VMEM((frames, height, width, chans), BF16),
            pltpu.VMEM((3, 3, 3, chans, chans), BF16),
            pltpu.VMEM((frames, half_h, half_w, chans), BF16),
            pltpu.VMEM((4, height + 2, width, 3 * chans), BF16),
            pltpu.VMEM((frames, height * width, chans), F32),
            pltpu.VMEM((frames * half_h, width, chans), F32),
            pltpu.VMEM((frames * half_h, width, chans), F32),
            pltpu.VMEM((frames, half_h, half_w, chans), BF16),
            pltpu.VMEM((height * width, frames * chans), BF16),
            pltpu.VMEM((n_tm, 2, chans), F32),
            tiles(2 * HALF),
            tiles(HALF),
            tiles(HALF),
            tiles(ny, nx * sa),
            tiles(nx, ny * sb),
            tiles(nx * sa),
            tiles(ny * sb),
            tiles(nz, nx * sa // nz),
            tiles(ny, sb),
            tiles(nx * sa // nz),
            tiles(sb),
            tiles(nx, nx * sa // nz),
            tiles(nz, sb),
            tiles(2 * HALF),
            sem((9,)),
            sem((5,)),
            sem((10,)),
            sem((3,)),
            sem((12,)),
            sem((ny,)),
            sem((nx,)),
            sem((ny + nx,)),
        ],
        compiler_params=pltpu.CompilerParams(
            collective_id=0, has_side_effects=True, vmem_limit_bytes=62 * 1024 * 1024
        ),
    )(clip_first, bias.reshape(1, chans), video, kernel, cotangent)
    grad, down = pl.pallas_call(
        widen_result,
        out_shape=(
            jax.ShapeDtypeStruct((27, chans, chans), F32),
            jax.ShapeDtypeStruct(cotangent.shape, BF16),
        ),
        in_specs=[any_space] * 2,
        out_specs=(any_space, any_space),
        scratch_shapes=[
            tiles(2 * HALF),
            pltpu.VMEM((27, chans, chans), F32),
            pltpu.VMEM(cotangent.shape, BF16),
            sem((16,)),
        ],
        compiler_params=pltpu.CompilerParams(vmem_limit_bytes=62 * 1024 * 1024),
    )(grad, down)
    return down, grad.reshape(3, 3, 3, chans, chans)


def solution(mesh):
    n_tm, n_dp = mesh.shape["tm"], mesh.shape["dp"]
    nz = 8 if n_tm == 32 else 2
    in_specs = (
        P("dp", "tm", None, None, None),
        P("dp", "tm"),
        P(),
        P(),
        P("dp", "tm", None, None, None),
    )
    out_specs = (P("dp", "tm", None, None, None), P())
    return jax.shard_map(
        functools.partial(per_device, n_tm // nz, nz, n_dp // 2),
        mesh=mesh,
        in_specs=in_specs,
        out_specs=out_specs,
        check_vma=False,
    )
```

```python
import functools

import jax
import jax.numpy as jnp
from jax import lax
from jax.experimental import pallas as pl
from jax.experimental.pallas import tpu as pltpu
from jax.sharding import PartitionSpec as P

F32 = jnp.float32
BF16 = jnp.bfloat16
HALF = 28 * 4
CHUNK = 9 * 4


def fused(
    nx,
    nz,
    ny,
    sa,
    sb,
    first_hbm,
    bias_hbm,
    video_hbm,
    kern_hbm,
    cot_hbm,
    down_hbm,
    grad_hbm,
    first_ref,
    bias_ref,
    vid,
    halo,
    kern,
    cot,
    xs,
    acc,
    spread,
    pool,
    down,
    dcs,
    gath,
    grads,
    r_pair,
    part,
    r1a,
    r1b,
    s1a,
    s1b,
    r2a,
    r2b,
    s2a,
    s2b,
    r3a,
    r3b,
    full,
    local_sem,
    sent,
    near_recv,
    pair_recv,
    stage,
    line_a,
    line_b,
    lines_out,
):
    _, frames, height, width, chans = video_hbm.shape
    half_h, half_w = height // 2, width // 2
    pixels = height * width
    n_tm = nx * nz
    n_a = nx * ny * sa
    za = nx * sa // nz

    tm = lax.axis_index("tm")
    dp = lax.axis_index("dp")
    x, z = lax.div(tm, nz), lax.rem(tm, nz)
    y, core = lax.div(dp, 2), lax.rem(dp, 2)

    def at(tm_to, dp_to):
        return {"tm": tm_to, "dp": dp_to}

    def x_peer(q):
        return at(q * nz + z, dp)

    def y_peer(q):
        return at(tm, q * 2 + core)

    def z_peer(q):
        return at(x * nz + q, dp)

    def far_first(n):
        return sorted(range(1, n), key=lambda d: -min(d, n - d))

    sibling = at(tm, y * 2 + 1 - core)
    right = at(lax.rem(tm + 1, n_tm), dp)
    left = at(lax.rem(tm + n_tm - 1, n_tm), dp)

    def remote(src, dst, send, recv, to):
        return pltpu.make_async_remote_copy(
            src_ref=src,
            dst_ref=dst,
            send_sem=send,
            recv_sem=recv,
            device_id=to,
            device_id_type=pl.DeviceIdType.MESH,
        )

    loads = [
        pltpu.make_async_copy(video_hbm.at[0], vid, local_sem.at[0]),
        pltpu.make_async_copy(first_hbm, first_ref, local_sem.at[1]),
        pltpu.make_async_copy(cot_hbm.at[0, 1], cot.at[0], local_sem.at[2]),
        pltpu.make_async_copy(bias_hbm, bias_ref, local_sem.at[3]),
        pltpu.make_async_copy(kern_hbm, kern, local_sem.at[4]),
    ]
    for load in loads:
        load.start()

    barrier = pltpu.get_barrier_semaphore()
    line = [at(lax.rem(tm + d, n_tm), dp) for d in range(1, n_tm)]
    peers = line + [y_peer(lax.rem(y + d, ny)) for d in range(1, ny)]
    peers += [sibling]
    for peer in peers:
        pl.semaphore_signal(barrier, inc=1, device_id=peer, device_id_type=pl.DeviceIdType.MESH)

    loads[0].wait()
    loads[1].wait()
    rows = []
    for f in range(frames):
        value = vid[f].astype(F32)
        rows.append(jnp.sum(jnp.sum(value, axis=0), axis=0, keepdims=True))
        rows.append(jnp.sum(jnp.sum(value * value, axis=0), axis=0, keepdims=True))
    rows.append(jnp.zeros((4, chans), F32))
    stat = jnp.concatenate(rows, axis=0)
    lane8 = lax.broadcasted_iota(jnp.int32, (8, chans), 1)
    stat = stat + jnp.where(lane8 % 2 == 0, pltpu.roll(stat, chans - 1, 1), pltpu.roll(stat, 1, 1))
    stat = stat + jnp.where(lane8 % 4 < 2, pltpu.roll(stat, chans - 2, 1), pltpu.roll(stat, 2, 1))
    lane = lax.broadcasted_iota(jnp.int32, (1, chans), 1)
    low = jnp.where(lane % 2 == 0, stat[0:1], stat[1:2])
    high = jnp.where(lane % 2 == 0, stat[2:3], stat[3:4])
    first0 = jnp.full((1, chans), first_ref[0, 0], jnp.int32)
    first1 = jnp.full((1, chans), first_ref[0, 1], jnp.int32)
    gath[tm, 0:1] = jnp.where(lane % 4 < 2, low, high)
    gath[tm, 1:2] = first0.astype(F32)

    pl.semaphore_wait(barrier, len(peers))

    parts = 4
    step = height // parts
    edges = [0] + [c * step + 1 for c in range(1, parts)] + [height]
    spans = [pl.ds(start, end - start) for start, end in zip(edges[:-1], edges[1:])]
    near = []
    for c, span in enumerate(spans):
        near += [
            remote(video_hbm.at[0, 1, span], halo.at[0, span], sent.at[0], near_recv.at[2 * c], right),
            remote(video_hbm.at[0, 0, span], halo.at[1, span], sent.at[0], near_recv.at[2 * c + 1], left),
        ]
    near_cot = remote(cot_hbm.at[0, 0], cot.at[1], sent.at[0], near_recv.at[2 * parts], left)
    for peer in line:
        remote(gath.at[tm], gath.at[tm], sent.at[4], stage.at[0], peer).start()
    for copy in near:
        copy.start()
    near_cot.start()

    rim = jnp.zeros((width, 3 * chans), BF16)
    for s in range(4):
        xs[s, 0] = rim
        xs[s, height + 1] = rim
    for h in range(2):
        for j in range(27 * 4, HALF):
            grads[h * HALF + j] = jnp.zeros((16, chans), BF16)

    def widen(f):
        for i in range(half_h):
            quarter = cot[f, i].astype(F32) * 0.25
            spread[f * half_h + i, pl.ds(0, half_w, stride=2), :] = quarter
            spread[f * half_h + i, pl.ds(1, half_w, stride=2), :] = quarter

    loads[2].wait()
    widen(0)
    loads[3].wait()
    loads[4].wait()

    others = gath.at[pl.ds(0, n_tm - 1)]
    remote(others, others, sent.at[4], stage.at[0], right).wait_recv()

    t0 = tm * frames
    t2 = lax.rem(t0 + 2, n_tm * frames)
    first2 = gath[lax.rem(tm + 1, n_tm), 1:2].astype(jnp.int32)
    gathered = gath[...]
    frame = lax.broadcasted_iota(jnp.int32, gathered.shape, 0) * frames
    frame = frame + lax.broadcasted_iota(jnp.int32, gathered.shape, 2) % 4 // 2

    def moments(first, last):
        chosen = jnp.where((frame >= first[None]) & (frame <= last), gathered, 0.0)
        total = jnp.sum(chosen, axis=0)[0:1]
        count = jnp.maximum((last + 1 - first) * (pixels * 4), 1).astype(F32)
        total = total + jnp.where(lane % 4 < 2, pltpu.roll(total, chans - 2, 1), pltpu.roll(total, 2, 1))
        mean = jnp.where(lane % 2 == 0, total, pltpu.roll(total, 1, 1)) / count
        var = jnp.where(lane % 2 == 1, total, pltpu.roll(total, chans - 1, 1)) / count - mean * mean
        return mean, lax.rsqrt(var + 1e-05)

    col = lax.broadcasted_iota(jnp.int32, (width, chans), 0)

    def place(source, f, slot, mean, scale, keep, span):
        for r in range(span.start, span.start + span.size):
            value = (source[f, r].astype(F32) - mean) * scale
            if keep is not None:
                value = jnp.where(keep, value, 0.0)
            before = jnp.where(col == 0, 0.0, pltpu.roll(value, 1, 0))
            after = jnp.where(col == width - 1, 0.0, pltpu.roll(value, width - 1, 0))
            xs[slot, r + 1, :, 0:chans] = before.astype(BF16)
            xs[slot, r + 1, :, chans : 2 * chans] = value.astype(BF16)
            xs[slot, r + 1, :, 2 * chans : 3 * chans] = after.astype(BF16)

    def flag(condition):
        return jnp.where(condition, 1.0, 0.0)

    t0_t1 = flag(first1 <= t0)
    t0_t2 = flag(first2 <= t2 - 2)
    t1_t2 = flag(first2 <= t2 - 1)
    block = min(8, height)

    def patches(slot, r, rows):
        shifts = [xs[slot, r + dy : r + dy + rows].reshape(rows * width, 3 * chans) for dy in range(3)]
        return jnp.concatenate(shifts, axis=1)

    def taps(k):
        return kern[k].reshape(9 * chans, chans)

    def dot(a, b):
        return jnp.dot(a, b, preferred_element_type=F32)

    rows = pl.ds(0, height)
    place(vid, 0, 1, *moments(first0, t0), None, rows)
    place(vid, 1, 2, *moments(first1, t0 + 1), None, rows)
    for r in range(0, height, block):
        px = pl.ds(r * width, block * width)
        one = dot(patches(1, r, block), jnp.concatenate([taps(1), taps(0)], axis=1))
        two = dot(patches(2, r, block), jnp.concatenate([taps(2), taps(1)], axis=1))
        acc[0, px] = one[:, :chans] * t0_t1 + two[:, :chans]
        acc[1, px] = one[:, chans:] * t0_t2 + two[:, chans:] * t1_t2

    bias = bias_ref[...]

    def finish_conv(f, slot, k, r):
        last = dot(patches(slot, r, step), taps(k))
        for m in range(step // 2):
            i = r // 2 + m
            px = slice(i * 2 * width, (i + 1) * 2 * width)
            value = acc[f, px] + last[m * 2 * width : (m + 1) * 2 * width] + bias
            logistic = 1.0 / (1.0 + jnp.exp(-value))
            active = value * logistic
            pool[f * half_h + i] = active[:width] + active[width:]
            slope = logistic * (1.0 + value * (1.0 - logistic))
            if f == 0:
                over = spread[i]
                dcs[px, :chans] = (jnp.concatenate([over, over], axis=0) * slope).astype(BF16)
            else:
                acc[f, px] = slope
        for i in range(r // 2, (r + step) // 2):
            even = pool[f * half_h + i, pl.ds(0, half_w, stride=2), :]
            odd = pool[f * half_h + i, pl.ds(1, half_w, stride=2), :]
            down[f, i] = ((even + odd) * 0.25).astype(BF16)

    earlier = (*moments(first1, t0 - 1), first1 <= t0 - 1)
    later = (*moments(first2, t2), None)
    for c, span in enumerate(spans):
        near[2 * c].wait_recv()
        near[2 * c + 1].wait_recv()
        place(halo, 0, 0, *earlier, span)
        place(halo, 1, 3, *later, span)
        finish_conv(0, 0, 0, c * step)
        finish_conv(1, 3, 2, c * step)

    near_cot.wait_recv()
    widen(1)
    for i in range(half_h):
        px = slice(i * 2 * width, (i + 1) * 2 * width)
        over = spread[half_h + i]
        dcs[px, chans:] = (jnp.concatenate([over, over], axis=0) * acc[1, px]).astype(BF16)
    out_far = remote(down.at[1], down_hbm.at[0, 0], sent.at[0], near_recv.at[2 * parts + 1], right)
    out_near = pltpu.make_async_copy(down.at[0], down_hbm.at[0, 1], local_sem.at[5])
    out_far.start()
    out_near.start()


    def pair(c):
        tiles = pl.ds(c * CHUNK, CHUNK if c < 2 else HALF - 2 * CHUNK)
        src = grads.at[pl.ds((1 - core) * HALF + tiles.start, tiles.size)]
        return remote(src, r_pair.at[tiles], sent.at[1], pair_recv.at[c], sibling)

    def join_pair(c):
        pair(c).wait_recv()
        tiles = pl.ds(c * CHUNK, CHUNK if c < 2 else HALF - 2 * CHUNK)
        own = grads[pl.ds(core * HALF + tiles.start, tiles.size)].astype(F32)
        part[tiles] = (own + r_pair[tiles].astype(F32)).astype(BF16)

    def first_a(q):
        src = part.at[pl.ds(q * nx * sa, nx * sa)]
        return remote(src, r1a.at[y], sent.at[1], stage.at[1], y_peer(q))

    def first_b(q):
        src = part.at[pl.ds(n_a + q * ny * sb, ny * sb)]
        return remote(src, r1b.at[x], sent.at[1], stage.at[2], x_peer(q))

    def go(make, me, owners):
        for q in owners:

            @pl.when(q != me)
            def _():
                make(q).start()

    def a_ready(done):
        return [q for q in range(ny) if (q + 1) * nx * sa <= done]

    def tap_dot(a, b):
        return lax.dot_general(a, b, (((0,), (0,)), ((), ())), preferred_element_type=F32)

    started = []
    for dy in range(3):
        shifted = [xs[s, dy : dy + height].reshape(pixels, 3 * chans) for s in range(4)]
        both = dcs[...]
        r0 = tap_dot(shifted[0], both[:, :chans])
        r1 = tap_dot(shifted[1], both)
        r2 = tap_dot(shifted[2], both)
        r3 = tap_dot(shifted[3], both[:, chans:])
        sums = [
            r0 + r1[:, chans:] * t0_t2,
            r1[:, :chans] * t0_t1 + r2[:, chans:] * t1_t2,
            r2[:, :chans] + r3,
        ]
        for k in range(3):
            for dx in range(3):
                tile = sums[k][dx * chans : (dx + 1) * chans].astype(BF16)
                spot = ((dy * 3 + k) * 3 + dx) * 4
                for h in range(2):
                    for q in range(4):
                        start = (h * 4 + q) * 16
                        grads[h * HALF + spot + q] = tile[start : start + 16]
        pair(dy).start()
        if dy > 0:
            join_pair(dy - 1)
            ready = [q for q in a_ready(dy * CHUNK) if q not in started]
            go(first_a, y, ready)
            started += ready
    join_pair(2)
    go(first_a, y, [q for q in range(ny) if q not in started])
    go(first_b, x, range(nx))

    def exchange(n, me, src_of, dst, place, peer):
        for d in far_first(n):
            q = lax.rem(me + d, n)
            remote(src_of(q), dst.at[me], sent.at[2], stage.at[place], peer(q)).start()

    def arrived(n, dst, place):
        rows = dst.at[pl.ds(0, n - 1)]
        remote(rows, rows, sent.at[2], stage.at[place], sibling).wait_recv()

    def summed(n, me, own, dst):
        total = own.astype(F32)
        for d in range(1, n):
            total = total + dst[lax.rem(me + n - d, n)].astype(F32)
        return total.astype(BF16)

    arrived(ny, r1a, 1)
    s1a[...] = summed(ny, y, part[pl.ds(y * nx * sa, nx * sa)], r1a)
    exchange(nz, z, lambda q: s1a.at[pl.ds(q * za, za)], r2a, 3, z_peer)
    arrived(nx, r1b, 2)
    s1b[...] = summed(nx, x, part[pl.ds(n_a + x * ny * sb, ny * sb)], r1b)
    exchange(ny, y, lambda q: s1b.at[pl.ds(q * sb, sb)], r2b, 4, y_peer)

    arrived(nz, r2a, 3)
    s2a[...] = summed(nz, z, s1a[pl.ds(z * za, za)], r2a)
    exchange(nx, x, lambda q: s2a, r3a, 5, x_peer)
    arrived(ny, r2b, 4)
    s2b[...] = summed(ny, y, s1b[pl.ds(y * sb, sb)], r2b)
    exchange(nz, z, lambda q: s2b, r3b, 6, z_peer)

    base = core * HALF

    def a_line(q, start=base):
        return full.at[pl.ds(start + q * nx * sa, nx * sa)]

    def b_line(q, start=base):
        return full.at[pl.ds(start + n_a + q * ny * sb, ny * sb)]

    def spread_out(n, me, piece, group, recv, peer):
        for d in far_first(n):
            remote(piece, piece, sent.at[group], recv, peer(lax.rem(me + d, n))).start()

    def some(tiles):
        return full.at[pl.ds(0, tiles)]

    arrived(nx, r3a, 5)
    a_piece = full.at[pl.ds(base + y * nx * sa + z * za, za)]
    a_piece[...] = summed(nx, x, s2a[...], r3a)
    spread_out(nz, z, a_piece, 2, stage.at[7], z_peer)
    arrived(nz, r3b, 6)
    b_piece = full.at[pl.ds(base + n_a + (x * ny + y) * sb, sb)]
    b_piece[...] = summed(nz, z, s2b[...], r3b)
    spread_out(ny, y, b_piece, 2, stage.at[8], y_peer)

    def give(tiles, place):
        remote(full.at[tiles], grad_hbm.at[tiles], sent.at[3], stage.at[9], sibling).start()
        copy = pltpu.make_async_copy(full.at[tiles], grad_hbm.at[tiles], lines_out.at[place])
        copy.start()
        writes.append(copy)

    writes = []

    def give_a(q):
        give(pl.ds(base + q * nx * sa, nx * sa), len(writes))

    def give_b(q):
        give(pl.ds(base + n_a + q * ny * sb, ny * sb), len(writes))

    remote(some((nz - 1) * za), some((nz - 1) * za), sent.at[2], stage.at[7], sibling).wait_recv()
    spread_out(ny, y, a_line(y), 3, line_a.at[y], y_peer)
    give_a(y)
    remote(some((ny - 1) * sb), some((ny - 1) * sb), sent.at[2], stage.at[8], sibling).wait_recv()
    spread_out(nx, x, b_line(x), 3, line_b.at[x], x_peer)
    give_b(x)
    for d in reversed(far_first(ny)):
        q = lax.rem(y + ny - d, ny)
        remote(a_line(q), a_line(q), sent.at[3], line_a.at[q], sibling).wait_recv()
        give_a(q)
    for d in reversed(far_first(nx)):
        q = lax.rem(x + nx - d, nx)
        remote(b_line(q), b_line(q), sent.at[3], line_b.at[q], sibling).wait_recv()
        give_b(q)

    remote(others, others, sent.at[4], stage.at[0], right).wait_send()
    lines = (ny - 1) * nx * sa + (nx - 1) * ny * sb
    pieces = 2 * ((nz - 1) * za + (ny - 1) * sb) + (nx - 1) * za + (nz - 1) * sb
    frames_out = frames * (pixels + half_h * half_w) // 16
    for group, tiles in ((0, frames_out), (1, HALF + lines), (2, pieces), (3, HALF + lines)):
        remote(some(tiles), some(tiles), sent.at[group], stage.at[0], sibling).wait_send()

    theirs = grad_hbm.at[pl.ds((1 - core) * HALF, HALF)]
    remote(theirs, theirs, sent.at[3], stage.at[9], sibling).wait_recv()
    out_far.wait_recv()
    out_near.wait()
    for copy in writes:
        copy.wait()


def widen_result(grad_hbm, down_hbm, grad_out, down_out, tiles, wide, down, sems):
    take = pltpu.make_async_copy(down_hbm, down, sems.at[0])
    pass_on = pltpu.make_async_copy(down, down_out, sems.at[0])
    loads = []
    for dy in range(3):
        for h in range(2):
            span = pl.ds(h * HALF + dy * CHUNK, CHUNK)
            loads.append(pltpu.make_async_copy(grad_hbm.at[span], tiles.at[span], sems.at[1 + dy * 2 + h]))
    for load in loads:
        load.start()
    take.start()
    stores = []
    for dy in range(3):
        for h in range(2):
            loads[dy * 2 + h].wait()
        for k in range(3):
            tap = k * 9 + dy * 3
            for dx in range(3):
                for h in range(2):
                    for q in range(4):
                        spot = h * HALF + ((dy * 3 + k) * 3 + dx) * 4 + q
                        start = (h * 4 + q) * 16
                        wide[tap + dx, start : start + 16] = tiles[spot].astype(F32)
            group = pl.ds(tap, 3)
            stores.append(pltpu.make_async_copy(wide.at[group], grad_out.at[group], sems.at[7 + dy * 3 + k]))
            stores[-1].start()
    take.wait()
    pass_on.start()
    for store in stores:
        store.wait()
    pass_on.wait()


def per_device(nx, nz, ny, video, clip_first, kernel, bias, cotangent):
    _, frames, height, width, chans = video.shape
    half_h, half_w = height // 2, width // 2
    n_tm = nx * nz
    owned = HALF // (nx * ny)
    sa, sb = owned - owned // 2, owned // 2
    any_space = pl.BlockSpec(memory_space=pl.ANY)
    sem = pltpu.SemaphoreType.DMA

    def tiles(*shape):
        return pltpu.VMEM((*shape, 16, chans), BF16)

    down, grad = pl.pallas_call(
        functools.partial(fused, nx, nz, ny, sa, sb),
        out_shape=(
            jax.ShapeDtypeStruct(cotangent.shape, BF16),
            jax.ShapeDtypeStruct((2 * HALF, 16, chans), BF16),
        ),
        in_specs=[any_space] * 5,
        out_specs=(any_space, any_space),
        scratch_shapes=[
            pltpu.SMEM(clip_first.shape, jnp.int32),
            pltpu.VMEM((1, chans), F32),
            pltpu.VMEM((frames, height, width, chans), BF16),
            pltpu.VMEM((frames, height, width, chans), BF16),
            pltpu.VMEM((3, 3, 3, chans, chans), BF16),
            pltpu.VMEM((frames, half_h, half_w, chans), BF16),
            pltpu.VMEM((4, height + 2, width, 3 * chans), BF16),
            pltpu.VMEM((frames, height * width, chans), F32),
            pltpu.VMEM((frames * half_h, width, chans), F32),
            pltpu.VMEM((frames * half_h, width, chans), F32),
            pltpu.VMEM((frames, half_h, half_w, chans), BF16),
            pltpu.VMEM((height * width, frames * chans), BF16),
            pltpu.VMEM((n_tm, 2, chans), F32),
            tiles(2 * HALF),
            tiles(HALF),
            tiles(HALF),
            tiles(ny, nx * sa),
            tiles(nx, ny * sb),
            tiles(nx * sa),
            tiles(ny * sb),
            tiles(nz, nx * sa // nz),
            tiles(ny, sb),
            tiles(nx * sa // nz),
            tiles(sb),
            tiles(nx, nx * sa // nz),
            tiles(nz, sb),
            tiles(2 * HALF),
            sem((9,)),
            sem((5,)),
            sem((10,)),
            sem((3,)),
            sem((12,)),
            sem((ny,)),
            sem((nx,)),
            sem((ny + nx,)),
        ],
        compiler_params=pltpu.CompilerParams(
            collective_id=0, has_side_effects=True, vmem_limit_bytes=62 * 1024 * 1024
        ),
    )(clip_first, bias.reshape(1, chans), video, kernel, cotangent)
    grad, down = pl.pallas_call(
        widen_result,
        out_shape=(
            jax.ShapeDtypeStruct((27, chans, chans), F32),
            jax.ShapeDtypeStruct(cotangent.shape, BF16),
        ),
        in_specs=[any_space] * 2,
        out_specs=(any_space, any_space),
        scratch_shapes=[
            tiles(2 * HALF),
            pltpu.VMEM((27, chans, chans), F32),
            pltpu.VMEM(cotangent.shape, BF16),
            sem((16,)),
        ],
        compiler_params=pltpu.CompilerParams(vmem_limit_bytes=62 * 1024 * 1024),
    )(grad, down)
    return down, grad.reshape(3, 3, 3, chans, chans)


def solution(mesh):
    n_tm, n_dp = mesh.shape["tm"], mesh.shape["dp"]
    nz = 8 if n_tm == 32 else 2
    in_specs = (
        P("dp", "tm", None, None, None),
        P("dp", "tm"),
        P(),
        P(),
        P("dp", "tm", None, None, None),
    )
    out_specs = (P("dp", "tm", None, None, None), P())
    return jax.shard_map(
        functools.partial(per_device, n_tm // nz, nz, n_dp // 2),
        mesh=mesh,
        in_specs=in_specs,
        out_specs=out_specs,
        check_vma=False,
    )
```
